32 devices in a mesh: dp: 8 (over y, x, core), seq: 4 (over z).
Axes of the slice: x: 2, y: 2, z: 4, core: 2. Of those that a mesh axis runs over, the one named last changes fastest.
Arguments:
- byte_input_rows: bfloat16 [8, 4096, 512], P('dp', 'seq'), may hold values from -6 to 6
- segment_ids: int32 [8, 4096], P('dp', 'seq'), may hold values from 0 to 1791, as said below
- attn_gain: float32 [512], replicated, may hold values from 0.5 to 1.5
- qkv_weight: bfloat16 [512, 1536], replicated, may hold values from -0.25 to 0.25
- out_weight: bfloat16 [512, 512], replicated, may hold values from -1 to 1
- ffn_gain: float32 [512], replicated, may hold values from 0.5 to 1.5
- up_weight: bfloat16 [512, 2048], replicated, may hold values from -0.25 to 0.25
- up_bias: float32 [2048], replicated, may hold values from -3 to 3
- down_weight: bfloat16 [2048, 512], replicated, may hold values from -0.125 to 0.125
- cotangent: bfloat16 [8, 4096, 512], P('dp', 'seq'), may hold values from -6 to 6
Outputs:
- layer_out: bfloat16 [8, 4096, 512], P('dp', 'seq')
- grad_input: bfloat16 [8, 4096, 512], P('dp', 'seq')
- grad_attn_gain: float32 [512], replicated
- grad_qkv: float32 [512, 1536], replicated
- grad_out_weight: float32 [512, 512], replicated
- grad_ffn_gain: float32 [512], replicated
- grad_up: float32 [512, 2048], replicated
- grad_up_bias: float32 [2048], replicated
- grad_down: float32 [2048, 512], replicated
The draws below stay inside these ranges and needn't reach their ends.
Inputs may be any that keep to these rules, and one draw needn't show every extreme that they name: `segment_ids`: in each sequence the ids start at 0 on the first byte, rise by 0 or 1 from one byte to the next and end at 1791 on the last byte, so every id names a run of one or more bytes.
All inputs are finite; a program needn't handle non-finite values.
Results may differ from the reference program's by a relative error of at most 0.023.
Values may be sent and summed in bfloat16 or wider, within the bound.
No kernel may reach another device: no remote copies, remote signals or barrier semaphores. Data moves between devices by JAX's collectives and lax.ppermute only.
A program may use at most 192 MiB of HBM per device.

```python
import math
import jax
import jax.numpy as jnp
from jax import lax

D = 512
HEADS = 8
HEAD = 64
FF = 2048
BLOCK = 1024
SEG_DEV = 448
SEQS = 8
LEN = 4096
SEGS = 1792


def group_ranks(scores):
    order = jnp.argsort(-scores, stable=True)
    return jnp.argsort(order, stable=True).astype(jnp.int32)


def draw_segment_ids(key, part):
    key = jax.random.fold_in(key, 11)
    block_total = LEN // BLOCK
    half_len = LEN // 2
    least_front = max(1, SEGS - half_len)
    most_front = SEG_DEV - 2

    def one_sequence_ids(seq_key):
        count_key, weight_key, score_key = jax.random.split(seq_key, 3)
        front_count = jax.random.randint(count_key, (), least_front, most_front + 1).astype(jnp.int32)
        back_count = SEGS - front_count - 1
        density = jax.random.randint(weight_key, (block_total,), 1, 11)
        byte_density = jnp.repeat(density, BLOCK)
        position = jnp.arange(LEN, dtype=jnp.int32)
        raw_scores = jax.random.randint(score_key, (LEN,), 0, 16384) * byte_density * LEN + position
        in_front = (position >= 1) & (position < half_len)
        in_back = position > half_len
        front_rank = group_ranks(jnp.where(in_front, raw_scores, -1))
        back_rank = group_ranks(jnp.where(in_back, raw_scores, -1))
        chosen = in_front & (front_rank < front_count - 1) | in_back & (back_rank < back_count) | (position == half_len)
        return jnp.cumsum(chosen.astype(jnp.int32)).astype(jnp.int32)
    seq_keys = jax.random.split(key, SEQS)
    return jax.vmap(one_sequence_ids)(seq_keys)


def levels(stream_key, dims, cuts, least, largest):
    gain, own = 1.0, jax.random.fold_in(stream_key, 6)
    for dim, blocks in cuts:
        draws = jnp.exp(jax.random.uniform(jax.random.fold_in(own, dim), (blocks,), jnp.float32, least / len(cuts), largest / len(cuts)))
        gain = gain * jnp.repeat(draws, dims[dim] // blocks).reshape([-1 if axis == dim else 1 for axis in range(len(dims))])
    return gain


def gaussian(rng, dims, width, bound, cuts=(), kind=jnp.bfloat16):
    values = jax.random.normal(rng, dims, jnp.float32) * width
    if len(cuts) > 0:
        values = levels(rng, dims, cuts, -0.22, 0.18) * values
    return jnp.clip(values, min=-bound, max=bound).astype(kind)


def setup_inputs(seed: int = 0) -> dict:
    key_list = jax.random.split(jax.random.key(seed), 11)
    return {
        "byte_input_rows": gaussian(key_list[0], (SEQS, LEN, D), 1.0, 6.0, ((0, 8), (1, 4))),
        "segment_ids": draw_segment_ids(jax.random.fold_in(key_list[10], 71), 0),
        "attn_gain": jnp.clip(1.0 + 0.1 * jax.random.normal(key_list[2], (D,), jnp.float32), 0.5, 1.5),
        "qkv_weight": gaussian(key_list[3], (D, 3 * D), D ** -0.5, 0.25),
        "out_weight": gaussian(key_list[4], (D, D), (D // 16) ** -0.5, 1.0),
        "ffn_gain": jnp.clip(1.0 + 0.1 * jax.random.normal(key_list[5], (D,), jnp.float32), 0.5, 1.5),
        "up_weight": gaussian(key_list[6], (D, FF), D ** -0.5, 0.25),
        "up_bias": gaussian(key_list[7], (FF,), 0.5, 3.0, (), jnp.float32),
        "down_weight": gaussian(key_list[8], (FF, D), FF ** -0.5, 0.125),
        "cotangent": gaussian(key_list[9], (SEQS, LEN, D), 1.0, 6.0, ((0, 8), (1, 4))),
    }


@jax.custom_vjp
def low(v):
    return lax.optimization_barrier(v.astype(jnp.bfloat16)).astype(jnp.float32)

@jax.custom_vjp
def low_back(v):
    return v

def low_keep(v):
    return (low(v), None)

def low_pass(kept, grad):
    return (grad,)

def back_keep(v):
    return (v, None)

def back_low(kept, grad):
    return (low(grad),)
low.defvjp(low_keep, low_pass)
low_back.defvjp(back_keep, back_low)
highest = lax.Precision.HIGHEST

def layer_norm(values, gain_row):
    center = lax.optimization_barrier(jnp.mean(values, axis=-1, keepdims=True))
    centered = values - center
    variance = lax.optimization_barrier(jnp.mean(centered * centered, axis=-1, keepdims=True))
    return centered * lax.rsqrt(variance + 1e-05) * gain_row

def rotate(values, byte_positions):
    half_size = values.shape[-1] // 2
    frequency = jnp.exp(jnp.arange(half_size, dtype=jnp.float32) * (-math.log(10000.0) / half_size))
    angles = byte_positions.astype(jnp.float32)[:, None] * frequency[None, :]
    cosine = jnp.cos(angles)[:, None, :]
    sine_part = jnp.sin(angles)[:, None, :]
    first_half = values[..., :half_size]
    second_half = values[..., half_size:]
    return jnp.concatenate([first_half * cosine - second_half * sine_part, second_half * cosine + first_half * sine_part], axis=-1)

def one_sequence(byte_input_rows, segment_ids, attn_gain, qkv_weight, out_weight, ffn_gain, up_weight, up_bias, down_weight):
    segment_sums = jax.ops.segment_sum(byte_input_rows, segment_ids, SEGS)
    counts = jax.ops.segment_sum(jnp.ones(segment_ids.shape, byte_input_rows.dtype), segment_ids, SEGS)
    pooled = segment_sums / counts[:, None]
    normed_attn = low(layer_norm(pooled, attn_gain))
    projected = jnp.dot(normed_attn, qkv_weight, precision=highest)
    query_raw = low_back(projected[:, :D]).reshape(SEGS, HEADS, HEAD)
    key_raw = low_back(projected[:, D:2 * D]).reshape(SEGS, HEADS, HEAD)
    value_rows = low(low_back(projected[:, 2 * D:])).reshape(SEGS, HEADS, HEAD)
    byte_positions = jnp.arange(SEGS, dtype=jnp.int32)
    query = low(rotate(query_raw, byte_positions) * (1.0 / math.sqrt(HEAD)))
    key_rows = low(rotate(key_raw, byte_positions))
    query_block = math.gcd(SEGS, 512)

    def attend(block_query, first_index):
        scores = low_back(jnp.einsum('qhd,khd->hqk', block_query, key_rows, precision=highest))
        key_index = jnp.arange(SEGS, dtype=jnp.int32)
        query_index = first_index + jnp.arange(query_block, dtype=jnp.int32)
        allowed = key_index[None, :] <= query_index[:, None]
        scores = jnp.where(allowed[None], scores, -1e+30)
        running_max = lax.optimization_barrier(jnp.max(scores, axis=-1, keepdims=True))
        exp_scores = jnp.exp(scores - running_max)
        attn_prob = low(exp_scores / lax.optimization_barrier(jnp.sum(exp_scores, axis=-1, keepdims=True)))
        return jnp.einsum('hqk,khd->qhd', attn_prob, value_rows, precision=highest)
    checked = jax.checkpoint(attend)
    query_blocks = query.reshape(SEGS // query_block, query_block, HEADS, HEAD)
    block_starts = jnp.arange(SEGS // query_block, dtype=jnp.int32) * query_block
    attended = lax.map(lambda pair_item: checked(pair_item[0], pair_item[1]), (query_blocks, block_starts))
    attended = low_back(low(attended.reshape(SEGS, D)))
    branch = low_back(jnp.dot(attended, out_weight, precision=highest))
    hidden = pooled + branch
    normed_ffn = low(layer_norm(hidden, ffn_gain))
    gate_in = low_back(jnp.dot(normed_ffn, up_weight, precision=highest) + up_bias)
    activated = low(jax.nn.gelu(gate_in, approximate=False))
    ffn_branch = low_back(jnp.dot(activated, down_weight, precision=highest))
    pooled_out = low(hidden + ffn_branch)
    return byte_input_rows + pooled_out[segment_ids]

def reference(byte_input_rows, segment_ids, attn_gain, qkv_weight, out_weight, ffn_gain, up_weight, up_bias, down_weight, cotangent):
    parameters = (attn_gain.astype(jnp.float32), qkv_weight.astype(jnp.float32), out_weight.astype(jnp.float32), ffn_gain.astype(jnp.float32), up_weight.astype(jnp.float32), up_bias.astype(jnp.float32), down_weight.astype(jnp.float32))
    rows_f32 = byte_input_rows.astype(jnp.float32)
    cot_f32 = cotangent.astype(jnp.float32)

    def step(totals, sequence_item):
        seq_rows, seq_ids, seq_cot = sequence_item

        def forward(rows_in, *weights_in):
            return one_sequence(rows_in, seq_ids, *weights_in)
        result, pullback = jax.vjp(forward, seq_rows, *parameters)
        gradients = pullback(seq_cot)
        totals = tuple((total_item + grad_item for total_item, grad_item in zip(totals, gradients[1:])))
        return (totals, (result.astype(jnp.bfloat16), gradients[0].astype(jnp.bfloat16)))
    initial = tuple((jnp.zeros(param_item.shape, jnp.float32) for param_item in parameters))
    totals, (layer_out, grad_input) = lax.scan(step, initial, (rows_f32, segment_ids, cot_f32))
    return (layer_out, grad_input, totals[0], totals[1], totals[2], totals[3], totals[4], totals[5], totals[6])
```

```python
import math

import jax
import jax.numpy as jnp
import numpy as np
from jax import lax
from jax.experimental import pallas as pl
from jax.experimental.pallas import tpu as pltpu
from jax.sharding import PartitionSpec as P

HEADS = 8
SEG_DEV = 448
TILE = 256
NEG = -1e30
NN = (((1,), (0,)), ((), ()))
NT = (((1,), (1,)), ((), ()))
TN = (((0,), (0,)), ((), ()))
F32 = jnp.float32
BF16 = jnp.bfloat16
VMEM_BYTES = 56 * 1024 * 1024

SMEM = pl.BlockSpec(memory_space=pltpu.SMEM)
VMEM = pl.BlockSpec(memory_space=pltpu.VMEM)
ANY = pl.BlockSpec(memory_space=pl.ANY)


def mm(left, right, dims=NN):
    return lax.dot_general(left, right, dims, preferred_element_type=F32)


def shape(dims, kind):
    return jax.ShapeDtypeStruct(dims, kind)


def cost(flops, moved, exps=0):
    return pl.CostEstimate(flops=int(flops), bytes_accessed=int(moved), transcendentals=int(exps))


def params():
    return pltpu.CompilerParams(vmem_limit_bytes=VMEM_BYTES)


def window_groups(parts, rows, block):
    total = rows * parts
    groups = {}
    for d in range(parts):
        low, high = max(0, total - (parts - d) * block), min(total, (d + 1) * block)
        for owner in range(parts):
            first, last = max(low, owner * rows), min(high, (owner + 1) * rows)
            if owner == d or first >= last:
                continue
            first = (first - owner * rows) // 16 * 16
            last = -(-(last - owner * rows) // 16) * 16
            groups.setdefault(((owner - d) % parts, last - first), []).append((d, owner, first))
    return [(shift, size, pairs) for (shift, size), pairs in sorted(groups.items())]


def pick(table, index):
    return jnp.take(jnp.asarray(np.array(table, np.int32)), index)


def pool_kernel(base_ref, ids_ref, rows_ref, *outs):
    ids = ids_ref[...]
    rows = rows_ref[...]
    for index, out in enumerate(outs):
        place = lax.broadcasted_iota(jnp.int32, (out.shape[0], ids.shape[1]), 0)
        hot = jnp.where(place == ids - base_ref[index], 1.0, 0.0).astype(BF16)
        out[...] = mm(hot, rows).astype(out.dtype)


def pool(bases, ids, rows, own_rows, sizes):
    block, width = rows.shape
    total = own_rows + sum(sizes)
    return pl.pallas_call(
        pool_kernel,
        out_shape=[shape((own_rows, width), F32)] + [shape((size, width), BF16) for size in sizes],
        in_specs=[SMEM, VMEM, VMEM],
        out_specs=[VMEM] * (1 + len(sizes)),
        compiler_params=params(),
        cost_estimate=cost(2 * total * block * width, 2 * block * width + 2 * total * width),
        name="pool",
    )(bases, ids, rows)


def select_kernel(base_ref, ids_ref, rows_ref, *refs):
    pieces, out = refs[:-1], refs[-1]
    ids = ids_ref[...]
    total = rows_ref[...].astype(F32)
    for index, piece in enumerate(pieces):
        size = piece.shape[0]
        place = lax.broadcasted_iota(jnp.int32, (ids.shape[0], size), 1)
        hot = jnp.where(place == ids - base_ref[index], 1.0, 0.0).astype(BF16)
        total = total + mm(hot, piece[...])
    out[...] = total.astype(BF16)


def select(bases, ids_column, rows, pieces):
    block, width = rows.shape
    total = sum(piece.shape[0] for piece in pieces)
    return pl.pallas_call(
        select_kernel,
        out_shape=shape((block, width), BF16),
        in_specs=[SMEM, VMEM, VMEM] + [VMEM] * len(pieces),
        out_specs=VMEM,
        compiler_params=params(),
        cost_estimate=cost(2 * total * block * width, 4 * block * width + 2 * total * width),
        name="select",
    )(bases, ids_column, rows, *pieces)


def add_windows(own, pieces, start_ref, total_ref):
    total_ref[...] = own[...]
    for index, piece in enumerate(pieces):
        size = piece.shape[0]
        if size == total_ref.shape[0]:
            total_ref[...] += piece[...].astype(F32)
        else:
            place = pl.ds(pl.multiple_of(start_ref[index], 16), size)
            total_ref[place, :] += piece[...].astype(F32)


def norm_parts(values):
    center = jnp.mean(values, axis=-1, keepdims=True)
    centered = values - center
    variance = jnp.mean(centered * centered, axis=-1, keepdims=True)
    scale = lax.rsqrt(variance + 1e-05)
    return centered * scale, scale


def norm_back(grad, xhat, scale, gain):
    e = grad * gain
    mean_e = jnp.mean(e, axis=-1, keepdims=True)
    mean_ex = jnp.mean(e * xhat, axis=-1, keepdims=True)
    return scale * (e - mean_e - xhat * mean_ex), jnp.sum(grad * xhat, axis=0, keepdims=True)


def partner(values):
    lanes = values.shape[1]
    lane = lax.broadcasted_iota(jnp.int32, values.shape, 1)
    return jnp.where(
        lax.rem(lane, 64) < 32, pltpu.roll(values, lanes - 32, 1), pltpu.roll(values, 32, 1)
    )


def dest(me, shift, parts):
    return lax.rem(me + shift, parts)


def source(me, shift, parts):
    return lax.rem(me + parts - shift, parts)


def pre_kernel(parts, groups, info_ref, own, *refs):
    pieces, refs = refs[:groups], refs[groups:]
    counts, gain, weight, cosine, sine, pooled_ref, normed_ref = refs[:7]
    outs, (total, send) = refs[7 : 7 + parts], refs[7 + parts :]
    me = info_ref[0]
    add_windows(own, pieces, info_ref.at[pl.ds(1, groups)], total)
    pooled = total[...] / counts[...]
    pooled_ref[...] = pooled
    xhat, unused = norm_parts(pooled)
    normed = (xhat * gain[...]).astype(BF16)
    normed_ref[...] = normed
    width = pooled.shape[1]
    part = width // parts
    step = 256
    for kind in range(3):
        for first in range(0, width, step):
            column = kind * width + first
            wide = mm(normed, weight[:, column : column + step])
            for inner in range(0, step, 128):
                block = wide[:, inner : inner + 128]
                if kind < 2:
                    block = block * cosine[...] + partner(block) * sine[...]
                if kind == 0:
                    block = block * (1.0 / math.sqrt(width // HEADS))
                block = block.astype(BF16)
                for small in range(0, 128, min(part, 128)):
                    place = first + inner + small
                    offset = kind * part + place % part
                    send[place // part, :, offset : offset + min(part, 128)] = block[
                        :, small : small + min(part, 128)
                    ]
    for shift, out in enumerate(outs):
        out[...] = send[dest(me, shift, parts)]


def copy_in(pieces, place, sems, me, parts):
    copies = []
    for shift, piece in enumerate(pieces):
        copies.append(
            pltpu.make_async_copy(piece, place(source(me, shift, parts)), sems.at[shift])
        )
    for copy in copies:
        copy.start()
    return copies


def row_place(ref, rows):
    return lambda index: ref.at[pl.ds(pl.multiple_of(index * rows, 16), rows)]


def head_mask(tile, head, heads):
    if heads == 1:
        return tile
    lane = lax.broadcasted_iota(jnp.int32, tile.shape, 1)
    return jnp.where(lane // 64 == head, tile.astype(F32), 0.0).astype(BF16)


def attend_kernel(parts, heads, info_ref, *refs):
    pieces, refs = refs[:parts], refs[parts:]
    outs, refs = refs[:parts], refs[parts:]
    qkv, out_t, prob_ref, v_t, scores, probs, attended, in_sems, prob_sems = refs
    me = info_ref[0]
    rows, part = outs[0].shape
    tiles = qkv.shape[0] // TILE
    for copy in copy_in(pieces, row_place(qkv, rows), in_sems, me, parts):
        copy.wait()
    v_t[...] = qkv[:, 2 * part :].astype(F32).T.astype(BF16)
    key_index = lax.broadcasted_iota(jnp.int32, (TILE, TILE), 0)
    query_index = lax.broadcasted_iota(jnp.int32, (TILE, TILE), 1)
    started = []
    for head in range(heads):
        for tile in range(tiles):
            step = head * tiles + tile
            slot = step % 2
            columns = slice(tile * TILE, (tile + 1) * TILE)
            limit = (tile + 1) * TILE
            query = head_mask(qkv[columns, :part], head, heads)
            top = jnp.full((8, TILE), NEG, F32)
            for chunk in range(tile + 1):
                span = slice(chunk * TILE, (chunk + 1) * TILE)
                score = mm(qkv[span, part : 2 * part], query, NT)
                if chunk == tile:
                    score = jnp.where(key_index <= query_index, score, NEG)
                scores[slot, span, :] = score
                top = jnp.maximum(top, jnp.max(score.reshape(TILE // 8, 8, TILE), axis=0))
            top = jnp.max(top, axis=0, keepdims=True)
            total = jnp.zeros((8, TILE), F32)
            for chunk in range(tile + 1):
                span = slice(chunk * TILE, (chunk + 1) * TILE)
                grown = jnp.exp(scores[slot, span, :] - top)
                scores[slot, span, :] = grown
                total = total + jnp.sum(grown.reshape(TILE // 8, 8, TILE), axis=0)
            inverse = 1.0 / jnp.sum(total, axis=0, keepdims=True)
            if step >= 2:
                started[step - 2].wait()
            for chunk in range(tile + 1):
                span = slice(chunk * TILE, (chunk + 1) * TILE)
                probs[slot, span, :] = (scores[slot, span, :] * inverse).astype(BF16)
            copy = pltpu.make_async_copy(
                probs.at[slot, pl.ds(0, limit)],
                prob_ref.at[head, tile, pl.ds(0, limit)],
                prob_sems.at[slot],
            )
            copy.start()
            started.append(copy)
            height = slice(head * 64, (head + 1) * 64)
            out_t[height, columns] = mm(v_t[height, :limit], probs[slot, :limit, :])
    for copy in started[-2:]:
        copy.wait()
    attended[...] = out_t[...].T.astype(BF16)
    for shift, out in enumerate(outs):
        out[...] = attended[pl.ds(pl.multiple_of(dest(me, shift, parts) * rows, 16), rows), :]


def attend(info, pieces, parts, heads):
    rows, triple = pieces[0].shape
    part = triple // 3
    length = rows * parts
    tiles = length // TILE
    return pl.pallas_call(
        lambda *refs: attend_kernel(parts, heads, *refs),
        out_shape=[shape((rows, part), BF16) for unused in range(parts)]
        + [
            shape((length, triple), BF16),
            shape((part, length), F32),
            shape((heads, tiles, length, TILE), BF16),
        ],
        in_specs=[SMEM] + [ANY] * parts,
        out_specs=[VMEM] * parts + [VMEM, VMEM, ANY],
        scratch_shapes=[
            pltpu.VMEM((part, length), BF16),
            pltpu.VMEM((2, length, TILE), F32),
            pltpu.VMEM((2, length, TILE), BF16),
            pltpu.VMEM((length, part), BF16),
            pltpu.SemaphoreType.DMA((parts,)),
            pltpu.SemaphoreType.DMA((2,)),
        ],
        compiler_params=params(),
        cost_estimate=cost(
            heads * length * length * 256, heads * length * length, heads * length * length // 2
        ),
        name="attend",
    )(info, *pieces)


def attend_back_kernel(parts, heads, info_ref, *refs):
    pieces, refs = refs[:parts], refs[parts:]
    qkv, out_t, prob_ref, cosine, sine = refs[:5]
    outs, refs = refs[5 : 5 + parts], refs[5 + parts :]
    grads, k_t, delta, probs, dq_t, dk, dv, low, in_sems, prob_sems = refs
    me = info_ref[0]
    rows = pieces[0].shape[0]
    length, part = dk.shape
    tiles = length // TILE
    steps = [(head, tile) for head in range(heads) for tile in range(tiles)]

    def fetch(index):
        head, tile = steps[index]
        limit = (tile + 1) * TILE
        return pltpu.make_async_copy(
            prob_ref.at[head, tile, pl.ds(0, limit)],
            probs.at[index % 3, pl.ds(0, limit)],
            prob_sems.at[index % 3],
        )

    arrivals = copy_in(pieces, row_place(grads, rows), in_sems, me, parts)
    fetch(0).start()
    fetch(1).start()
    k_t[...] = qkv[:, part : 2 * part].astype(F32).T.astype(BF16)
    dk[...] = jnp.zeros_like(dk)
    dv[...] = jnp.zeros_like(dv)
    for copy in arrivals:
        copy.wait()
    product = grads[...].astype(F32).T * out_t[...]
    for head in range(heads):
        delta[head : head + 1, :] = jnp.sum(
            product[head * 64 : (head + 1) * 64, :], axis=0, keepdims=True
        )
    for index, (head, tile) in enumerate(steps):
        slot = index % 3
        if index + 2 < len(steps):
            fetch(index + 2).start()
        fetch(index).wait()
        columns = slice(tile * TILE, (tile + 1) * TILE)
        limit = (tile + 1) * TILE
        height = slice(head * 64, (head + 1) * 64)
        query = head_mask(qkv[columns, :part], head, heads)
        grad = head_mask(grads[columns, :], head, heads)
        shift = delta[head : head + 1, columns]
        dq = jnp.zeros((64, TILE), F32)
        for chunk in range(tile + 1):
            span = slice(chunk * TILE, (chunk + 1) * TILE)
            prob = probs[slot, span, :]
            grad_prob = mm(qkv[span, 2 * part :], grad, NT)
            grad_score = (prob.astype(F32) * (grad_prob - shift)).astype(BF16)
            dv[span, :] += mm(prob, grad)
            dk[span, :] += mm(grad_score, query)
            dq = dq + mm(k_t[height, span], grad_score)
        dq_t[height, columns] = dq
    head_scale = 1.0 / math.sqrt(64)
    turned = dq_t[...].T * head_scale
    for kind, values in enumerate((turned, dk[...], dv[...])):
        if kind < 2:
            values = values * cosine[:, :part] - partner(values) * sine[:, :part]
        low[:, kind * part : (kind + 1) * part] = values.astype(BF16)
    for shift, out in enumerate(outs):
        out[...] = low[pl.ds(pl.multiple_of(dest(me, shift, parts) * rows, 16), rows), :]


def attend_back(info, pieces, qkv, out_t, probs, cosine, sine, parts, heads):
    rows, part = pieces[0].shape
    length = rows * parts
    return pl.pallas_call(
        lambda *refs: attend_back_kernel(parts, heads, *refs),
        out_shape=[shape((rows, 3 * part), BF16) for unused in range(parts)],
        in_specs=[SMEM] + [ANY] * parts + [VMEM, VMEM, ANY, VMEM, VMEM],
        out_specs=[VMEM] * parts,
        scratch_shapes=[
            pltpu.VMEM((length, part), BF16),
            pltpu.VMEM((part, length), BF16),
            pltpu.VMEM((8, length), F32),
            pltpu.VMEM((3, length, TILE), BF16),
            pltpu.VMEM((part, length), F32),
            pltpu.VMEM((length, part), F32),
            pltpu.VMEM((length, part), F32),
            pltpu.VMEM((length, 3 * part), BF16),
            pltpu.SemaphoreType.DMA((parts,)),
            pltpu.SemaphoreType.DMA((3,)),
        ],
        compiler_params=params(),
        cost_estimate=cost(heads * length * length * 512, heads * length * length, 0),
        name="attend_back",
    )(info, *pieces, qkv, out_t, probs, cosine, sine)


def pre(info, own, pieces, counts, gain, weight, cosine, sine, parts):
    rows, width = own.shape
    part = width // parts
    return pl.pallas_call(
        lambda *refs: pre_kernel(parts, len(pieces), *refs),
        out_shape=[shape((rows, width), F32), shape((rows, width), BF16)]
        + [shape((rows, 3 * part), BF16) for unused in range(parts)],
        in_specs=[SMEM] + [VMEM] * (6 + len(pieces)),
        out_specs=[VMEM] * (2 + parts),
        scratch_shapes=[pltpu.VMEM((rows, width), F32), pltpu.VMEM((parts, rows, 3 * part), BF16)],
        compiler_params=params(),
        cost_estimate=cost(6 * rows * width * width, 8 * rows * width + 6 * width * width),
        name="pre",
    )(info, own, *pieces, counts, gain, weight, cosine, sine)


def ffn_kernel(parts, groups, info_ref, *refs):
    pieces, refs = refs[:parts], refs[parts:]
    pooled, out_weight, gain, up, bias, down, cot_own = refs[:7]
    cots, refs = refs[7 : 7 + groups], refs[7 + groups :]
    hidden_ref, attended_ref, normed_ref, active_ref, gate_ref, ffn_ref = refs[:6]
    branch_ref, grad_hidden_ref, bias_grad, gain_grad = refs[6:10]
    outs, refs = refs[10 : 10 + parts], refs[10 + parts :]
    arrived, total, back, send, sems = refs
    me = info_ref[0]
    step = pl.program_id(0)
    rows, width = pooled.shape
    part = width // parts

    @pl.when(step == 0)
    def first():
        copies = copy_in(pieces, lambda index: arrived.at[index], sems, me, parts)
        add_windows(cot_own, cots, info_ref.at[pl.ds(1, groups)], total)
        ffn_ref[...] = total[...].astype(BF16)
        back[...] = jnp.zeros_like(back)
        for copy in copies:
            copy.wait()
        for index in range(parts):
            attended_ref[:, index * part : (index + 1) * part] = arrived[index]
        hidden = pooled[...] + mm(attended_ref[...], out_weight[...])
        hidden_ref[...] = hidden
        xhat, unused = norm_parts(hidden)
        normed_ref[...] = (xhat * gain[...]).astype(BF16)

    gate_in = mm(normed_ref[...], up[...]) + bias[...]
    grad_active = mm(ffn_ref[...], down[...], NT)
    bell = 0.5 * (1.0 + lax.erf(gate_in * (1.0 / math.sqrt(2.0))))
    active_ref[...] = (gate_in * bell).astype(BF16)
    slope = bell + gate_in * jnp.exp(-0.5 * gate_in * gate_in) * (1.0 / math.sqrt(2.0 * math.pi))
    grad_gate = (grad_active * slope).astype(BF16)
    gate_ref[...] = grad_gate
    bias_grad[...] = jnp.sum(grad_gate.astype(F32), axis=0, keepdims=True)
    back[...] += mm(grad_gate, up[...], NT)

    @pl.when(step == pl.num_programs(0) - 1)
    def last():
        xhat, scale = norm_parts(hidden_ref[...])
        grad, gain_sum = norm_back(back[...], xhat, scale, gain[...])
        gain_grad[...] = gain_sum
        grad_hidden = total[...] + grad
        grad_hidden_ref[...] = grad_hidden
        branch = grad_hidden.astype(BF16)
        branch_ref[...] = branch
        attended_grad = mm(branch, out_weight[...], NT).astype(BF16)
        for index in range(parts):
            send[index] = attended_grad[:, index * part : (index + 1) * part]
        for shift, out in enumerate(outs):
            out[...] = send[dest(me, shift, parts)]


def ffn(info, pieces, pooled, out_weight, gain, up, bias, down, cot_own, cots, parts):
    rows, width = pooled.shape
    units = up.shape[1]
    part = width // parts
    chunk = 512
    whole = lambda *dims: pl.BlockSpec(dims, lambda step: (0,) * len(dims))
    wide = pl.BlockSpec((rows, chunk), lambda step: (0, step))
    line = pl.BlockSpec((1, chunk), lambda step: (0, step))
    square = whole(rows, width)
    return pl.pallas_call(
        lambda *refs: ffn_kernel(parts, len(cots), *refs),
        grid=(units // chunk,),
        out_shape=[
            shape((rows, width), F32),
            shape((rows, width), BF16),
            shape((rows, width), BF16),
            shape((rows, units), BF16),
            shape((rows, units), BF16),
            shape((rows, width), BF16),
            shape((rows, width), BF16),
            shape((rows, width), F32),
            shape((1, units), F32),
            shape((1, width), F32),
        ]
        + [shape((rows, part), BF16) for unused in range(parts)],
        in_specs=[SMEM]
        + [ANY] * parts
        + [
            square,
            whole(width, width),
            whole(1, width),
            pl.BlockSpec((width, chunk), lambda step: (0, step)),
            line,
            pl.BlockSpec((chunk, width), lambda step: (step, 0)),
            square,
        ]
        + [whole(*cot.shape) for cot in cots],
        out_specs=[square, square, square, wide, wide, square, square, square, line]
        + [whole(1, width)]
        + [whole(rows, part) for unused in range(parts)],
        scratch_shapes=[
            pltpu.VMEM((parts, rows, part), BF16),
            pltpu.VMEM((rows, width), F32),
            pltpu.VMEM((rows, width), F32),
            pltpu.VMEM((parts, rows, part), BF16),
            pltpu.SemaphoreType.DMA((parts,)),
        ],
        compiler_params=params(),
        cost_estimate=cost(
            6 * rows * width * units + 4 * rows * width * width, 12 * width * units, 2 * rows * units
        ),
        name="ffn",
    )(info, *pieces, pooled, out_weight, gain, up, bias, down, cot_own, *cots)


def weight_kernel(blocks, active, grad_ffn, normed, gate, attended, branch, out):
    step = pl.program_id(0)

    @pl.when(step < blocks)
    def down_part():
        out[...] = mm(active[...], grad_ffn[...], TN).astype(BF16)

    @pl.when((step >= blocks) & (step < 2 * blocks))
    def up_part():
        out[...] = mm(normed[...], gate[...], TN).astype(BF16)

    @pl.when(step == 2 * blocks)
    def out_part():
        out[...] = mm(attended[...], branch[...], TN).astype(BF16)


def ffn_weights(active, grad_ffn, normed, gate, attended, branch):
    rows, width = normed.shape
    units = active.shape[1]
    blocks = units // width
    square = pl.BlockSpec((rows, width), lambda step: (0, 0))
    return pl.pallas_call(
        lambda *refs: weight_kernel(blocks, *refs),
        grid=(2 * blocks + 1,),
        out_shape=shape(((2 * blocks + 1) * width, width), BF16),
        in_specs=[
            pl.BlockSpec((rows, width), lambda step: (0, jnp.minimum(step, blocks - 1))),
            square,
            square,
            pl.BlockSpec((rows, width), lambda step: (0, jnp.clip(step - blocks, 0, blocks - 1))),
            square,
            square,
        ],
        out_specs=pl.BlockSpec((width, width), lambda step: (step, 0)),
        compiler_params=params(),
        cost_estimate=cost(4 * rows * width * units, 4 * rows * units + 4 * width * units),
        name="ffn_weights",
    )(active, grad_ffn, normed, gate, attended, branch)


def down_kernel(hidden, active, down, out):
    out[...] = (hidden[...] + mm(active[...], down[...])).astype(BF16)


def ffn_out(hidden, active, down):
    rows, width = hidden.shape
    return pl.pallas_call(
        down_kernel,
        out_shape=shape((rows, width), BF16),
        in_specs=[VMEM] * 3,
        out_specs=VMEM,
        compiler_params=params(),
        cost_estimate=cost(2 * rows * width * down.shape[0], 4 * width * down.shape[0]),
        name="ffn_out",
    )(hidden, active, down)


def post_kernel(parts, info_ref, *refs):
    pieces, refs = refs[:parts], refs[parts:]
    pooled, grad_hidden, counts, gain, weight, share_ref, low, gain_grad, arrived, sems = refs
    me = info_ref[0]
    width = pooled.shape[1]
    part = width // parts
    copies = copy_in(pieces, lambda index: arrived.at[index], sems, me, parts)
    xhat, scale = norm_parts(pooled[...])
    for copy in copies:
        copy.wait()
    for index in range(parts):
        for kind in range(3):
            place = kind * width + index * part
            low[:, place : place + part] = arrived[index, :, kind * part : (kind + 1) * part]
    grad = mm(low[...], weight[...], NT)
    grad, gain_sum = norm_back(grad, xhat, scale, gain[...])
    gain_grad[...] = gain_sum
    share_ref[...] = ((grad_hidden[...] + grad) / counts[...]).astype(BF16)


def post(info, pieces, pooled, grad_hidden, counts, gain, weight, parts):
    rows, width = pooled.shape
    part = width // parts
    return pl.pallas_call(
        lambda *refs: post_kernel(parts, *refs),
        out_shape=[
            shape((rows, width), BF16),
            shape((rows, 3 * width), BF16),
            shape((1, width), F32),
        ],
        in_specs=[SMEM] + [ANY] * parts + [VMEM] * 5,
        out_specs=[VMEM] * 3,
        scratch_shapes=[
            pltpu.VMEM((parts, rows, 3 * part), BF16),
            pltpu.SemaphoreType.DMA((parts,)),
        ],
        compiler_params=params(),
        cost_estimate=cost(6 * rows * width * width, 8 * rows * width + 6 * width * width),
        name="post",
    )(info, *pieces, pooled, grad_hidden, counts, gain, weight)


def qkv_weights_kernel(normed, low, out):
    out[...] = mm(normed[...], low[...], TN).astype(BF16)


def qkv_weights(normed, low):
    rows, width = normed.shape
    return pl.pallas_call(
        qkv_weights_kernel,
        grid=(3,),
        out_shape=shape((width, 3 * width), BF16),
        in_specs=[
            pl.BlockSpec((rows, width), lambda step: (0, 0)),
            pl.BlockSpec((rows, width), lambda step: (0, step)),
        ],
        out_specs=pl.BlockSpec((width, width), lambda step: (0, step)),
        compiler_params=params(),
        cost_estimate=cost(6 * rows * width * width, 8 * rows * width + 6 * width * width),
        name="qkv_weights",
    )(normed, low)


def swap(values, bit, size):
    return lax.ppermute(values, "dp", [(i, i ^ (1 << bit)) for i in range(size)])


def rotated(values, shift, parts):
    return lax.ppermute(values, "seq", [(i, (i + shift) % parts) for i in range(parts)])


def add_low(first, second):
    return (first.astype(F32) + second.astype(F32)).astype(BF16)


def halve(values, bit, dp_index, dp_size):
    half = values.shape[0] // 2
    mine = (dp_index >> bit) & 1
    sent = lax.dynamic_slice_in_dim(values, (1 - mine) * half, half, 0)
    kept = lax.dynamic_slice_in_dim(values, mine * half, half, 0)
    return add_low(kept, swap(sent, bit, dp_size))


def double(values, bit, dp_index, dp_size):
    other = swap(values, bit, dp_size)
    mine = (dp_index >> bit) & 1
    low = jnp.where(mine == 0, values, other)
    high = jnp.where(mine == 0, other, values)
    return jnp.concatenate([low, high], axis=0)


def sum_seq(values, me, parts):
    size = values.shape[0] // parts
    piece = lambda index: lax.dynamic_slice_in_dim(values, index * size, size, 0)
    total = piece(me).astype(F32)
    for shift in range(1, parts):
        total = total + rotated(piece((me + shift) % parts), shift, parts).astype(F32)
    own = total.astype(BF16)
    result = jnp.zeros(values.shape, BF16)
    result = lax.dynamic_update_slice_in_dim(result, own, me * size, 0)
    for shift in range(1, parts):
        got = rotated(own, shift, parts)
        index = (me + parts - shift) % parts
        result = lax.dynamic_update_slice_in_dim(result, got, index * size, 0)
    return result


def sum_all(values, dp_index, dp_size, me, parts):
    bits = dp_size.bit_length() - 1
    values = halve(values, 0, dp_index, dp_size)
    outer = list(range(1, bits))
    cut = len(outer) // 2
    half = values.shape[0] // 2
    orders = (outer, outer[cut:] + outer[:cut])
    lanes = [values[:half], values[half:]]
    for step in range(len(outer)):
        lanes = [halve(lane, order[step], dp_index, dp_size) for lane, order in zip(lanes, orders)]
    size = lanes[0].shape[0]
    joined = sum_seq(jnp.concatenate(lanes, axis=0), me, parts)
    lanes = [joined[:size], joined[size:]]
    for step in reversed(range(len(outer))):
        lanes = [double(lane, order[step], dp_index, dp_size) for lane, order in zip(lanes, orders)]
    return double(jnp.concatenate(lanes, axis=0), 0, dp_index, dp_size)


def sum_small(values, dp_size, parts):
    for bit in range(dp_size.bit_length() - 1):
        values = values + swap(values, bit, dp_size)
    total = values
    for shift in range(1, parts):
        total = total + rotated(values, shift, parts)
    return total


def body(
    byte_input_rows,
    segment_ids,
    attn_gain,
    qkv_weight,
    out_weight,
    ffn_gain,
    up_weight,
    up_bias,
    down_weight,
    cotangent,
):
    rows_in, cot = byte_input_rows[0], cotangent[0]
    ids = segment_ids
    block, width = rows_in.shape
    parts, dp_size = lax.axis_size("seq"), lax.axis_size("dp")
    me, dp_index = lax.axis_index("seq"), lax.axis_index("dp")
    own_rows = SEG_DEV
    length = own_rows * parts
    heads = HEADS // parts
    groups = window_groups(parts, own_rows, block)
    sizes = [size for unused, size, unused_pairs in groups]

    byte_start, owner_start, to_owner, to_bytes = [], [], [], []
    byte_base, owner_from = [me * own_rows], []
    for shift, size, pairs in groups:
        at_bytes, at_owner = [0] * parts, [0] * parts
        for holder, owner, first in pairs:
            at_bytes[holder], at_owner[owner] = first, first
        byte_start.append(pick(at_bytes, me))
        owner_start.append(pick(at_owner, me))
        byte_base.append((me + shift) % parts * own_rows + byte_start[-1])
        to_owner.append([(holder, owner) for holder, owner, unused in pairs])
        to_bytes.append([(owner, holder) for holder, owner, unused in pairs])
    byte_base = jnp.stack(byte_base).astype(jnp.int32)
    info = jnp.stack([me] + owner_start).astype(jnp.int32)

    def gather_owner(messages):
        return [lax.ppermute(m, "seq", perm) for m, perm in zip(messages, to_owner)]

    def spread(values):
        pieces = [values]
        for start, size, perm in zip(owner_start, sizes, to_bytes):
            window = lax.dynamic_slice_in_dim(values, start, size, 0) if size < own_rows else values
            pieces.append(lax.ppermute(window, "seq", perm))
        return pieces

    def exchange(messages):
        return [messages[0]] + [
            rotated(message, shift, parts) for shift, message in enumerate(messages) if shift
        ]

    half = 32
    lane = jnp.arange(128, dtype=jnp.int32)
    frequency = jnp.exp((lane % half).astype(F32) * (-math.log(10000.0) / half))
    angles = jnp.arange(length, dtype=jnp.int32).astype(F32)[:, None] * frequency[None, :]
    cosine = jnp.cos(angles)
    sine = jnp.sin(angles) * jnp.where(lane % 64 < half, -1.0, 1.0)
    own_cosine = lax.dynamic_slice_in_dim(cosine, me * own_rows, own_rows, 0)
    own_sine = lax.dynamic_slice_in_dim(sine, me * own_rows, own_rows, 0)

    ids_all = [ids] + [rotated(ids, shift, parts) for shift in range(1, parts)]
    positions = me * own_rows + jnp.arange(own_rows, dtype=jnp.int32)
    counts = sum(
        jnp.sum((piece == positions[:, None]).astype(F32), axis=1, keepdims=True)
        for piece in ids_all
    )
    ids_column = ids.reshape(block, 1)

    own_sums, *sums_out = pool(byte_base, ids, rows_in, own_rows, sizes)
    sums_in = gather_owner(sums_out)
    cot_own, *cots_out = pool(byte_base, ids, cot, own_rows, sizes)
    cots_out, sums_in = lax.optimization_barrier((cots_out, sums_in))
    cots_in = gather_owner(cots_out)

    gain_row = attn_gain[None, :]
    pooled, normed_attn, *qkv_out = pre(
        info, own_sums, sums_in, counts, gain_row, qkv_weight, own_cosine, own_sine, parts
    )
    qkv_in = exchange(qkv_out)
    *attended_out, qkv, out_t, probs = attend(info, qkv_in, parts, heads)
    attended_in = exchange(attended_out)
    (
        hidden,
        attended,
        normed_ffn,
        active,
        grad_gate,
        grad_ffn,
        branch,
        grad_hidden,
        grad_bias,
        grad_ffn_gain,
        *grads_out,
    ) = ffn(
        info,
        attended_in,
        pooled,
        out_weight,
        ffn_gain[None, :],
        up_weight,
        up_bias[None, :],
        down_weight,
        cot_own,
        cots_in,
        parts,
    )
    grads_in = exchange(grads_out)

    ffn_grads = ffn_weights(active, grad_ffn, normed_ffn, grad_gate, attended, branch)
    ffn_grads = sum_all(ffn_grads, dp_index, dp_size, me, parts)
    pooled_out = ffn_out(hidden, active, down_weight)
    layer_out = select(byte_base, ids_column, rows_in, spread(pooled_out))

    low_out = attend_back(info, grads_in, qkv, out_t, probs, cosine, sine, parts, heads)
    low_in = exchange(low_out)
    share, low, grad_attn_gain = post(
        info, low_in, pooled, grad_hidden, counts, gain_row, qkv_weight, parts
    )
    grad_input = select(byte_base, ids_column, cot, spread(share))
    qkv_grads = sum_all(qkv_weights(normed_attn, low), dp_index, dp_size, me, parts)

    units = up_weight.shape[1]
    small = jnp.concatenate([grad_bias.reshape(-1, width), grad_ffn_gain, grad_attn_gain], axis=0)
    small = sum_small(small, dp_size, parts)
    lines = units // width
    up_blocks = ffn_grads[units : 2 * units].reshape(lines, width, width)
    grad_up = jnp.concatenate([up_blocks[i] for i in range(lines)], axis=1).astype(F32)
    return (
        layer_out[None],
        grad_input[None],
        small[lines + 1],
        qkv_grads.astype(F32),
        ffn_grads[2 * units :].astype(F32),
        small[lines],
        grad_up,
        small[:lines].reshape(units),
        ffn_grads[:units].astype(F32),
    )


def solution(mesh):
    placed = (
        P("dp", "seq", None),
        P("dp", "seq"),
        P(),
        P(),
        P(),
        P(),
        P(),
        P(),
        P(),
        P("dp", "seq", None),
    )
    return jax.shard_map(
        body,
        mesh=mesh,
        in_specs=placed,
        out_specs=(P("dp", "seq", None), P("dp", "seq", None), P(), P(), P(), P(), P(), P(), P()),
        check_vma=False,
    )
```

```python
import math

import jax
import jax.numpy as jnp
import numpy as np
from jax import lax
from jax.experimental import pallas as pl
from jax.experimental.pallas import tpu as pltpu
from jax.sharding import PartitionSpec as P

HEADS = 8
SEG_DEV = 448
TILE = 256
BAND = TILE + 16
WEIGHT = 20
NEG = -1e30
NN = (((1,), (0,)), ((), ()))
NT = (((1,), (1,)), ((), ()))
TN = (((0,), (0,)), ((), ()))
F32 = jnp.float32
BF16 = jnp.bfloat16
VMEM_BYTES = 56 * 1024 * 1024

SMEM = pl.BlockSpec(memory_space=pltpu.SMEM)
VMEM = pl.BlockSpec(memory_space=pltpu.VMEM)
ANY = pl.BlockSpec(memory_space=pl.ANY)


def mm(left, right, dims=NN):
    return lax.dot_general(left, right, dims, preferred_element_type=F32)


def shape(dims, kind):
    return jax.ShapeDtypeStruct(dims, kind)


def cost(flops, moved, exps=0, weight=1):
    return pl.CostEstimate(
        flops=int(weight * flops), bytes_accessed=int(weight * moved), transcendentals=int(weight * exps)
    )


def params():
    return pltpu.CompilerParams(vmem_limit_bytes=VMEM_BYTES)


def reach_of(parts, rows, block):
    total = rows * parts
    reach = 0
    for d in range(parts):
        low = max(0, total - (parts - d) * block)
        high = min(total, (d + 1) * block) - 1
        reach = max(reach, d - low // rows, high // rows - d)
    return reach


def band_start(first_ref, base_ref, tile):
    return pl.multiple_of((first_ref[tile] - base_ref[0]) // 16 * 16, 16)


def pool_kernel(base_ref, side_ref, first_ref, ids_ref, rows_ref, *refs):
    outs, total = refs[:-1], refs[-1]
    size = outs[0].shape[0]
    total[...] = jnp.zeros_like(total)
    place = lax.broadcasted_iota(jnp.int32, (BAND, TILE), 0)
    for tile in range(rows_ref.shape[0] // TILE):
        span = slice(tile * TILE, (tile + 1) * TILE)
        start = band_start(first_ref, base_ref, tile)
        local = ids_ref[:, span] - (base_ref[0] + start)
        hot = jnp.where(place == local, 1.0, 0.0).astype(BF16)
        total[pl.ds(start, BAND), :] += mm(hot, rows_ref[span, :])
    reach = len(outs) // 2
    for index, out in enumerate(outs):
        place = pl.multiple_of((reach + (index - reach) * side_ref[0]) * size, 16)
        out[...] = total[pl.ds(place, size), :].astype(BF16)


def pool(base, side, firsts, ids, rows, own_rows, count):
    block, width = rows.shape
    return pl.pallas_call(
        pool_kernel,
        out_shape=[shape((own_rows, width), BF16)] * count,
        in_specs=[SMEM, SMEM, SMEM, VMEM, VMEM],
        out_specs=[VMEM] * count,
        scratch_shapes=[pltpu.VMEM((count * own_rows + BAND, width), F32)],
        compiler_params=params(),
        cost_estimate=cost(2 * BAND * block * width, 2 * block * width + 2 * count * own_rows * width),
        name="pool",
    )(base, side, firsts, ids, rows)


def select_kernel(half, base_ref, side_ref, first_ref, ids_ref, rows_ref, *refs):
    pieces, (out, table, sems) = refs[:-3], refs[-3:]
    size = pieces[0].shape[0] // 2
    reach = len(pieces) // 2
    copies = []
    for index, piece in enumerate(pieces):
        away = (index + 1) // 2 * (1 if index % 2 else -1)
        place = pl.multiple_of((reach + away * side_ref[0]) * size, 16)
        copies.append(
            pltpu.make_async_copy(
                piece.at[pl.ds(half * size, size)], table.at[pl.ds(place, size)], sems.at[index]
            )
        )
    for copy in copies:
        copy.start()
    table[len(pieces) * size :, :] = jnp.zeros((BAND, table.shape[1]), BF16)
    for copy in copies:
        copy.wait()
    place = lax.broadcasted_iota(jnp.int32, (TILE, BAND), 1)
    for tile in range(rows_ref.shape[0] // TILE):
        span = slice(tile * TILE, (tile + 1) * TILE)
        start = band_start(first_ref, base_ref, tile)
        local = ids_ref[span, :] - (base_ref[0] + start)
        hot = jnp.where(place == local, 1.0, 0.0).astype(BF16)
        chosen = mm(hot, table[pl.ds(start, BAND), :])
        out[span, :] = (rows_ref[span, :].astype(F32) + chosen).astype(BF16)


def select(base, side, firsts, ids_column, rows, pieces, half, weight=1):
    block, width = rows.shape
    total = sum(piece.shape[0] for piece in pieces) // 2
    return pl.pallas_call(
        lambda *refs: select_kernel(half, *refs),
        out_shape=shape((block, width), BF16),
        in_specs=[SMEM, SMEM, SMEM, VMEM, VMEM] + [ANY] * len(pieces),
        out_specs=VMEM,
        scratch_shapes=[
            pltpu.VMEM((total + BAND, width), BF16),
            pltpu.SemaphoreType.DMA((len(pieces),)),
        ],
        compiler_params=params(),
        cost_estimate=cost(
            2 * BAND * block * width, 4 * block * width + 2 * total * width, 0, weight
        ),
        name="select",
    )(base, side, firsts, ids_column, rows, *pieces)


def norm_parts(values):
    center = jnp.mean(values, axis=-1, keepdims=True)
    centered = values - center
    variance = jnp.mean(centered * centered, axis=-1, keepdims=True)
    scale = lax.rsqrt(variance + 1e-05)
    return centered * scale, scale


def norm_back(grad, xhat, scale, gain):
    e = grad * gain
    mean_e = jnp.mean(e, axis=-1, keepdims=True)
    mean_ex = jnp.mean(e * xhat, axis=-1, keepdims=True)
    return scale * (e - mean_e - xhat * mean_ex), jnp.sum(grad * xhat, axis=0, keepdims=True)


def partner(values):
    lanes = values.shape[1]
    lane = lax.broadcasted_iota(jnp.int32, values.shape, 1)
    return jnp.where(
        lax.rem(lane, 64) < 32, pltpu.roll(values, lanes - 32, 1), pltpu.roll(values, 32, 1)
    )


def dest(me, shift, parts):
    return lax.rem(me + shift, parts)


def source(me, shift, parts):
    return lax.rem(me + parts - shift, parts)


def pre_kernel(parts, info_ref, own, left, right, *refs):
    counts, gain, weight, cosine, sine, pooled_ref, normed_ref = refs[:7]
    outs, (send,) = refs[7 : 7 + parts], refs[7 + parts :]
    me = info_ref[0]
    total = own[...].astype(F32) + left[...].astype(F32) + right[...].astype(F32)
    pooled = total / counts[...]
    pooled_ref[...] = pooled
    xhat, unused = norm_parts(pooled)
    normed = (xhat * gain[...]).astype(BF16)
    normed_ref[...] = normed
    width = pooled.shape[1]
    part = width // parts
    step = 256
    for kind in range(3):
        for first in range(0, width, step):
            column = kind * width + first
            wide = mm(normed, weight[:, column : column + step])
            for inner in range(0, step, 128):
                block = wide[:, inner : inner + 128]
                if kind < 2:
                    block = block * cosine[...] + partner(block) * sine[...]
                if kind == 0:
                    block = block * (1.0 / math.sqrt(width // HEADS))
                block = block.astype(BF16)
                for small in range(0, 128, min(part, 128)):
                    place = first + inner + small
                    offset = kind * part + place % part
                    send[place // part, :, offset : offset + min(part, 128)] = block[
                        :, small : small + min(part, 128)
                    ]
    for shift, out in enumerate(outs):
        out[...] = send[dest(me, shift, parts)]


def copy_in(pieces, place, sems, me, parts):
    copies = []
    for shift, piece in enumerate(pieces):
        copies.append(
            pltpu.make_async_copy(piece, place(source(me, shift, parts)), sems.at[shift])
        )
    for copy in copies:
        copy.start()
    return copies


def row_place(ref, rows):
    return lambda index: ref.at[pl.ds(pl.multiple_of(index * rows, 16), rows)]


def head_mask(tile, head, heads):
    if heads == 1:
        return tile
    lane = lax.broadcasted_iota(jnp.int32, tile.shape, 1)
    return jnp.where(lane // 64 == head, tile.astype(F32), 0.0).astype(BF16)


def attend_kernel(parts, heads, info_ref, *refs):
    pieces, refs = refs[:parts], refs[parts:]
    outs, refs = refs[:parts], refs[parts:]
    qkv, out_t, prob_ref, v_t, scores, probs, attended, in_sems, prob_sems = refs
    me = info_ref[0]
    rows, part = outs[0].shape
    tiles = qkv.shape[0] // TILE
    for copy in copy_in(pieces, row_place(qkv, rows), in_sems, me, parts):
        copy.wait()
    v_t[...] = qkv[:, 2 * part :].astype(F32).T.astype(BF16)
    key_index = lax.broadcasted_iota(jnp.int32, (TILE, TILE), 0)
    query_index = lax.broadcasted_iota(jnp.int32, (TILE, TILE), 1)
    started = []
    for head in range(heads):
        for tile in range(tiles):
            step = head * tiles + tile
            slot = step % 2
            columns = slice(tile * TILE, (tile + 1) * TILE)
            limit = (tile + 1) * TILE
            query = head_mask(qkv[columns, :part], head, heads)
            top = jnp.full((8, TILE), NEG, F32)
            for chunk in range(tile + 1):
                span = slice(chunk * TILE, (chunk + 1) * TILE)
                score = mm(qkv[span, part : 2 * part], query, NT)
                if chunk == tile:
                    score = jnp.where(key_index <= query_index, score, NEG)
                scores[slot, span, :] = score
                top = jnp.maximum(top, jnp.max(score.reshape(TILE // 8, 8, TILE), axis=0))
            top = jnp.max(top, axis=0, keepdims=True)
            total = jnp.zeros((8, TILE), F32)
            for chunk in range(tile + 1):
                span = slice(chunk * TILE, (chunk + 1) * TILE)
                grown = jnp.exp(scores[slot, span, :] - top)
                scores[slot, span, :] = grown
                total = total + jnp.sum(grown.reshape(TILE // 8, 8, TILE), axis=0)
            inverse = 1.0 / jnp.sum(total, axis=0, keepdims=True)
            if step >= 2:
                started[step - 2].wait()
            for chunk in range(tile + 1):
                span = slice(chunk * TILE, (chunk + 1) * TILE)
                probs[slot, span, :] = (scores[slot, span, :] * inverse).astype(BF16)
            copy = pltpu.make_async_copy(
                probs.at[slot, pl.ds(0, limit)],
                prob_ref.at[head, tile, pl.ds(0, limit)],
                prob_sems.at[slot],
            )
            copy.start()
            started.append(copy)
            height = slice(head * 64, (head + 1) * 64)
            out_t[height, columns] = mm(v_t[height, :limit], probs[slot, :limit, :])
    for copy in started[-2:]:
        copy.wait()
    attended[...] = out_t[...].T.astype(BF16)
    for shift, out in enumerate(outs):
        out[...] = attended[pl.ds(pl.multiple_of(dest(me, shift, parts) * rows, 16), rows), :]


def attend(info, pieces, parts, heads):
    rows, triple = pieces[0].shape
    part = triple // 3
    length = rows * parts
    tiles = length // TILE
    return pl.pallas_call(
        lambda *refs: attend_kernel(parts, heads, *refs),
        out_shape=[shape((rows, part), BF16) for unused in range(parts)]
        + [
            shape((length, triple), BF16),
            shape((part, length), F32),
            shape((heads, tiles, length, TILE), BF16),
        ],
        in_specs=[SMEM] + [ANY] * parts,
        out_specs=[VMEM] * parts + [VMEM, VMEM, ANY],
        scratch_shapes=[
            pltpu.VMEM((part, length), BF16),
            pltpu.VMEM((2, length, TILE), F32),
            pltpu.VMEM((2, length, TILE), BF16),
            pltpu.VMEM((length, part), BF16),
            pltpu.SemaphoreType.DMA((parts,)),
            pltpu.SemaphoreType.DMA((2,)),
        ],
        compiler_params=params(),
        cost_estimate=cost(
            heads * length * length * 256,
            heads * length * length,
            heads * length * length // 2,
            WEIGHT,
        ),
        name="attend",
    )(info, *pieces)


def attend_back_kernel(parts, heads, info_ref, *refs):
    pieces, refs = refs[:parts], refs[parts:]
    qkv, out_t, prob_ref, cosine, sine = refs[:5]
    outs, refs = refs[5 : 5 + parts], refs[5 + parts :]
    grads, k_t, delta, probs, dq_t, dk, dv, low, in_sems, prob_sems = refs
    me = info_ref[0]
    rows = pieces[0].shape[0]
    length, part = dk.shape
    tiles = length // TILE
    steps = [(head, tile) for head in range(heads) for tile in range(tiles)]

    def fetch(index):
        head, tile = steps[index]
        limit = (tile + 1) * TILE
        return pltpu.make_async_copy(
            prob_ref.at[head, tile, pl.ds(0, limit)],
            probs.at[index % 3, pl.ds(0, limit)],
            prob_sems.at[index % 3],
        )

    arrivals = copy_in(pieces, row_place(grads, rows), in_sems, me, parts)
    fetch(0).start()
    fetch(1).start()
    k_t[...] = qkv[:, part : 2 * part].astype(F32).T.astype(BF16)
    dk[...] = jnp.zeros_like(dk)
    dv[...] = jnp.zeros_like(dv)
    for copy in arrivals:
        copy.wait()
    product = grads[...].astype(F32).T * out_t[...]
    for head in range(heads):
        delta[head : head + 1, :] = jnp.sum(
            product[head * 64 : (head + 1) * 64, :], axis=0, keepdims=True
        )
    for index, (head, tile) in enumerate(steps):
        slot = index % 3
        if index + 2 < len(steps):
            fetch(index + 2).start()
        fetch(index).wait()
        columns = slice(tile * TILE, (tile + 1) * TILE)
        limit = (tile + 1) * TILE
        height = slice(head * 64, (head + 1) * 64)
        query = head_mask(qkv[columns, :part], head, heads)
        grad = head_mask(grads[columns, :], head, heads)
        shift = delta[head : head + 1, columns]
        dq = jnp.zeros((64, TILE), F32)
        for chunk in range(tile + 1):
            span = slice(chunk * TILE, (chunk + 1) * TILE)
            prob = probs[slot, span, :]
            grad_prob = mm(qkv[span, 2 * part :], grad, NT)
            grad_score = (prob.astype(F32) * (grad_prob - shift)).astype(BF16)
            dv[span, :] += mm(prob, grad)
            dk[span, :] += mm(grad_score, query)
            dq = dq + mm(k_t[height, span], grad_score)
        dq_t[height, columns] = dq
    head_scale = 1.0 / math.sqrt(64)
    turned = dq_t[...].T * head_scale
    for kind, values in enumerate((turned, dk[...], dv[...])):
        if kind < 2:
            values = values * cosine[:, :part] - partner(values) * sine[:, :part]
        low[:, kind * part : (kind + 1) * part] = values.astype(BF16)
    for shift, out in enumerate(outs):
        out[...] = low[pl.ds(pl.multiple_of(dest(me, shift, parts) * rows, 16), rows), :]


def attend_back(info, pieces, qkv, out_t, probs, cosine, sine, parts, heads):
    rows, part = pieces[0].shape
    length = rows * parts
    return pl.pallas_call(
        lambda *refs: attend_back_kernel(parts, heads, *refs),
        out_shape=[shape((rows, 3 * part), BF16) for unused in range(parts)],
        in_specs=[SMEM] + [ANY] * parts + [VMEM, VMEM, ANY, VMEM, VMEM],
        out_specs=[VMEM] * parts,
        scratch_shapes=[
            pltpu.VMEM((length, part), BF16),
            pltpu.VMEM((part, length), BF16),
            pltpu.VMEM((8, length), F32),
            pltpu.VMEM((3, length, TILE), BF16),
            pltpu.VMEM((part, length), F32),
            pltpu.VMEM((length, part), F32),
            pltpu.VMEM((length, part), F32),
            pltpu.VMEM((length, 3 * part), BF16),
            pltpu.SemaphoreType.DMA((parts,)),
            pltpu.SemaphoreType.DMA((3,)),
        ],
        compiler_params=params(),
        cost_estimate=cost(heads * length * length * 512, heads * length * length, 0, WEIGHT),
        name="attend_back",
    )(info, *pieces, qkv, out_t, probs, cosine, sine)


def pre(info, own, left, right, counts, gain, weight, cosine, sine, parts):
    rows, width = own.shape
    part = width // parts
    return pl.pallas_call(
        lambda *refs: pre_kernel(parts, *refs),
        out_shape=[shape((rows, width), F32), shape((rows, width), BF16)]
        + [shape((rows, 3 * part), BF16) for unused in range(parts)],
        in_specs=[SMEM] + [VMEM] * 8,
        out_specs=[VMEM] * (2 + parts),
        scratch_shapes=[pltpu.VMEM((parts, rows, 3 * part), BF16)],
        compiler_params=params(),
        cost_estimate=cost(6 * rows * width * width, 8 * rows * width + 6 * width * width),
        name="pre",
    )(info, own, left, right, counts, gain, weight, cosine, sine)


def ffn_kernel(parts, info_ref, *refs):
    pieces, refs = refs[:parts], refs[parts:]
    pooled, out_weight, gain, up, bias, down, *cots = refs[:9]
    refs = refs[9:]
    result_ref, grad_hidden_ref, bias_grad, gain_grad, sent, kept = refs[:6]
    outs, refs = refs[6 : 6 + parts], refs[6 + parts :]
    attended_ref, normed_ref, ffn_ref, hidden_ref, forward, arrived, back, send = refs[:8]
    products, sems, product_sems = refs[8:]
    me, bit = info_ref[0], info_ref[1]
    step = pl.program_id(0)
    steps = pl.num_programs(0)
    rows, width = pooled.shape
    part = width // parts
    high = width // 2
    halves = sent.shape[0] // high

    def product_copy(index, target):
        place = pl.multiple_of(lax.rem(index, halves) * high, high)
        return pltpu.make_async_copy(
            products.at[index], target.at[pl.ds(place, high)], product_sems.at[index]
        )

    def give(index, value):
        products[index] = value.astype(BF16)

        @pl.when(index // halves == bit)
        def to_kept():
            product_copy(index, kept).start()

        @pl.when(index // halves != bit)
        def to_sent():
            product_copy(index, sent).start()

    @pl.when(step == 0)
    def first():
        copies = copy_in(pieces, lambda index: arrived.at[index], sems, me, parts)
        ffn_ref[...] = sum(cot[...].astype(F32) for cot in cots).astype(BF16)
        back[...] = jnp.zeros_like(back)
        for copy in copies:
            copy.wait()
        for index in range(parts):
            attended_ref[:, index * part : (index + 1) * part] = arrived[index]
        hidden = pooled[...] + mm(attended_ref[...], out_weight[...])
        hidden_ref[...] = hidden
        forward[...] = hidden
        xhat, unused = norm_parts(hidden)
        normed_ref[...] = (xhat * gain[...]).astype(BF16)

    gate_in = mm(normed_ref[...], up[...]) + bias[...]
    grad_active = mm(ffn_ref[...], down[...], NT)
    bell = 0.5 * (1.0 + lax.erf(gate_in * (1.0 / math.sqrt(2.0))))
    active = (gate_in * bell).astype(BF16)
    forward[...] += mm(active, down[...])
    slope = bell + gate_in * jnp.exp(-0.5 * gate_in * gate_in) * (1.0 / math.sqrt(2.0 * math.pi))
    grad_gate = (grad_active * slope).astype(BF16)
    bias_grad[...] = jnp.sum(grad_gate.astype(F32), axis=0, keepdims=True)
    back[...] += mm(grad_gate, up[...], NT)
    for half in range(2):
        side = slice(half * high, (half + 1) * high)
        give(2 * step + half, mm(active[:, side], ffn_ref[...], TN))
        give(2 * (steps + step) + half, mm(normed_ref[:, side], grad_gate, TN))

    @pl.when(step == pl.num_programs(0) - 1)
    def last():
        result_ref[...] = forward[...].astype(BF16)
        xhat, scale = norm_parts(hidden_ref[...])
        grad, gain_sum = norm_back(back[...], xhat, scale, gain[...])
        gain_grad[...] = gain_sum
        grad_hidden = ffn_ref[...].astype(F32) + grad
        grad_hidden_ref[...] = grad_hidden
        branch = grad_hidden.astype(BF16)
        for half in range(2):
            side = slice(half * high, (half + 1) * high)
            give(4 * steps + half, mm(attended_ref[:, side], branch, TN))
        attended_grad = mm(branch, out_weight[...], NT).astype(BF16)
        for index in range(parts):
            send[index] = attended_grad[:, index * part : (index + 1) * part]
        for shift, out in enumerate(outs):
            out[...] = send[dest(me, shift, parts)]
        for index in range(2 * halves):
            product_copy(index, kept).wait()


def ffn(info, pieces, pooled, out_weight, gain, up, bias, down, cots, parts):
    rows, width = pooled.shape
    units = up.shape[1]
    part = width // parts
    chunk = 512
    whole = lambda *dims: pl.BlockSpec(dims, lambda step: (0,) * len(dims))
    line = pl.BlockSpec((1, chunk), lambda step: (0, step))
    square = whole(rows, width)
    return pl.pallas_call(
        lambda *refs: ffn_kernel(parts, *refs),
        grid=(units // chunk,),
        out_shape=[
            shape((rows, width), BF16),
            shape((rows, width), F32),
            shape((1, units), F32),
            shape((1, width), F32),
            shape((units + width // 2, width), BF16),
            shape((units + width // 2, width), BF16),
        ]
        + [shape((rows, part), BF16) for unused in range(parts)],
        in_specs=[SMEM]
        + [ANY] * parts
        + [
            square,
            whole(width, width),
            whole(1, width),
            pl.BlockSpec((width, chunk), lambda step: (0, step)),
            line,
            pl.BlockSpec((chunk, width), lambda step: (step, 0)),
            square,
            square,
            square,
        ],
        out_specs=[square, square, line, whole(1, width), ANY, ANY]
        + [whole(rows, part) for unused in range(parts)],
        scratch_shapes=[
            pltpu.VMEM((rows, width), BF16),
            pltpu.VMEM((rows, width), BF16),
            pltpu.VMEM((rows, width), BF16),
            pltpu.VMEM((rows, width), F32),
            pltpu.VMEM((rows, width), F32),
            pltpu.VMEM((parts, rows, part), BF16),
            pltpu.VMEM((rows, width), F32),
            pltpu.VMEM((parts, rows, part), BF16),
            pltpu.VMEM((4 * units // width + 2, width // 2, width), BF16),
            pltpu.SemaphoreType.DMA((parts,)),
            pltpu.SemaphoreType.DMA((4 * units // width + 2,)),
        ],
        compiler_params=params(),
        cost_estimate=cost(
            12 * rows * width * units + 4 * rows * width * width, 12 * width * units, 2 * rows * units, WEIGHT
        ),
        name="ffn",
    )(info, *pieces, pooled, out_weight, gain, up, bias, down, *cots)


def post_kernel(parts, info_ref, *refs):
    pieces, refs = refs[:parts], refs[parts:]
    pooled, grad_hidden, result, counts, gain, weight, both_ref, low, gain_grad, arrived, sems = refs
    me = info_ref[0]
    width = pooled.shape[1]
    part = width // parts
    copies = copy_in(pieces, lambda index: arrived.at[index], sems, me, parts)
    xhat, scale = norm_parts(pooled[...])
    for copy in copies:
        copy.wait()
    for index in range(parts):
        for kind in range(3):
            place = kind * width + index * part
            low[:, place : place + part] = arrived[index, :, kind * part : (kind + 1) * part]
    grad = mm(low[...], weight[...], NT)
    grad, gain_sum = norm_back(grad, xhat, scale, gain[...])
    gain_grad[...] = gain_sum
    rows = result.shape[0]
    both_ref[:rows, :] = ((grad_hidden[...] + grad) / counts[...]).astype(BF16)
    both_ref[rows:, :] = result[...]


def post(info, pieces, pooled, grad_hidden, result, counts, gain, weight, parts):
    rows, width = pooled.shape
    part = width // parts
    return pl.pallas_call(
        lambda *refs: post_kernel(parts, *refs),
        out_shape=[
            shape((2 * rows, width), BF16),
            shape((rows, 3 * width), BF16),
            shape((1, width), F32),
        ],
        in_specs=[SMEM] + [ANY] * parts + [VMEM] * 6,
        out_specs=[VMEM] * 3,
        scratch_shapes=[
            pltpu.VMEM((parts, rows, 3 * part), BF16),
            pltpu.SemaphoreType.DMA((parts,)),
        ],
        compiler_params=params(),
        cost_estimate=cost(6 * rows * width * width, 8 * rows * width + 6 * width * width, 0, WEIGHT),
        name="post",
    )(info, *pieces, pooled, grad_hidden, result, counts, gain, weight)


def qkv_weights_kernel(bit_ref, normed, low, bias, *refs):
    step = pl.program_id(0)
    gains, (sent, kept) = refs[:-2], refs[-2:]
    half = sent.shape[0]
    wide = low.shape[1]
    first = jnp.where(step == 0, 1 - bit_ref[0], bit_ref[0])
    value = mm(normed[...], low[...], TN).astype(BF16)
    width = normed.shape[1] * 2
    lines = [
        bias[:, pl.ds(pl.multiple_of(place + first * half, 128), half)]
        for place in range(0, bias.shape[1], width)
    ]
    lines += [gain[:, pl.ds(pl.multiple_of(first * half, 128), half)] for gain in gains]
    lines = jnp.concatenate(lines + [jnp.zeros((128 - len(lines), half), F32)], axis=0)

    def store(out):
        out[:, :wide] = value
        out[:, wide:] = lines.T.astype(BF16)

    @pl.when(step == 0)
    def to_sent():
        store(sent)

    @pl.when(step == 1)
    def to_kept():
        store(kept)


def qkv_weights(bit, normed, low, bias, *gains):
    rows, width = normed.shape
    wide = low.shape[1]
    half = width // 2
    whole = lambda *dims: pl.BlockSpec(dims, lambda step, ref: (0, 0))
    return pl.pallas_call(
        qkv_weights_kernel,
        grid_spec=pltpu.PrefetchScalarGridSpec(
            num_scalar_prefetch=1,
            grid=(2,),
            in_specs=[
                pl.BlockSpec(
                    (rows, half),
                    lambda step, ref: (0, jnp.where(step == 0, 1 - ref[0], ref[0])),
                ),
                whole(rows, wide),
                whole(*bias.shape),
            ]
            + [whole(*gain.shape) for gain in gains],
            out_specs=[whole(half, wide + 128)] * 2,
        ),
        out_shape=[shape((half, wide + 128), BF16)] * 2,
        compiler_params=params(),
        cost_estimate=cost(2 * rows * width * wide, 8 * rows * width + 6 * width * width, 0, WEIGHT),
        name="qkv_weights",
    )(bit, normed, low, bias, *gains)


def ffn_result_kernel(bit_ref, own, other, down, up, out):
    swapped = bit_ref[0] == 1
    half, width = own.shape
    units = down.shape[0]
    first = half - units

    def piece(which, place, size):
        return jnp.where(
            swapped == (which == 0),
            other[place : place + size, :].astype(F32),
            own[place : place + size, :].astype(F32),
        )

    for place in range(0, units, 256):
        down[place : place + 256, :] = piece(0, place, 256)
    for block in range(0, 2 * units // width):
        place = units + block * (width // 2)
        column = block // 2 * width
        row = block % 2 * (width // 2)
        up[row : row + width // 2, column : column + width] = piece(
            place // half, place % half, width // 2
        )
    for row in range(0, width, 256):
        out[row : row + 256, :] = piece(1, half - width + row, 256)


def ffn_result(bit, own, other, units):
    half, width = own.shape
    return pl.pallas_call(
        ffn_result_kernel,
        out_shape=[shape((units, width), F32), shape((width, units), F32), shape((width, width), F32)],
        in_specs=[SMEM, VMEM, VMEM],
        out_specs=[VMEM] * 3,
        compiler_params=params(),
        cost_estimate=cost(0, 12 * half * width),
        name="ffn_result",
    )(bit, own, other)


def qkv_result_kernel(bit_ref, own, other, out, small):
    value = jnp.where(
        pl.program_id(0) == bit_ref[0], own[...].astype(F32), other[...].astype(F32)
    )
    wide = out.shape[1]
    out[...] = value[:, :wide]
    small[...] = value[:, wide:].T[: small.shape[0], :]


def qkv_result(bit, own, other):
    half, wide = own.shape
    piece = pl.BlockSpec((half, wide), lambda step, ref: (0, 0))
    return pl.pallas_call(
        qkv_result_kernel,
        grid_spec=pltpu.PrefetchScalarGridSpec(
            num_scalar_prefetch=1,
            grid=(2,),
            in_specs=[piece, piece],
            out_specs=[
                pl.BlockSpec((half, wide - 128), lambda step, ref: (step, 0)),
                pl.BlockSpec((8, half), lambda step, ref: (0, step)),
            ],
        ),
        out_shape=[shape((2 * half, wide - 128), F32), shape((8, 2 * half), F32)],
        compiler_params=params(),
        cost_estimate=cost(0, 12 * half * wide, 0, 4 * WEIGHT),
        name="qkv_result",
    )(bit, own, other)


def join_kernel(order_ref, *refs):
    pieces, out = refs[:-1], refs[-1]
    size = pieces[0].shape[0]
    for index, piece in enumerate(pieces):
        out[pl.ds(pl.multiple_of(order_ref[index] * size, size), size), :] = piece[...]


def join(pieces, order):
    size, width = pieces[0].shape
    count = len(pieces)
    if size % 16:
        whole = jnp.zeros((count * size, width), BF16)
        for index, piece in enumerate(pieces):
            whole = lax.dynamic_update_slice_in_dim(whole, piece, order[index] * size, 0)
        return whole
    return pl.pallas_call(
        join_kernel,
        out_shape=shape((count * size, width), BF16),
        in_specs=[SMEM] + [VMEM] * count,
        out_specs=VMEM,
        compiler_params=params(),
        cost_estimate=cost(0, 4 * count * size * width),
        name="join",
    )(order, *pieces)


def pairwise(values, odd, parts):
    firsts = range(1 if odd else 0, parts - 1, 2)
    pairs = [(i, i + 1) for i in firsts] + [(i + 1, i) for i in firsts]
    return lax.ppermute(values, "seq", pairs)


def rotated(values, shift, parts):
    return lax.ppermute(values, "seq", [(i, (i + shift) % parts) for i in range(parts)])


def swap(values):
    return lax.ppermute(values, "core", [(0, 1), (1, 0)])


def turned(values, axis):
    return lax.all_to_all(values, axis, 0, 0)


def add_low(first, second):
    return (first.astype(F32) + second.astype(F32)).astype(BF16)


def total_of(values):
    return jnp.sum(values.astype(F32), axis=0).astype(BF16)


def sum_plane_out(half, chips):
    rows, width = half.shape
    return turned(half.reshape(chips, rows // chips, width), "chip")


def sum_plane_back(own, chips):
    chunks = turned(jnp.broadcast_to(own, (chips,) + own.shape), "chip")
    return chunks.reshape(chips * own.shape[0], own.shape[1])


class SeqSum:
    def __init__(self, pieces, me, parts):
        self.values, self.me, self.parts = pieces, me, parts
        self.bits = parts.bit_length() - 1
        self.ways = [(bit, 0) for bit in range(self.bits - 1)] + [(self.bits - 1, 1)]
        self.ways += [(bit, 2) for bit in reversed(range(self.bits - 1))]

    def exchange(self, values, bit):
        return lax.ppermute(values, "seq", [(i, i ^ (1 << bit)) for i in range(self.parts)])

    def start(self, way):
        bit, kind = self.ways[way]
        if kind == 0:
            half = self.values.shape[1] // 2
            mine = (self.me >> bit) & 1
            piece = lambda side: total_of(
                lax.dynamic_slice_in_dim(self.values, side * half, half, 1)
            )
            self.kept, self.sent = piece(mine), piece(1 - mine)
            return self.exchange(self.sent, bit)
        if kind == 1:
            self.kept = total_of(self.values)
        else:
            self.kept = self.values
        self.sent = self.kept
        return self.exchange(self.sent, bit)

    def finish(self, way, got):
        bit, kind = self.ways[way]
        if kind < 2:
            self.values = add_low(self.kept, got)
            if kind == 0 or way + 1 == len(self.ways):
                self.values = self.values[None] if kind == 0 else self.values
            return
        first = ((self.me >> bit) & 1) == 0
        low, high = jnp.where(first, self.kept, got), jnp.where(first, got, self.kept)
        self.values = jnp.concatenate([low, high], axis=0)


def near_pieces(own, chips):
    chip = lax.axis_index("chip")
    pairs = lambda k: [(i, i ^ k) for i in range(chips)]
    pieces = [lax.ppermute(own, "chip", pairs(k)) if k else own for k in range(chips)]
    return join(pieces, jnp.stack([chip ^ k for k in range(chips)]).astype(jnp.int32))


def after(values, *earlier):
    return lax.optimization_barrier((values,) + earlier)[0]


def tie(*groups):
    return lax.optimization_barrier(groups)


def body(
    byte_input_rows,
    segment_ids,
    attn_gain,
    qkv_weight,
    out_weight,
    ffn_gain,
    up_weight,
    up_bias,
    down_weight,
    cotangent,
):
    rows_in, cot = byte_input_rows[0], cotangent[0]
    ids = segment_ids
    block, width = rows_in.shape
    parts, chips = lax.axis_size("seq"), lax.axis_size("chip")
    me, core = lax.axis_index("seq"), lax.axis_index("core")
    own_rows = SEG_DEV
    length = own_rows * parts
    heads = HEADS // parts
    reach = reach_of(parts, own_rows, block)
    place = jnp.stack([me, core]).astype(jnp.int32)
    base = ((me - reach) * own_rows).astype(jnp.int32)[None]
    side = (1 - 2 * (me & 1)).astype(jnp.int32)[None]
    firsts = ids[0, ::TILE]

    def both_ways(carried):
        return [pairwise(carried[0], False, parts), pairwise(carried[1], True, parts)]

    def to_owners(windows, hold=lambda carried: carried):
        carried = [windows[2 * reach], windows[0]]
        for away in range(reach - 1, -1, -1):
            carried = both_ways(carried)
            if away:
                carried = [
                    add_low(carried[1], windows[reach + away]),
                    add_low(carried[0], windows[reach - away]),
                ]
                carried = hold(carried)
        return [windows[reach]] + carried

    def exchange(messages):
        return [messages[0]] + [
            rotated(message, shift, parts) for shift, message in enumerate(messages) if shift
        ]

    half = 32
    lane = jnp.arange(128, dtype=jnp.int32)
    frequency = jnp.exp((lane % half).astype(F32) * (-math.log(10000.0) / half))
    angles = jnp.arange(length, dtype=jnp.int32).astype(F32)[:, None] * frequency[None, :]
    cosine = jnp.cos(angles)
    sine = jnp.sin(angles) * jnp.where(lane % 64 < half, -1.0, 1.0)
    own_cosine = lax.dynamic_slice_in_dim(cosine, me * own_rows, own_rows, 0)
    own_sine = lax.dynamic_slice_in_dim(sine, me * own_rows, own_rows, 0)

    windows = pool(base, side, firsts, ids, rows_in, own_rows, 2 * reach + 1)
    sums_in = to_owners(windows)
    ids_late = after(ids, windows)
    ids_all = turned(jnp.broadcast_to(ids_late, (parts,) + ids.shape), "seq")
    positions = me * own_rows + jnp.arange(own_rows, dtype=jnp.int32)
    same = ids_all.reshape(1, -1) == positions[:, None]
    counts = jnp.sum(same.astype(F32), axis=1, keepdims=True)
    ids_column = ids.reshape(block, 1)

    cot_windows = pool(base, side, firsts, ids, after(cot, counts), own_rows, 2 * reach + 1)

    gain_row = attn_gain[None, :]
    pooled, normed_attn, *qkv_out = pre(
        place, *sums_in, counts, gain_row, qkv_weight, own_cosine, own_sine, parts
    )
    qkv_in = exchange(qkv_out)
    cot_windows = after(cot_windows, qkv_out)
    cots_in = to_owners(cot_windows, lambda carried: after(carried, qkv_in))
    *attended_out, qkv, out_t, probs = attend(place, qkv_in, parts, heads)
    attended_in = exchange(attended_out)
    (
        pooled_out,
        grad_hidden,
        grad_bias,
        grad_ffn_gain,
        sent,
        kept,
        *grads_out,
    ) = ffn(
        place,
        attended_in,
        pooled,
        out_weight,
        ffn_gain[None, :],
        up_weight,
        up_bias[None, :],
        down_weight,
        cots_in,
        parts,
    )
    bit = core.astype(jnp.int32)[None]

    grads_in = exchange(grads_out)
    half = add_low(kept, swap(sent))
    grads_in = after(grads_in, half)
    pieces = sum_plane_out(half, chips)
    low_out = attend_back(place, grads_in, qkv, out_t, probs, cosine, sine, parts, heads)
    low_in = exchange(low_out)
    low_in, pieces = tie(low_in, pieces)
    ffn_sum = SeqSum(pieces, me, parts)
    ways = len(ffn_sum.ways)
    got = ffn_sum.start(0)
    low_in = after(low_in, ffn_sum.sent)
    both, low, grad_attn_gain = post(
        place, low_in, pooled, grad_hidden, pooled_out, counts, gain_row, qkv_weight, parts
    )

    qkv_sent, qkv_kept = qkv_weights(bit, normed_attn, low, grad_bias, grad_ffn_gain, grad_attn_gain)
    ffn_sum.finish(0, after(got, qkv_sent))
    pieces = sum_plane_out(add_low(qkv_kept, swap(qkv_sent)), chips)
    qkv_sum = SeqSum(pieces, me, parts)
    if ways > 1:
        ffn_sum.finish(1, after(ffn_sum.start(1), pieces))
    hop = after([both, both], ffn_sum.values)
    hop = both_ways(hop)
    both_in = [both] + hop
    for way in range(ways):
        qkv_sum.finish(way, qkv_sum.start(way))
        if way + 2 < ways:
            ffn_sum.finish(way + 2, after(ffn_sum.start(way + 2), qkv_sum.values))
    ffn_own = sum_plane_back(ffn_sum.values, chips)
    qkv_sum.values, hop = tie(qkv_sum.values, hop)
    for unused in range(1, reach):
        hop = both_ways(hop[::-1])
        both_in += hop
    qkv_own = near_pieces(qkv_sum.values, chips)
    grad_input = select(base, side, firsts, ids_column, cot, both_in, 0)
    layer_out = select(base, side, firsts, ids_column, rows_in, both_in, 1)
    qkv_own = after(qkv_own, grad_input, layer_out)
    units = up_weight.shape[1]
    ffn_own = after(ffn_own, qkv_own)
    grad_down, grad_up, grad_out = ffn_result(bit, ffn_own, swap(ffn_own), units)
    grad_qkv, small = qkv_result(bit, qkv_own, swap(qkv_own))
    lines = units // width
    return (
        layer_out[None],
        grad_input[None],
        small[lines + 1],
        grad_qkv,
        grad_out,
        small[lines],
        grad_up,
        small[:lines].reshape(units),
        grad_down,
    )


def solution(mesh):
    dp, seq = mesh.shape["dp"], mesh.shape["seq"]
    inner = jax.sharding.Mesh(mesh.devices.reshape(dp // 2, 2, seq), ("chip", "core", "seq"))
    rows, ids = P(("chip", "core"), "seq", None), P(("chip", "core"), "seq")
    placed = (rows, ids, P(), P(), P(), P(), P(), P(), P(), rows)
    return jax.shard_map(
        body,
        mesh=inner,
        in_specs=placed,
        out_specs=(rows, rows, P(), P(), P(), P(), P(), P(), P()),
        check_vma=False,
    )
```

```python
import math

import jax
import jax.numpy as jnp
import numpy as np
from jax import lax
from jax.experimental import pallas as pl
from jax.experimental.pallas import tpu as pltpu
from jax.sharding import PartitionSpec as P

HEADS = 8
SEG_DEV = 448
TILE = 256
BAND = TILE + 16
WEIGHT = 20
NEG = -1e30
NN = (((1,), (0,)), ((), ()))
NT = (((1,), (1,)), ((), ()))
TN = (((0,), (0,)), ((), ()))
F32 = jnp.float32
BF16 = jnp.bfloat16

SMEM = pl.BlockSpec(memory_space=pltpu.SMEM)
VMEM = pl.BlockSpec(memory_space=pltpu.VMEM)
HBM = pl.BlockSpec(memory_space=pltpu.HBM)


def mm(left, right, dims=NN):
    return lax.dot_general(left, right, dims, preferred_element_type=F32)


def shape(dims, kind):
    return jax.ShapeDtypeStruct(dims, kind)


def cost(flops, moved, exps=0, weight=1):
    return pl.CostEstimate(
        flops=int(weight * flops), bytes_accessed=int(weight * moved), transcendentals=int(weight * exps)
    )


def params(mebibytes):
    return pltpu.CompilerParams(vmem_limit_bytes=int(mebibytes * 1024 * 1024))


def begin(moves, sems):
    copies = [pltpu.make_async_copy(*move, sems.at[index]) for index, move in enumerate(moves)]
    for copy in copies:
        copy.start()
    return copies


def end(copies):
    for copy in copies:
        copy.wait()


def reach_of(parts, rows, block):
    total = rows * parts
    reach = 0
    for d in range(parts):
        low = max(0, total - (parts - d) * block)
        high = min(total, (d + 1) * block) - 1
        reach = max(reach, d - low // rows, high // rows - d)
    return reach


def band_start(first_ref, base_ref, tile):
    return pl.multiple_of((first_ref[tile] - base_ref[0]) // 16 * 16, 16)


def pool_kernel(base_ref, side_ref, first_ref, ids_ref, rows_ref, *refs):
    outs, total = refs[:-1], refs[-1]
    size = outs[0].shape[0]
    total[...] = jnp.zeros_like(total)
    place = lax.broadcasted_iota(jnp.int32, (BAND, TILE), 0)
    for tile in range(rows_ref.shape[0] // TILE):
        span = slice(tile * TILE, (tile + 1) * TILE)
        start = band_start(first_ref, base_ref, tile)
        local = ids_ref[:, span] - (base_ref[0] + start)
        hot = jnp.where(place == local, 1.0, 0.0).astype(BF16)
        total[pl.ds(start, BAND), :] += mm(hot, rows_ref[span, :])
    reach = len(outs) // 2
    for index, out in enumerate(outs):
        place = pl.multiple_of((reach + (index - reach) * side_ref[0]) * size, 16)
        out[...] = total[pl.ds(place, size), :].astype(BF16)


def pool(base, side, firsts, ids, rows, own_rows, count):
    block, width = rows.shape
    return pl.pallas_call(
        pool_kernel,
        out_shape=[shape((own_rows, width), BF16)] * count,
        in_specs=[SMEM, SMEM, SMEM, VMEM, VMEM],
        out_specs=[VMEM] * count,
        scratch_shapes=[pltpu.VMEM((count * own_rows + BAND, width), F32)],
        compiler_params=params(60),
        cost_estimate=cost(2 * BAND * block * width, 2 * block * width + 2 * count * own_rows * width),
        name="pool",
    )(base, side, firsts, ids, rows)


def select_kernel(base_ref, side_ref, first_ref, ids_ref, rows_ref, *refs):
    pieces, (out, table, sems) = refs[:-3], refs[-3:]
    size = pieces[0].shape[0]
    reach = len(pieces) // 2
    copies = []
    for index, piece in enumerate(pieces):
        away = (index + 1) // 2 * (1 if index % 2 else -1)
        place = pl.multiple_of((reach + away * side_ref[0]) * size, 16)
        copies.append(
            pltpu.make_async_copy(piece, table.at[pl.ds(place, size)], sems.at[index])
        )
    for copy in copies:
        copy.start()
    table[len(pieces) * size :, :] = jnp.zeros((BAND, table.shape[1]), BF16)
    for copy in copies:
        copy.wait()
    place = lax.broadcasted_iota(jnp.int32, (TILE, BAND), 1)
    for tile in range(rows_ref.shape[0] // TILE):
        span = slice(tile * TILE, (tile + 1) * TILE)
        start = band_start(first_ref, base_ref, tile)
        local = ids_ref[span, :] - (base_ref[0] + start)
        hot = jnp.where(place == local, 1.0, 0.0).astype(BF16)
        chosen = mm(hot, table[pl.ds(start, BAND), :])
        out[span, :] = (rows_ref[span, :].astype(F32) + chosen).astype(BF16)


def select(base, side, firsts, ids_column, rows, pieces, weight=1):
    block, width = rows.shape
    total = sum(piece.shape[0] for piece in pieces)
    return pl.pallas_call(
        select_kernel,
        out_shape=shape((block, width), BF16),
        in_specs=[SMEM, SMEM, SMEM, VMEM, VMEM] + [HBM] * len(pieces),
        out_specs=VMEM,
        scratch_shapes=[
            pltpu.VMEM((total + BAND, width), BF16),
            pltpu.SemaphoreType.DMA((len(pieces),)),
        ],
        compiler_params=params(60),
        cost_estimate=cost(
            2 * BAND * block * width, 4 * block * width + 2 * total * width, 0, weight
        ),
        name="select",
    )(base, side, firsts, ids_column, rows, *pieces)


def norm_parts(values):
    center = jnp.mean(values, axis=-1, keepdims=True)
    centered = values - center
    variance = jnp.mean(centered * centered, axis=-1, keepdims=True)
    scale = lax.rsqrt(variance + 1e-05)
    return centered * scale, scale


def norm_back(grad, xhat, scale, gain):
    e = grad * gain
    mean_e = jnp.mean(e, axis=-1, keepdims=True)
    mean_ex = jnp.mean(e * xhat, axis=-1, keepdims=True)
    return scale * (e - mean_e - xhat * mean_ex), jnp.sum(grad * xhat, axis=0, keepdims=True)


def partner(values):
    lanes = values.shape[1]
    lane = lax.broadcasted_iota(jnp.int32, values.shape, 1)
    return jnp.where(
        lax.rem(lane, 64) < 32, pltpu.roll(values, lanes - 32, 1), pltpu.roll(values, 32, 1)
    )


def dest(me, shift, parts):
    return lax.rem(me + shift, parts)


def source(me, shift, parts):
    return lax.rem(me + parts - shift, parts)


def pre_kernel(parts, info_ref, own, left, right, weight_ref, *refs):
    counts, gain, cosine, sine, pooled_ref, normed_ref = refs[:6]
    outs, refs = refs[6 : 6 + parts], refs[6 + parts :]
    sums, weight, pooled, normed, send, in_sems, out_sems = refs
    me = info_ref[0]
    loads = begin(
        [(own, sums.at[0]), (left, sums.at[1]), (right, sums.at[2]), (weight_ref, weight)], in_sems
    )
    end(loads[:3])
    total = sums[0].astype(F32) + sums[1].astype(F32) + sums[2].astype(F32)
    pooled[...] = total / counts[...]
    xhat, unused = norm_parts(pooled[...])
    normed[...] = (xhat * gain[...]).astype(BF16)
    stores = begin([(pooled, pooled_ref), (normed, normed_ref)], out_sems)
    loads[3].wait()
    width = pooled.shape[1]
    part = width // parts
    step = 256
    for kind in range(3):
        for first in range(0, width, step):
            column = kind * width + first
            wide = mm(normed[...], weight[:, column : column + step])
            for inner in range(0, step, 128):
                block = wide[:, inner : inner + 128]
                if kind < 2:
                    block = block * cosine[...] + partner(block) * sine[...]
                if kind == 0:
                    block = block * (1.0 / math.sqrt(width // HEADS))
                block = block.astype(BF16)
                for small in range(0, 128, min(part, 128)):
                    place = first + inner + small
                    offset = kind * part + place % part
                    send[place // part, :, offset : offset + min(part, 128)] = block[
                        :, small : small + min(part, 128)
                    ]
    end(stores)
    end(begin([(send.at[dest(me, k, parts)], out) for k, out in enumerate(outs)], out_sems))


def copy_in(pieces, place, sems, me, parts):
    copies = []
    for shift, piece in enumerate(pieces):
        copies.append(
            pltpu.make_async_copy(piece, place(source(me, shift, parts)), sems.at[shift])
        )
    for copy in copies:
        copy.start()
    return copies


def row_place(ref, rows):
    return lambda index: ref.at[pl.ds(pl.multiple_of(index * rows, 16), rows)]


def head_mask(tile, head, heads):
    if heads == 1:
        return tile
    lane = lax.broadcasted_iota(jnp.int32, tile.shape, 1)
    return jnp.where(lane // 64 == head, tile.astype(F32), 0.0).astype(BF16)


def attend_kernel(parts, heads, info_ref, *refs):
    pieces, refs = refs[:parts], refs[parts:]
    outs, refs = refs[:parts], refs[parts:]
    qkv_ref, out_ref, inverse_ref, prob_ref = refs[:4]
    qkv, out_t, v_t, scores, probs, attended, in_sems, prob_sems, out_sems = refs[4:]
    me = info_ref[0]
    rows, part = outs[0].shape
    tiles = qkv.shape[0] // TILE
    for copy in copy_in(pieces, row_place(qkv, rows), in_sems, me, parts):
        copy.wait()
    stores = begin([(qkv, qkv_ref)], out_sems)
    v_t[...] = qkv[:, 2 * part :].astype(F32).T.astype(BF16)
    key_index = lax.broadcasted_iota(jnp.int32, (TILE, TILE), 0)
    query_index = lax.broadcasted_iota(jnp.int32, (TILE, TILE), 1)
    started = []
    for head in range(heads):
        for tile in range(tiles):
            step = head * tiles + tile
            slot = step % 2
            columns = slice(tile * TILE, (tile + 1) * TILE)
            limit = (tile + 1) * TILE
            query = head_mask(qkv[columns, :part], head, heads)
            top = jnp.full((8, TILE), NEG, F32)
            for chunk in range(tile + 1):
                span = slice(chunk * TILE, (chunk + 1) * TILE)
                score = mm(qkv[span, part : 2 * part], query, NT)
                if chunk == tile:
                    score = jnp.where(key_index <= query_index, score, NEG)
                scores[slot, span, :] = score
                top = jnp.maximum(top, jnp.max(score.reshape(TILE // 8, 8, TILE), axis=0))
            top = jnp.max(top, axis=0, keepdims=True)
            if step >= 2:
                started[step - 2].wait()
            total = jnp.zeros((8, TILE), F32)
            for chunk in range(tile + 1):
                span = slice(chunk * TILE, (chunk + 1) * TILE)
                grown = jnp.exp(scores[slot, span, :] - top)
                probs[slot, span, :] = grown.astype(BF16)
                total = total + jnp.sum(grown.reshape(TILE // 8, 8, TILE), axis=0)
            inverse = 1.0 / jnp.sum(total, axis=0, keepdims=True)
            inverse_ref[head : head + 1, columns] = inverse
            copy = pltpu.make_async_copy(
                probs.at[slot, pl.ds(0, limit)],
                prob_ref.at[head, tile, pl.ds(0, limit)],
                prob_sems.at[slot],
            )
            copy.start()
            started.append(copy)
            height = slice(head * 64, (head + 1) * 64)
            out_t[height, columns] = mm(v_t[height, :limit], probs[slot, :limit, :]) * inverse
    copy = pltpu.make_async_copy(out_t, out_ref, out_sems.at[1])
    copy.start()
    attended[...] = out_t[...].T.astype(BF16)
    part_of = row_place(attended, rows)
    end(begin([(part_of(dest(me, k, parts)), out) for k, out in enumerate(outs)], in_sems))
    end(started[-2:] + stores + [copy])


def attend(info, pieces, parts, heads):
    rows, triple = pieces[0].shape
    part = triple // 3
    length = rows * parts
    tiles = length // TILE
    return pl.pallas_call(
        lambda *refs: attend_kernel(parts, heads, *refs),
        out_shape=[shape((rows, part), BF16) for unused in range(parts)]
        + [
            shape((length, triple), BF16),
            shape((part, length), F32),
            shape((8, length), F32),
            shape((heads, tiles, length, TILE), BF16),
        ],
        in_specs=[SMEM] + [HBM] * parts,
        out_specs=[HBM] * (parts + 2) + [VMEM, HBM],
        scratch_shapes=[
            pltpu.VMEM((length, triple), BF16),
            pltpu.VMEM((part, length), F32),
            pltpu.VMEM((part, length), BF16),
            pltpu.VMEM((2, length, TILE), F32),
            pltpu.VMEM((2, length, TILE), BF16),
            pltpu.VMEM((length, part), BF16),
            pltpu.SemaphoreType.DMA((parts,)),
            pltpu.SemaphoreType.DMA((2,)),
            pltpu.SemaphoreType.DMA((2,)),
        ],
        compiler_params=params(60),
        cost_estimate=cost(
            heads * length * length * 256,
            heads * length * length,
            heads * length * length // 2,
            WEIGHT,
        ),
        name="attend",
    )(info, *pieces)


def attend_back_kernel(parts, heads, info_ref, *refs):
    pieces, refs = refs[:parts], refs[parts:]
    inverse, prob_ref = refs[:2]
    sources, refs = refs[2:6], refs[6:]
    outs, refs = refs[:parts], refs[parts:]
    grads, k_t, delta, probs, dq_t, dk, dv, low = refs[:8]
    qkv, out_t, cosine, sine, in_sems, prob_sems, load_sems = refs[8:]
    me = info_ref[0]
    rows = pieces[0].shape[0]
    length, part = dk.shape
    tiles = length // TILE
    steps = [(head, tile) for head in range(heads) for tile in range(tiles)]

    def fetch(index):
        head, tile = steps[index]
        limit = (tile + 1) * TILE
        return pltpu.make_async_copy(
            prob_ref.at[head, tile, pl.ds(0, limit)],
            probs.at[index % 3, pl.ds(0, limit)],
            prob_sems.at[index % 3],
        )

    loads = begin(list(zip(sources, (qkv, out_t, cosine, sine))), load_sems)
    arrivals = copy_in(pieces, row_place(grads, rows), in_sems, me, parts)
    fetch(0).start()
    fetch(1).start()
    loads[0].wait()
    k_t[...] = qkv[:, part : 2 * part].astype(F32).T.astype(BF16)
    dk[...] = jnp.zeros_like(dk)
    dv[...] = jnp.zeros_like(dv)
    for copy in arrivals:
        copy.wait()
    turned_grads = grads[...].astype(F32).T
    turned_grads = jnp.concatenate(
        [turned_grads[h * 64 : (h + 1) * 64, :] * inverse[h : h + 1, :] for h in range(heads)]
    )
    grads[...] = turned_grads.T.astype(BF16)
    loads[1].wait()
    product = turned_grads * out_t[...]
    for head in range(heads):
        delta[head : head + 1, :] = jnp.sum(
            product[head * 64 : (head + 1) * 64, :], axis=0, keepdims=True
        )
    for index, (head, tile) in enumerate(steps):
        slot = index % 3
        if index + 2 < len(steps):
            fetch(index + 2).start()
        fetch(index).wait()
        columns = slice(tile * TILE, (tile + 1) * TILE)
        limit = (tile + 1) * TILE
        height = slice(head * 64, (head + 1) * 64)
        query = head_mask(qkv[columns, :part], head, heads)
        grad = head_mask(grads[columns, :], head, heads)
        shift = delta[head : head + 1, columns]
        dq = jnp.zeros((64, TILE), F32)
        for chunk in range(tile + 1):
            span = slice(chunk * TILE, (chunk + 1) * TILE)
            prob = probs[slot, span, :]
            grad_prob = mm(qkv[span, 2 * part :], grad, NT)
            grad_score = (prob.astype(F32) * (grad_prob - shift)).astype(BF16)
            dv[span, :] += mm(prob, grad)
            dk[span, :] += mm(grad_score, query)
            dq = dq + mm(k_t[height, span], grad_score)
        dq_t[height, columns] = dq
    end(loads[2:])
    head_scale = 1.0 / math.sqrt(64)
    turned = dq_t[...].T * head_scale
    for kind, values in enumerate((turned, dk[...], dv[...])):
        if kind < 2:
            values = values * cosine[:, :part] - partner(values) * sine[:, :part]
        low[:, kind * part : (kind + 1) * part] = values.astype(BF16)
    part_of = row_place(low, rows)
    end(begin([(part_of(dest(me, k, parts)), out) for k, out in enumerate(outs)], in_sems))


def attend_back(info, pieces, qkv, out_t, inverse, probs, cosine, sine, parts, heads):
    rows, part = pieces[0].shape
    length = rows * parts
    return pl.pallas_call(
        lambda *refs: attend_back_kernel(parts, heads, *refs),
        out_shape=[shape((rows, 3 * part), BF16) for unused in range(parts)],
        in_specs=[SMEM] + [HBM] * parts + [VMEM] + [HBM] * 5,
        out_specs=[HBM] * parts,
        scratch_shapes=[
            pltpu.VMEM((length, part), BF16),
            pltpu.VMEM((part, length), BF16),
            pltpu.VMEM((8, length), F32),
            pltpu.VMEM((3, length, TILE), BF16),
            pltpu.VMEM((part, length), F32),
            pltpu.VMEM((length, part), F32),
            pltpu.VMEM((length, part), F32),
            pltpu.VMEM((length, 3 * part), BF16),
            pltpu.VMEM(qkv.shape, BF16),
            pltpu.VMEM(out_t.shape, F32),
            pltpu.VMEM(cosine.shape, F32),
            pltpu.VMEM(sine.shape, F32),
            pltpu.SemaphoreType.DMA((parts,)),
            pltpu.SemaphoreType.DMA((3,)),
            pltpu.SemaphoreType.DMA((4,)),
        ],
        compiler_params=params(60),
        cost_estimate=cost(heads * length * length * 512, heads * length * length, 0, WEIGHT),
        name="attend_back",
    )(info, *pieces, inverse, probs, qkv, out_t, cosine, sine)


def pre(info, own, left, right, counts, gain, weight, cosine, sine, parts):
    rows, width = own.shape
    part = width // parts
    return pl.pallas_call(
        lambda *refs: pre_kernel(parts, *refs),
        out_shape=[shape((rows, width), F32), shape((rows, width), BF16)]
        + [shape((rows, 3 * part), BF16) for unused in range(parts)],
        in_specs=[SMEM] + [HBM] * 4 + [VMEM] * 4,
        out_specs=[HBM] * (2 + parts),
        scratch_shapes=[
            pltpu.VMEM((3, rows, width), BF16),
            pltpu.VMEM(weight.shape, BF16),
            pltpu.VMEM((rows, width), F32),
            pltpu.VMEM((rows, width), BF16),
            pltpu.VMEM((parts, rows, 3 * part), BF16),
            pltpu.SemaphoreType.DMA((4,)),
            pltpu.SemaphoreType.DMA((max(2, parts),)),
        ],
        compiler_params=params(60),
        cost_estimate=cost(6 * rows * width * width, 8 * rows * width + 6 * width * width),
        name="pre",
    )(info, own, left, right, weight, counts, gain, cosine, sine)


def ffn_kernel(parts, info_ref, *refs):
    pieces, refs = refs[:parts], refs[parts:]
    pooled_ref, out_ref, gain, up, bias, down, *cots = refs[:9]
    refs = refs[9:]
    result_ref, grad_hidden_ref, bias_grad, gain_grad, sent, kept = refs[:6]
    outs, refs = refs[6 : 6 + parts], refs[6 + parts :]
    attended_ref, normed_ref, ffn_ref, hidden_ref, forward, arrived, back, send = refs[:8]
    products, windows, pooled, out_weight, sems, product_sems, load_sems = refs[8:]
    me, bit = info_ref[0], info_ref[1]
    step = pl.program_id(0)
    steps = pl.num_programs(0)
    rows, width = pooled_ref.shape
    part = width // parts
    high = width // 2
    halves = sent.shape[0] // high

    def product_copy(index, target):
        place = pl.multiple_of(lax.rem(index, halves) * high, high)
        return pltpu.make_async_copy(
            products.at[index], target.at[pl.ds(place, high)], product_sems.at[index]
        )

    def give(index, value):
        products[index] = value.astype(BF16)

        @pl.when(index // halves == bit)
        def to_kept():
            product_copy(index, kept).start()

        @pl.when(index // halves != bit)
        def to_sent():
            product_copy(index, sent).start()

    @pl.when(step == 0)
    def first():
        copies = copy_in(pieces, lambda index: arrived.at[index], sems, me, parts)
        moves = [(out_ref, out_weight), (pooled_ref, pooled)]
        loads = begin(moves + [(cot, windows.at[k]) for k, cot in enumerate(cots)], load_sems)
        back[...] = jnp.zeros_like(back)
        end(copies + loads[:1])
        for index in range(parts):
            attended_ref[:, index * part : (index + 1) * part] = arrived[index]
        branch_in = mm(attended_ref[...], out_weight[...])
        end(loads[1:])
        ffn_ref[...] = sum(windows[k].astype(F32) for k in range(3)).astype(BF16)
        hidden = pooled[...] + branch_in
        hidden_ref[...] = hidden
        forward[...] = hidden
        xhat, unused = norm_parts(hidden)
        normed_ref[...] = (xhat * gain[...]).astype(BF16)

    gate_in = mm(normed_ref[...], up[...]) + bias[...]
    grad_active = mm(ffn_ref[...], down[...], NT)
    bell = 0.5 * (1.0 + lax.erf(gate_in * (1.0 / math.sqrt(2.0))))
    active = (gate_in * bell).astype(BF16)
    forward[...] += mm(active, down[...])
    slope = bell + gate_in * jnp.exp(-0.5 * gate_in * gate_in) * (1.0 / math.sqrt(2.0 * math.pi))
    grad_gate = (grad_active * slope).astype(BF16)
    bias_grad[...] = jnp.sum(grad_gate.astype(F32), axis=0, keepdims=True)
    back[...] += mm(grad_gate, up[...], NT)
    for half in range(2):
        side = slice(half * high, (half + 1) * high)
        give(2 * step + half, mm(active[:, side], ffn_ref[...], TN))
        give(2 * (steps + step) + half, mm(normed_ref[:, side], grad_gate, TN))

    @pl.when(step == pl.num_programs(0) - 1)
    def last():
        result_ref[...] = forward[...].astype(BF16)
        xhat, scale = norm_parts(hidden_ref[...])
        grad, gain_sum = norm_back(back[...], xhat, scale, gain[...])
        gain_grad[...] = gain_sum
        grad_hidden = ffn_ref[...].astype(F32) + grad
        grad_hidden_ref[...] = grad_hidden
        branch = grad_hidden.astype(BF16)
        for half in range(2):
            side = slice(half * high, (half + 1) * high)
            give(4 * steps + half, mm(attended_ref[:, side], branch, TN))
        attended_grad = mm(branch, out_weight[...], NT).astype(BF16)
        for index in range(parts):
            send[index] = attended_grad[:, index * part : (index + 1) * part]
        moves = [(send.at[dest(me, k, parts)], out) for k, out in enumerate(outs)]
        copies = begin(moves, sems)
        for index in range(2 * halves):
            product_copy(index, kept).wait()
        end(copies)


def ffn(info, pieces, pooled, out_weight, gain, up, bias, down, cots, parts):
    rows, width = pooled.shape
    units = up.shape[1]
    part = width // parts
    chunk = 512
    whole = lambda *dims: pl.BlockSpec(dims, lambda step: (0,) * len(dims))
    line = pl.BlockSpec((1, chunk), lambda step: (0, step))
    square = whole(rows, width)
    return pl.pallas_call(
        lambda *refs: ffn_kernel(parts, *refs),
        grid=(units // chunk,),
        out_shape=[
            shape((rows, width), BF16),
            shape((rows, width), F32),
            shape((1, units), F32),
            shape((1, width), F32),
            shape((units + width // 2, width), BF16),
            shape((units + width // 2, width), BF16),
        ]
        + [shape((rows, part), BF16) for unused in range(parts)],
        in_specs=[SMEM]
        + [HBM] * parts
        + [
            HBM,
            HBM,
            whole(1, width),
            pl.BlockSpec((width, chunk), lambda step: (0, step)),
            line,
            pl.BlockSpec((chunk, width), lambda step: (step, 0)),
            HBM,
            HBM,
            HBM,
        ],
        out_specs=[square, square, line, whole(1, width), HBM, HBM] + [HBM] * parts,
        scratch_shapes=[
            pltpu.VMEM((rows, width), BF16),
            pltpu.VMEM((rows, width), BF16),
            pltpu.VMEM((rows, width), BF16),
            pltpu.VMEM((rows, width), F32),
            pltpu.VMEM((rows, width), F32),
            pltpu.VMEM((parts, rows, part), BF16),
            pltpu.VMEM((rows, width), F32),
            pltpu.VMEM((parts, rows, part), BF16),
            pltpu.VMEM((4 * units // width + 2, width // 2, width), BF16),
            pltpu.VMEM((3, rows, width), BF16),
            pltpu.VMEM((rows, width), F32),
            pltpu.VMEM((width, width), BF16),
            pltpu.SemaphoreType.DMA((parts,)),
            pltpu.SemaphoreType.DMA((4 * units // width + 2,)),
            pltpu.SemaphoreType.DMA((5,)),
        ],
        compiler_params=params(60),
        cost_estimate=cost(
            12 * rows * width * units + 4 * rows * width * width, 12 * width * units, 2 * rows * units, WEIGHT
        ),
        name="ffn",
    )(info, *pieces, pooled, out_weight, gain, up, bias, down, *cots)


def post_kernel(parts, info_ref, *refs):
    pieces, refs = refs[:parts], refs[parts:]
    sources, (counts, gain, bias, ffn_gain) = refs[:4], refs[4:8]
    share_ref, sent_ref, kept_ref, arrived, low, share, products, small = refs[8:16]
    pooled, weight, normed, grad_hidden, sems, load_sems, out_sems = refs[16:]
    me, bit = info_ref[0], info_ref[1]
    rows, width = pooled.shape
    part = width // parts
    half = width // 2
    copies = copy_in(pieces, lambda index: arrived.at[index], sems, me, parts)
    loads = begin(list(zip(sources, (pooled, weight, normed, grad_hidden))), load_sems)
    loads[0].wait()
    xhat, scale = norm_parts(pooled[...])
    end(copies)
    for index in range(parts):
        for kind in range(3):
            place = kind * width + index * part
            low[:, place : place + part] = arrived[index, :, kind * part : (kind + 1) * part]
    loads[1].wait()
    grad, gain_sum = norm_back(mm(low[...], weight[...], NT), xhat, scale, gain[...])
    small[...] = jnp.zeros_like(small)
    lines = bias.shape[1] // width
    for line in range(lines):
        small[line : line + 1, :] = bias[:, line * width : (line + 1) * width]
    small[lines : lines + 1, :] = ffn_gain[...]
    small[lines + 1 : lines + 2, :] = gain_sum
    loads[2].wait()
    stores = []
    for index, out in enumerate((sent_ref, kept_ref)):
        first = pl.multiple_of((1 - bit if index == 0 else bit) * half, 128)
        value = mm(normed[:, pl.ds(first, half)], low[...], TN)
        products[index, :, : 3 * width] = value.astype(BF16)
        products[index, :, 3 * width :] = small[:, pl.ds(first, half)].T.astype(BF16)
        stores += begin([(products.at[index], out)], out_sems.at[pl.ds(index, 1)])
    loads[3].wait()
    share[...] = ((grad_hidden[...] + grad) / counts[...]).astype(BF16)
    end(stores + begin([(share, share_ref)], out_sems.at[pl.ds(2, 1)]))


def post(info, pieces, pooled, weight, normed, grad_hidden, counts, gain, bias, ffn_gain, parts):
    rows, width = pooled.shape
    part = width // parts
    half = shape((width // 2, 3 * width + 128), BF16)
    return pl.pallas_call(
        lambda *refs: post_kernel(parts, *refs),
        out_shape=[shape((rows, width), BF16), half, half],
        in_specs=[SMEM] + [HBM] * (parts + 4) + [VMEM] * 4,
        out_specs=[HBM] * 3,
        scratch_shapes=[
            pltpu.VMEM((parts, rows, 3 * part), BF16),
            pltpu.VMEM((rows, 3 * width), BF16),
            pltpu.VMEM((rows, width), BF16),
            pltpu.VMEM((2,) + half.shape, BF16),
            pltpu.VMEM((128, width), F32),
            pltpu.VMEM((rows, width), F32),
            pltpu.VMEM(weight.shape, BF16),
            pltpu.VMEM((rows, width), BF16),
            pltpu.VMEM((rows, width), F32),
            pltpu.SemaphoreType.DMA((parts,)),
            pltpu.SemaphoreType.DMA((4,)),
            pltpu.SemaphoreType.DMA((3,)),
        ],
        compiler_params=params(60),
        cost_estimate=cost(12 * rows * width * width, 8 * rows * width + 6 * width * width, 0, WEIGHT),
        name="post",
    )(info, *pieces, pooled, weight, normed, grad_hidden, counts, gain, bias, ffn_gain)


def ffn_result_kernel(bit_ref, own, other, down, up, out, whole, wide, in_sems, out_sems):
    half, width = own.shape
    units = down.shape[0]
    high = width // 2
    blocks = 2 * half // high
    bit = bit_ref[0]

    def arrival(index, source):
        place = index * high % half
        return pltpu.make_async_copy(
            source.at[pl.ds(place, high)], whole.at[index], in_sems.at[index]
        )

    for index in range(blocks):
        mine = index * high // half == bit

        @pl.when(mine)
        def from_own():
            arrival(index, own).start()

        @pl.when(jnp.logical_not(mine))
        def from_other():
            arrival(index, other).start()

    copies = []
    for index in range(blocks):
        arrival(index, own).wait()
        wide[index] = whole[index].astype(F32)
        first = index * high
        if first < units:
            target = down.at[pl.ds(first, high)]
        elif first < 2 * units:
            column = (first - units) // width * width
            target = up.at[pl.ds(first % width, high), pl.ds(column, width)]
        else:
            target = out.at[pl.ds(first - 2 * units, high)]
        copies.append(pltpu.make_async_copy(wide.at[index], target, out_sems.at[index]))
        copies[-1].start()
    end(copies)


def ffn_result(bit, own, other, units):
    half, width = own.shape
    high = width // 2
    blocks = 2 * half // high
    return pl.pallas_call(
        ffn_result_kernel,
        out_shape=[shape((units, width), F32), shape((width, units), F32), shape((width, width), F32)],
        in_specs=[SMEM, HBM, HBM],
        out_specs=[HBM] * 3,
        scratch_shapes=[
            pltpu.VMEM((blocks, high, width), BF16),
            pltpu.VMEM((blocks, high, width), F32),
            pltpu.SemaphoreType.DMA((blocks,)),
            pltpu.SemaphoreType.DMA((blocks,)),
        ],
        compiler_params=params(60),
        cost_estimate=cost(0, 12 * half * width),
        name="ffn_result",
    )(bit, own, other)


def qkv_result_kernel(bit_ref, own, other, out, small):
    value = jnp.where(
        pl.program_id(0) == bit_ref[0], own[...].astype(F32), other[...].astype(F32)
    )
    wide = out.shape[1]
    out[...] = value[:, :wide]
    small[...] = value[:, wide:].T[: small.shape[0], :]


def qkv_result(bit, own, other):
    half, wide = own.shape
    piece = pl.BlockSpec((half, wide), lambda step, ref: (0, 0))
    return pl.pallas_call(
        qkv_result_kernel,
        grid_spec=pltpu.PrefetchScalarGridSpec(
            num_scalar_prefetch=1,
            grid=(2,),
            in_specs=[piece, piece],
            out_specs=[
                pl.BlockSpec((half, wide - 128), lambda step, ref: (step, 0)),
                pl.BlockSpec((8, half), lambda step, ref: (0, step)),
            ],
        ),
        out_shape=[shape((2 * half, wide - 128), F32), shape((8, 2 * half), F32)],
        compiler_params=params(60),
        cost_estimate=cost(0, 12 * half * wide, 0, 4 * WEIGHT),
        name="qkv_result",
    )(bit, own, other)


def join_kernel(order_ref, *refs):
    pieces, out = refs[:-1], refs[-1]
    size = pieces[0].shape[0]
    for index, piece in enumerate(pieces):
        out[pl.ds(pl.multiple_of(order_ref[index] * size, size), size), :] = piece[...]


def join(pieces, order):
    size, width = pieces[0].shape
    count = len(pieces)
    if size % 16:
        whole = jnp.zeros((count * size, width), BF16)
        for index, piece in enumerate(pieces):
            whole = lax.dynamic_update_slice_in_dim(whole, piece, order[index] * size, 0)
        return whole
    return pl.pallas_call(
        join_kernel,
        out_shape=shape((count * size, width), BF16),
        in_specs=[SMEM] + [VMEM] * count,
        out_specs=VMEM,
        compiler_params=params(60),
        cost_estimate=cost(0, 4 * count * size * width),
        name="join",
    )(order, *pieces)


def pairwise(values, odd, parts):
    firsts = range(1 if odd else 0, parts - 1, 2)
    pairs = [(i, i + 1) for i in firsts] + [(i + 1, i) for i in firsts]
    return lax.ppermute(values, "seq", pairs)


def rotated(values, shift, parts):
    return lax.ppermute(values, "seq", [(i, (i + shift) % parts) for i in range(parts)])


def swap(values):
    return lax.ppermute(values, "core", [(0, 1), (1, 0)])


def turned(values, axis):
    return lax.all_to_all(values, axis, 0, 0)


def add_low(first, second):
    return (first.astype(F32) + second.astype(F32)).astype(BF16)


def total_of(values):
    return jnp.sum(values.astype(F32), axis=0).astype(BF16)


def sum_plane_out(half, chips):
    rows, width = half.shape
    return turned(half.reshape(chips, rows // chips, width), "chip")


def sum_plane_back(own, chips):
    chunks = turned(jnp.broadcast_to(own, (chips,) + own.shape), "chip")
    return chunks.reshape(chips * own.shape[0], own.shape[1])


class SeqSum:
    def __init__(self, pieces, me, parts):
        self.values, self.me, self.parts = pieces, me, parts
        self.bits = parts.bit_length() - 1
        self.ways = [(bit, 0) for bit in range(self.bits - 1)] + [(self.bits - 1, 1)]
        self.ways += [(bit, 2) for bit in reversed(range(self.bits - 1))]

    def exchange(self, values, bit):
        return lax.ppermute(values, "seq", [(i, i ^ (1 << bit)) for i in range(self.parts)])

    def start(self, way):
        bit, kind = self.ways[way]
        if kind == 0:
            half = self.values.shape[1] // 2
            mine = (self.me >> bit) & 1
            piece = lambda side: total_of(
                lax.dynamic_slice_in_dim(self.values, side * half, half, 1)
            )
            self.kept, self.sent = piece(mine), piece(1 - mine)
            return self.exchange(self.sent, bit)
        if kind == 1:
            self.kept = total_of(self.values)
        else:
            self.kept = self.values
        self.sent = self.kept
        return self.exchange(self.sent, bit)

    def finish(self, way, got):
        bit, kind = self.ways[way]
        if kind < 2:
            self.values = add_low(self.kept, got)
            if kind == 0 or way + 1 == len(self.ways):
                self.values = self.values[None] if kind == 0 else self.values
            return
        first = ((self.me >> bit) & 1) == 0
        low, high = jnp.where(first, self.kept, got), jnp.where(first, got, self.kept)
        self.values = jnp.concatenate([low, high], axis=0)


def near_pieces(own, chips):
    pairs = lambda k: [(i, i ^ k) for i in range(chips)]
    return [lax.ppermute(own, "chip", pairs(k)) if k else own for k in range(chips)]


def join_near(pieces):
    chip = lax.axis_index("chip")
    return join(pieces, jnp.stack([chip ^ k for k in range(len(pieces))]).astype(jnp.int32))


def after(values, *earlier):
    return lax.optimization_barrier((values,) + earlier)[0]


def tie(*groups):
    return lax.optimization_barrier(groups)


def body(
    byte_input_rows,
    segment_ids,
    attn_gain,
    qkv_weight,
    out_weight,
    ffn_gain,
    up_weight,
    up_bias,
    down_weight,
    cotangent,
):
    rows_in, cot = byte_input_rows[0], cotangent[0]
    ids = segment_ids
    block, width = rows_in.shape
    parts, chips = lax.axis_size("seq"), lax.axis_size("chip")
    me, core = lax.axis_index("seq"), lax.axis_index("core")
    own_rows = SEG_DEV
    length = own_rows * parts
    heads = HEADS // parts
    reach = reach_of(parts, own_rows, block)
    place = jnp.stack([me, core]).astype(jnp.int32)
    base = ((me - reach) * own_rows).astype(jnp.int32)[None]
    side = (1 - 2 * (me & 1)).astype(jnp.int32)[None]
    firsts = ids[0, ::TILE]

    def both_ways(carried):
        return [pairwise(carried[0], False, parts), pairwise(carried[1], True, parts)]

    def to_owners(windows, hold=lambda carried: carried):
        carried = [windows[2 * reach], windows[0]]
        for away in range(reach - 1, -1, -1):
            carried = both_ways(carried)
            if away:
                carried = [
                    add_low(carried[1], windows[reach + away]),
                    add_low(carried[0], windows[reach - away]),
                ]
                carried = hold(carried)
        return [windows[reach]] + carried

    def exchange(messages):
        return [messages[0]] + [
            rotated(message, shift, parts) for shift, message in enumerate(messages) if shift
        ]

    half = 32
    lane = jnp.arange(128, dtype=jnp.int32)
    frequency = jnp.exp((lane % half).astype(F32) * (-math.log(10000.0) / half))
    angles = jnp.arange(length, dtype=jnp.int32).astype(F32)[:, None] * frequency[None, :]
    cosine = jnp.cos(angles)
    sine = jnp.sin(angles) * jnp.where(lane % 64 < half, -1.0, 1.0)
    own_cosine = lax.dynamic_slice_in_dim(cosine, me * own_rows, own_rows, 0)
    own_sine = lax.dynamic_slice_in_dim(sine, me * own_rows, own_rows, 0)

    windows = pool(base, side, firsts, ids, rows_in, own_rows, 2 * reach + 1)
    cot_windows = pool(base, side, firsts, ids, after(cot, windows), own_rows, 2 * reach + 1)

    def behind_first(carried):
        nonlocal cot_windows
        carried, cot_windows = tie(carried, cot_windows)
        return carried

    sums_in = to_owners(windows, behind_first)
    ids_late = after(ids, windows)
    ids_all = turned(jnp.broadcast_to(ids_late, (parts,) + ids.shape), "seq")
    positions = me * own_rows + jnp.arange(own_rows, dtype=jnp.int32)
    same = ids_all.reshape(1, -1) == positions[:, None]
    counts = jnp.sum(same.astype(F32), axis=1, keepdims=True)
    ids_column = ids.reshape(block, 1)

    gain_row = attn_gain[None, :]
    pooled, normed_attn, *qkv_out = pre(
        place, *sums_in, counts, gain_row, qkv_weight, own_cosine, own_sine, parts
    )
    qkv_in = exchange(qkv_out)
    cots_in = to_owners(cot_windows, lambda carried: after(carried, qkv_in))
    *attended_out, qkv, out_t, inverse, probs = attend(place, qkv_in, parts, heads)
    attended_in = exchange(attended_out)
    (
        pooled_out,
        grad_hidden,
        grad_bias,
        grad_ffn_gain,
        sent,
        kept,
        *grads_out,
    ) = ffn(
        place,
        attended_in,
        pooled,
        out_weight,
        ffn_gain[None, :],
        up_weight,
        up_bias[None, :],
        down_weight,
        cots_in,
        parts,
    )
    bit = core.astype(jnp.int32)[None]

    grads_in = exchange(grads_out)
    half = add_low(kept, swap(sent))
    grads_in = after(grads_in, half)
    pieces = sum_plane_out(half, chips)
    pooled_hop = both_ways(after([pooled_out, pooled_out], grads_in))
    pooled_in = [pooled_out] + pooled_hop
    low_out = attend_back(
        place, grads_in, qkv, out_t, inverse, probs, cosine, sine, parts, heads
    )
    low_out, pooled_hop = tie(low_out, pooled_hop)
    low_in = exchange(low_out)
    low_in, pieces = tie(low_in, pieces)
    ffn_sum = SeqSum(pieces, me, parts)
    ways = len(ffn_sum.ways)
    got = ffn_sum.start(0)
    low_in = after(low_in, ffn_sum.sent)
    share, qkv_sent, qkv_kept = post(
        place,
        low_in,
        pooled,
        qkv_weight,
        normed_attn,
        grad_hidden,
        counts,
        gain_row,
        grad_bias,
        grad_ffn_gain,
        parts,
    )

    share_hop = both_ways([share, share])
    share_in = [share] + share_hop
    ffn_sum.finish(0, after(got, qkv_sent))
    pieces = sum_plane_out(add_low(qkv_kept, swap(qkv_sent)), chips)
    qkv_sum = SeqSum(pieces, me, parts)
    if ways > 1:
        ffn_sum.finish(1, after(ffn_sum.start(1), pieces))
    pooled_hop = after(pooled_hop, share)
    for unused in range(1, reach):
        pooled_hop = both_ways(pooled_hop[::-1])
        pooled_in += pooled_hop
    for way in range(ways):
        qkv_sum.finish(way, qkv_sum.start(way))
        if way == 0:
            qkv_sum.values, share_hop, pooled_in = tie(qkv_sum.values, share_hop, pooled_in)
        if way + 2 < ways:
            ffn_sum.finish(way + 2, after(ffn_sum.start(way + 2), qkv_sum.values))
    ffn_own = sum_plane_back(ffn_sum.values, chips)
    share_hop = after(share_hop, qkv_sum.values)
    for unused in range(1, reach):
        share_hop = both_ways(share_hop[::-1])
        share_in += share_hop
    near = near_pieces(qkv_sum.values, chips)
    grad_input = select(base, side, firsts, ids_column, cot, share_in)
    layer_out = select(base, side, firsts, ids_column, rows_in, pooled_in)
    qkv_own = join_near(after(near, grad_input, layer_out))
    units = up_weight.shape[1]
    ffn_own = after(ffn_own, qkv_own)
    grad_down, grad_up, grad_out = ffn_result(bit, ffn_own, swap(ffn_own), units)
    grad_qkv, small = qkv_result(bit, qkv_own, swap(qkv_own))
    lines = units // width
    return (
        layer_out[None],
        grad_input[None],
        small[lines + 1],
        grad_qkv,
        grad_out,
        small[lines],
        grad_up,
        small[:lines].reshape(units),
        grad_down,
    )


def solution(mesh):
    dp, seq = mesh.shape["dp"], mesh.shape["seq"]
    inner = jax.sharding.Mesh(mesh.devices.reshape(dp // 2, 2, seq), ("chip", "core", "seq"))
    rows, ids = P(("chip", "core"), "seq", None), P(("chip", "core"), "seq")
    placed = (rows, ids, P(), P(), P(), P(), P(), P(), P(), rows)
    return jax.shard_map(
        body,
        mesh=inner,
        in_specs=placed,
        out_specs=(rows, rows, P(), P(), P(), P(), P(), P(), P()),
        check_vma=False,
    )
```

```python
import math

import jax
import jax.numpy as jnp
import numpy as np
from jax import lax
from jax.experimental import pallas as pl
from jax.experimental.pallas import tpu as pltpu
from jax.sharding import PartitionSpec as P

HEADS = 8
SEG_DEV = 448
TILE = 256
BAND = TILE + 16
WEIGHT = 20
NEG = -1e30
NN = (((1,), (0,)), ((), ()))
NT = (((1,), (1,)), ((), ()))
TN = (((0,), (0,)), ((), ()))
F32 = jnp.float32
BF16 = jnp.bfloat16

SMEM = pl.BlockSpec(memory_space=pltpu.SMEM)
VMEM = pl.BlockSpec(memory_space=pltpu.VMEM)
HBM = pl.BlockSpec(memory_space=pltpu.HBM)


def mm(left, right, dims=NN):
    return lax.dot_general(left, right, dims, preferred_element_type=F32)


def shape(dims, kind):
    return jax.ShapeDtypeStruct(dims, kind)


def cost(flops, moved, exps=0, weight=1):
    return pl.CostEstimate(
        flops=int(weight * flops), bytes_accessed=int(weight * moved), transcendentals=int(weight * exps)
    )


def params(mebibytes):
    return pltpu.CompilerParams(vmem_limit_bytes=int(mebibytes * 1024 * 1024))


def begin(moves, sems):
    copies = [pltpu.make_async_copy(*move, sems.at[index]) for index, move in enumerate(moves)]
    for copy in copies:
        copy.start()
    return copies


def end(copies):
    for copy in copies:
        copy.wait()


def reach_of(parts, rows, block):
    total = rows * parts
    reach = 0
    for d in range(parts):
        low = max(0, total - (parts - d) * block)
        high = min(total, (d + 1) * block) - 1
        reach = max(reach, d - low // rows, high // rows - d)
    return reach


def band_start(first_ref, base_ref, tile):
    return pl.multiple_of((first_ref[0, tile * TILE] - base_ref[0]) // 16 * 16, 16)


def pool_kernel(base_ref, side_ref, first_ref, ids_ref, rows_ref, *refs):
    outs, total = refs[:-1], refs[-1]
    size = outs[0].shape[0]
    total[...] = jnp.zeros_like(total)
    place = lax.broadcasted_iota(jnp.int32, (BAND, TILE), 0)
    for tile in range(rows_ref.shape[0] // TILE):
        span = slice(tile * TILE, (tile + 1) * TILE)
        start = band_start(first_ref, base_ref, tile)
        local = ids_ref[:, span] - (base_ref[0] + start)
        hot = jnp.where(place == local, 1.0, 0.0).astype(BF16)
        total[pl.ds(start, BAND), :] += mm(hot, rows_ref[span, :])
    reach = len(outs) // 2
    for index, out in enumerate(outs):
        place = pl.multiple_of((reach + (index - reach) * side_ref[0]) * size, 16)
        out[...] = total[pl.ds(place, size), :].astype(BF16)


def pool(base, side, firsts, ids, rows, own_rows, count):
    block, width = rows.shape
    return pl.pallas_call(
        pool_kernel,
        out_shape=[shape((own_rows, width), BF16)] * count,
        in_specs=[SMEM, SMEM, SMEM, VMEM, VMEM],
        out_specs=[VMEM] * count,
        scratch_shapes=[pltpu.VMEM((count * own_rows + BAND, width), F32)],
        compiler_params=params(60),
        cost_estimate=cost(2 * BAND * block * width, 2 * block * width + 2 * count * own_rows * width),
        name="pool",
    )(base, side, firsts, ids, rows)


def select_kernel(base_ref, side_ref, first_ref, ids_ref, rows_ref, *refs):
    pieces, (out, table, sems) = refs[:-3], refs[-3:]
    size = pieces[0].shape[0]
    reach = len(pieces) // 2
    copies = []
    for index, piece in enumerate(pieces):
        away = (index + 1) // 2 * (1 if index % 2 else -1)
        place = pl.multiple_of((reach + away * side_ref[0]) * size, 16)
        copies.append(
            pltpu.make_async_copy(piece, table.at[pl.ds(place, size)], sems.at[index])
        )
    for copy in copies:
        copy.start()
    table[len(pieces) * size :, :] = jnp.zeros((BAND, table.shape[1]), BF16)
    for copy in copies:
        copy.wait()
    place = lax.broadcasted_iota(jnp.int32, (TILE, BAND), 1)
    for tile in range(rows_ref.shape[0] // TILE):
        span = slice(tile * TILE, (tile + 1) * TILE)
        start = band_start(first_ref, base_ref, tile)
        local = ids_ref[span, :] - (base_ref[0] + start)
        hot = jnp.where(place == local, 1.0, 0.0).astype(BF16)
        chosen = mm(hot, table[pl.ds(start, BAND), :])
        out[span, :] = (rows_ref[span, :].astype(F32) + chosen).astype(BF16)


def select(base, side, firsts, ids_column, rows, pieces, weight=1):
    block, width = rows.shape
    total = sum(piece.shape[0] for piece in pieces)
    return pl.pallas_call(
        select_kernel,
        out_shape=shape((block, width), BF16),
        in_specs=[SMEM, SMEM, SMEM, VMEM, VMEM] + [HBM] * len(pieces),
        out_specs=VMEM,
        scratch_shapes=[
            pltpu.VMEM((total + BAND, width), BF16),
            pltpu.SemaphoreType.DMA((len(pieces),)),
        ],
        compiler_params=params(60),
        cost_estimate=cost(
            2 * BAND * block * width, 4 * block * width + 2 * total * width, 0, weight
        ),
        name="select",
    )(base, side, firsts, ids_column, rows, *pieces)


def norm_parts(values):
    center = jnp.mean(values, axis=-1, keepdims=True)
    centered = values - center
    variance = jnp.mean(centered * centered, axis=-1, keepdims=True)
    scale = lax.rsqrt(variance + 1e-05)
    return centered * scale, scale


def norm_back(grad, xhat, scale, gain):
    e = grad * gain
    mean_e = jnp.mean(e, axis=-1, keepdims=True)
    mean_ex = jnp.mean(e * xhat, axis=-1, keepdims=True)
    return scale * (e - mean_e - xhat * mean_ex), jnp.sum(grad * xhat, axis=0, keepdims=True)


def partner(values):
    lanes = values.shape[1]
    lane = lax.broadcasted_iota(jnp.int32, values.shape, 1)
    return jnp.where(
        lax.rem(lane, 64) < 32, pltpu.roll(values, lanes - 32, 1), pltpu.roll(values, 32, 1)
    )


def dest(me, shift, parts):
    return lax.rem(me + shift, parts)


def source(me, shift, parts):
    return lax.rem(me + parts - shift, parts)


def pre_kernel(parts, info_ref, own, left, right, weight_ref, *refs):
    counts, gain, cosine, sine, pooled_ref, normed_ref = refs[:6]
    outs, refs = refs[6 : 6 + parts], refs[6 + parts :]
    sums, weight, pooled, normed, send, in_sems, out_sems = refs
    me = info_ref[0]
    loads = begin(
        [(own, sums.at[0]), (left, sums.at[1]), (right, sums.at[2]), (weight_ref, weight)], in_sems
    )
    end(loads[:3])
    total = sums[0].astype(F32) + sums[1].astype(F32) + sums[2].astype(F32)
    pooled[...] = total / counts[...]
    xhat, unused = norm_parts(pooled[...])
    normed[...] = (xhat * gain[...]).astype(BF16)
    stores = begin([(pooled, pooled_ref), (normed, normed_ref)], out_sems)
    loads[3].wait()
    width = pooled.shape[1]
    part = width // parts
    step = 256
    for kind in range(3):
        for first in range(0, width, step):
            column = kind * width + first
            wide = mm(normed[...], weight[:, column : column + step])
            for inner in range(0, step, 128):
                block = wide[:, inner : inner + 128]
                if kind < 2:
                    block = block * cosine[...] + partner(block) * sine[...]
                if kind == 0:
                    block = block * (1.0 / math.sqrt(width // HEADS))
                block = block.astype(BF16)
                for small in range(0, 128, min(part, 128)):
                    place = first + inner + small
                    offset = kind * part + place % part
                    send[place // part, :, offset : offset + min(part, 128)] = block[
                        :, small : small + min(part, 128)
                    ]
    end(stores)
    end(begin([(send.at[dest(me, k, parts)], out) for k, out in enumerate(outs)], out_sems))


def copy_in(pieces, place, sems, me, parts):
    copies = []
    for shift, piece in enumerate(pieces):
        copies.append(
            pltpu.make_async_copy(piece, place(source(me, shift, parts)), sems.at[shift])
        )
    for copy in copies:
        copy.start()
    return copies


def row_place(ref, rows):
    return lambda index: ref.at[pl.ds(pl.multiple_of(index * rows, 16), rows)]


def head_mask(tile, head, heads):
    if heads == 1:
        return tile
    lane = lax.broadcasted_iota(jnp.int32, tile.shape, 1)
    return jnp.where(lane // 64 == head, tile.astype(F32), 0.0).astype(BF16)


def attend_kernel(parts, heads, info_ref, *refs):
    pieces, refs = refs[:parts], refs[parts:]
    outs, refs = refs[:parts], refs[parts:]
    qkv_ref, out_ref, inverse_ref, prob_ref = refs[:4]
    qkv, out_t, v_t, scores, probs, attended, in_sems, prob_sems, out_sems = refs[4:]
    me = info_ref[0]
    rows, part = outs[0].shape
    tiles = qkv.shape[0] // TILE
    for copy in copy_in(pieces, row_place(qkv, rows), in_sems, me, parts):
        copy.wait()
    stores = begin([(qkv, qkv_ref)], out_sems)
    v_t[...] = qkv[:, 2 * part :].astype(F32).T.astype(BF16)
    key_index = lax.broadcasted_iota(jnp.int32, (TILE, TILE), 0)
    query_index = lax.broadcasted_iota(jnp.int32, (TILE, TILE), 1)
    started = []
    for head in range(heads):
        for tile in range(tiles):
            step = head * tiles + tile
            slot = step % 2
            columns = slice(tile * TILE, (tile + 1) * TILE)
            limit = (tile + 1) * TILE
            query = head_mask(qkv[columns, :part], head, heads)
            top = jnp.full((8, TILE), NEG, F32)
            for chunk in range(tile + 1):
                span = slice(chunk * TILE, (chunk + 1) * TILE)
                score = mm(qkv[span, part : 2 * part], query, NT)
                if chunk == tile:
                    score = jnp.where(key_index <= query_index, score, NEG)
                scores[slot, span, :] = score
                top = jnp.maximum(top, jnp.max(score.reshape(TILE // 8, 8, TILE), axis=0))
            top = jnp.max(top, axis=0, keepdims=True)
            if step >= 2:
                started[step - 2].wait()
            total = jnp.zeros((8, TILE), F32)
            for chunk in range(tile + 1):
                span = slice(chunk * TILE, (chunk + 1) * TILE)
                grown = jnp.exp(scores[slot, span, :] - top)
                probs[slot, span, :] = grown.astype(BF16)
                total = total + jnp.sum(grown.reshape(TILE // 8, 8, TILE), axis=0)
            inverse = 1.0 / jnp.sum(total, axis=0, keepdims=True)
            inverse_ref[head : head + 1, columns] = inverse
            copy = pltpu.make_async_copy(
                probs.at[slot, pl.ds(0, limit)],
                prob_ref.at[head, tile, pl.ds(0, limit)],
                prob_sems.at[slot],
            )
            copy.start()
            started.append(copy)
            height = slice(head * 64, (head + 1) * 64)
            out_t[height, columns] = mm(v_t[height, :limit], probs[slot, :limit, :]) * inverse
    copy = pltpu.make_async_copy(out_t, out_ref, out_sems.at[1])
    copy.start()
    attended[...] = out_t[...].T.astype(BF16)
    part_of = row_place(attended, rows)
    end(begin([(part_of(dest(me, k, parts)), out) for k, out in enumerate(outs)], in_sems))
    end(started[-2:] + stores + [copy])


def attend(info, pieces, parts, heads):
    rows, triple = pieces[0].shape
    part = triple // 3
    length = rows * parts
    tiles = length // TILE
    return pl.pallas_call(
        lambda *refs: attend_kernel(parts, heads, *refs),
        out_shape=[shape((rows, part), BF16) for unused in range(parts)]
        + [
            shape((length, triple), BF16),
            shape((part, length), F32),
            shape((8, length), F32),
            shape((heads, tiles, length, TILE), BF16),
        ],
        in_specs=[SMEM] + [HBM] * parts,
        out_specs=[HBM] * (parts + 2) + [VMEM, HBM],
        scratch_shapes=[
            pltpu.VMEM((length, triple), BF16),
            pltpu.VMEM((part, length), F32),
            pltpu.VMEM((part, length), BF16),
            pltpu.VMEM((2, length, TILE), F32),
            pltpu.VMEM((2, length, TILE), BF16),
            pltpu.VMEM((length, part), BF16),
            pltpu.SemaphoreType.DMA((parts,)),
            pltpu.SemaphoreType.DMA((2,)),
            pltpu.SemaphoreType.DMA((2,)),
        ],
        compiler_params=params(60),
        cost_estimate=cost(
            heads * length * length * 256,
            heads * length * length,
            heads * length * length // 2,
            WEIGHT,
        ),
        name="attend",
    )(info, *pieces)


def attend_back_kernel(parts, heads, info_ref, *refs):
    pieces, refs = refs[:parts], refs[parts:]
    inverse, prob_ref = refs[:2]
    sources, refs = refs[2:6], refs[6:]
    outs, refs = refs[:parts], refs[parts:]
    grads, k_t, delta, probs, dq_t, dk, dv, low = refs[:8]
    qkv, out_t, cosine, sine, in_sems, prob_sems, load_sems = refs[8:]
    me = info_ref[0]
    rows = pieces[0].shape[0]
    length, part = dk.shape
    tiles = length // TILE
    steps = [(head, tile) for head in range(heads) for tile in range(tiles)]

    def fetch(index):
        head, tile = steps[index]
        limit = (tile + 1) * TILE
        return pltpu.make_async_copy(
            prob_ref.at[head, tile, pl.ds(0, limit)],
            probs.at[index % 3, pl.ds(0, limit)],
            prob_sems.at[index % 3],
        )

    loads = begin(list(zip(sources, (qkv, out_t, cosine, sine))), load_sems)
    arrivals = copy_in(pieces, row_place(grads, rows), in_sems, me, parts)
    fetch(0).start()
    fetch(1).start()
    loads[0].wait()
    k_t[...] = qkv[:, part : 2 * part].astype(F32).T.astype(BF16)
    dk[...] = jnp.zeros_like(dk)
    dv[...] = jnp.zeros_like(dv)
    for copy in arrivals:
        copy.wait()
    turned_grads = grads[...].astype(F32).T
    turned_grads = jnp.concatenate(
        [turned_grads[h * 64 : (h + 1) * 64, :] * inverse[h : h + 1, :] for h in range(heads)]
    )
    grads[...] = turned_grads.T.astype(BF16)
    loads[1].wait()
    product = turned_grads * out_t[...]
    for head in range(heads):
        delta[head : head + 1, :] = jnp.sum(
            product[head * 64 : (head + 1) * 64, :], axis=0, keepdims=True
        )
    for index, (head, tile) in enumerate(steps):
        slot = index % 3
        if index + 2 < len(steps):
            fetch(index + 2).start()
        fetch(index).wait()
        columns = slice(tile * TILE, (tile + 1) * TILE)
        limit = (tile + 1) * TILE
        height = slice(head * 64, (head + 1) * 64)
        query = head_mask(qkv[columns, :part], head, heads)
        grad = head_mask(grads[columns, :], head, heads)
        shift = delta[head : head + 1, columns]
        prob = probs[slot, :limit, :]
        grad_prob = mm(qkv[:limit, 2 * part :], grad, NT)
        grad_score = (prob.astype(F32) * (grad_prob - shift)).astype(BF16)
        dv[:limit, :] += mm(prob, grad)
        dk[:limit, :] += mm(grad_score, query)
        dq = mm(k_t[height, :limit], grad_score)
        dq_t[height, columns] = dq
    end(loads[2:])
    head_scale = 1.0 / math.sqrt(64)
    turned = dq_t[...].T * head_scale
    for kind, values in enumerate((turned, dk[...], dv[...])):
        if kind < 2:
            values = values * cosine[:, :part] - partner(values) * sine[:, :part]
        low[:, kind * part : (kind + 1) * part] = values.astype(BF16)
    part_of = row_place(low, rows)
    end(begin([(part_of(dest(me, k, parts)), out) for k, out in enumerate(outs)], in_sems))


def attend_back(info, pieces, qkv, out_t, inverse, probs, cosine, sine, parts, heads):
    rows, part = pieces[0].shape
    length = rows * parts
    return pl.pallas_call(
        lambda *refs: attend_back_kernel(parts, heads, *refs),
        out_shape=[shape((rows, 3 * part), BF16) for unused in range(parts)],
        in_specs=[SMEM] + [HBM] * parts + [VMEM] + [HBM] * 5,
        out_specs=[HBM] * parts,
        scratch_shapes=[
            pltpu.VMEM((length, part), BF16),
            pltpu.VMEM((part, length), BF16),
            pltpu.VMEM((8, length), F32),
            pltpu.VMEM((3, length, TILE), BF16),
            pltpu.VMEM((part, length), F32),
            pltpu.VMEM((length, part), F32),
            pltpu.VMEM((length, part), F32),
            pltpu.VMEM((length, 3 * part), BF16),
            pltpu.VMEM(qkv.shape, BF16),
            pltpu.VMEM(out_t.shape, F32),
            pltpu.VMEM(cosine.shape, F32),
            pltpu.VMEM(sine.shape, F32),
            pltpu.SemaphoreType.DMA((parts,)),
            pltpu.SemaphoreType.DMA((3,)),
            pltpu.SemaphoreType.DMA((4,)),
        ],
        compiler_params=params(60),
        cost_estimate=cost(heads * length * length * 512, heads * length * length, 0, WEIGHT),
        name="attend_back",
    )(info, *pieces, inverse, probs, qkv, out_t, cosine, sine)


def pre(info, own, left, right, counts, gain, weight, cosine, sine, parts):
    rows, width = own.shape
    part = width // parts
    return pl.pallas_call(
        lambda *refs: pre_kernel(parts, *refs),
        out_shape=[shape((rows, width), F32), shape((rows, width), BF16)]
        + [shape((rows, 3 * part), BF16) for unused in range(parts)],
        in_specs=[SMEM] + [HBM] * 4 + [VMEM] * 4,
        out_specs=[HBM] * (2 + parts),
        scratch_shapes=[
            pltpu.VMEM((3, rows, width), BF16),
            pltpu.VMEM(weight.shape, BF16),
            pltpu.VMEM((rows, width), F32),
            pltpu.VMEM((rows, width), BF16),
            pltpu.VMEM((parts, rows, 3 * part), BF16),
            pltpu.SemaphoreType.DMA((4,)),
            pltpu.SemaphoreType.DMA((max(2, parts),)),
        ],
        compiler_params=params(60),
        cost_estimate=cost(6 * rows * width * width, 8 * rows * width + 6 * width * width),
        name="pre",
    )(info, own, left, right, weight, counts, gain, cosine, sine)


def ffn_kernel(parts, info_ref, *refs):
    pieces, refs = refs[:parts], refs[parts:]
    pooled_ref, out_ref, gain, up, bias, down, *cots = refs[:9]
    refs = refs[9:]
    result_ref, grad_hidden_ref, bias_grad, gain_grad, sent, kept = refs[:6]
    outs, refs = refs[6 : 6 + parts], refs[6 + parts :]
    attended_ref, normed_ref, ffn_ref, hidden_ref, forward, arrived, back, send = refs[:8]
    products, windows, pooled, out_weight, sems, product_sems, load_sems = refs[8:]
    me, bit = info_ref[0], info_ref[1]
    step = pl.program_id(0)
    steps = pl.num_programs(0)
    rows, width = pooled_ref.shape
    part = width // parts
    high = width // 2
    halves = sent.shape[0] // high

    def product_copy(index, target):
        place = pl.multiple_of(lax.rem(index, halves) * high, high)
        return pltpu.make_async_copy(
            products.at[index], target.at[pl.ds(place, high)], product_sems.at[index]
        )

    def give(index, value):
        products[index] = value.astype(BF16)

        @pl.when(index // halves == bit)
        def to_kept():
            product_copy(index, kept).start()

        @pl.when(index // halves != bit)
        def to_sent():
            product_copy(index, sent).start()

    @pl.when(step == 0)
    def first():
        copies = copy_in(pieces, lambda index: arrived.at[index], sems, me, parts)
        moves = [(out_ref, out_weight), (pooled_ref, pooled)]
        loads = begin(moves + [(cot, windows.at[k]) for k, cot in enumerate(cots)], load_sems)
        back[...] = jnp.zeros_like(back)
        end(copies + loads[:1])
        for index in range(parts):
            attended_ref[:, index * part : (index + 1) * part] = arrived[index]
        branch_in = mm(attended_ref[...], out_weight[...])
        end(loads[1:])
        ffn_ref[...] = sum(windows[k].astype(F32) for k in range(3)).astype(BF16)
        hidden = pooled[...] + branch_in
        hidden_ref[...] = hidden
        forward[...] = hidden
        xhat, unused = norm_parts(hidden)
        normed_ref[...] = (xhat * gain[...]).astype(BF16)

    gate_in = mm(normed_ref[...], up[...]) + bias[...]
    grad_active = mm(ffn_ref[...], down[...], NT)
    bell = 0.5 * (1.0 + lax.erf(gate_in * (1.0 / math.sqrt(2.0))))
    active = (gate_in * bell).astype(BF16)
    forward[...] += mm(active, down[...])
    slope = bell + gate_in * jnp.exp(-0.5 * gate_in * gate_in) * (1.0 / math.sqrt(2.0 * math.pi))
    grad_gate = (grad_active * slope).astype(BF16)
    bias_grad[...] = jnp.sum(grad_gate.astype(F32), axis=0, keepdims=True)
    back[...] += mm(grad_gate, up[...], NT)
    for half in range(2):
        side = slice(half * high, (half + 1) * high)
        give(2 * step + half, mm(active[:, side], ffn_ref[...], TN))
        give(2 * (steps + step) + half, mm(normed_ref[:, side], grad_gate, TN))

    @pl.when(step == pl.num_programs(0) - 1)
    def last():
        result_ref[...] = forward[...].astype(BF16)
        xhat, scale = norm_parts(hidden_ref[...])
        grad, gain_sum = norm_back(back[...], xhat, scale, gain[...])
        gain_grad[...] = gain_sum
        grad_hidden = ffn_ref[...].astype(F32) + grad
        grad_hidden_ref[...] = grad_hidden
        branch = grad_hidden.astype(BF16)
        for half in range(2):
            side = slice(half * high, (half + 1) * high)
            give(4 * steps + half, mm(attended_ref[:, side], branch, TN))
        attended_grad = mm(branch, out_weight[...], NT).astype(BF16)
        for index in range(parts):
            send[index] = attended_grad[:, index * part : (index + 1) * part]
        moves = [(send.at[dest(me, k, parts)], out) for k, out in enumerate(outs)]
        copies = begin(moves, sems)
        for index in range(2 * halves):
            product_copy(index, kept).wait()
        end(copies)


def ffn(info, pieces, pooled, out_weight, gain, up, bias, down, cots, parts):
    rows, width = pooled.shape
    units = up.shape[1]
    part = width // parts
    chunk = 512
    whole = lambda *dims: pl.BlockSpec(dims, lambda step: (0,) * len(dims))
    line = pl.BlockSpec((1, chunk), lambda step: (0, step))
    square = whole(rows, width)
    return pl.pallas_call(
        lambda *refs: ffn_kernel(parts, *refs),
        grid=(units // chunk,),
        out_shape=[
            shape((rows, width), BF16),
            shape((rows, width), F32),
            shape((1, units), F32),
            shape((1, width), F32),
            shape((units + width // 2, width), BF16),
            shape((units + width // 2, width), BF16),
        ]
        + [shape((rows, part), BF16) for unused in range(parts)],
        in_specs=[SMEM]
        + [HBM] * parts
        + [
            HBM,
            HBM,
            whole(1, width),
            pl.BlockSpec((width, chunk), lambda step: (0, step)),
            line,
            pl.BlockSpec((chunk, width), lambda step: (step, 0)),
            HBM,
            HBM,
            HBM,
        ],
        out_specs=[square, square, line, whole(1, width), HBM, HBM] + [HBM] * parts,
        scratch_shapes=[
            pltpu.VMEM((rows, width), BF16),
            pltpu.VMEM((rows, width), BF16),
            pltpu.VMEM((rows, width), BF16),
            pltpu.VMEM((rows, width), F32),
            pltpu.VMEM((rows, width), F32),
            pltpu.VMEM((parts, rows, part), BF16),
            pltpu.VMEM((rows, width), F32),
            pltpu.VMEM((parts, rows, part), BF16),
            pltpu.VMEM((4 * units // width + 2, width // 2, width), BF16),
            pltpu.VMEM((3, rows, width), BF16),
            pltpu.VMEM((rows, width), F32),
            pltpu.VMEM((width, width), BF16),
            pltpu.SemaphoreType.DMA((parts,)),
            pltpu.SemaphoreType.DMA((4 * units // width + 2,)),
            pltpu.SemaphoreType.DMA((5,)),
        ],
        compiler_params=params(60),
        cost_estimate=cost(
            12 * rows * width * units + 4 * rows * width * width, 12 * width * units, 2 * rows * units, WEIGHT
        ),
        name="ffn",
    )(info, *pieces, pooled, out_weight, gain, up, bias, down, *cots)


def post_kernel(parts, info_ref, *refs):
    pieces, refs = refs[:parts], refs[parts:]
    sources, (counts, gain, bias, ffn_gain) = refs[:4], refs[4:8]
    share_ref, sent_ref, kept_ref, arrived, low, share, products, small = refs[8:16]
    pooled, weight, normed, grad_hidden, sems, load_sems, out_sems = refs[16:]
    me, bit = info_ref[0], info_ref[1]
    rows, width = pooled.shape
    part = width // parts
    half = width // 2
    copies = copy_in(pieces, lambda index: arrived.at[index], sems, me, parts)
    loads = begin(list(zip(sources, (pooled, weight, normed, grad_hidden))), load_sems)
    loads[0].wait()
    xhat, scale = norm_parts(pooled[...])
    end(copies)
    for index in range(parts):
        for kind in range(3):
            place = kind * width + index * part
            low[:, place : place + part] = arrived[index, :, kind * part : (kind + 1) * part]
    loads[1].wait()
    grad, gain_sum = norm_back(mm(low[...], weight[...], NT), xhat, scale, gain[...])
    small[...] = jnp.zeros_like(small)
    lines = bias.shape[1] // width
    for line in range(lines):
        small[line : line + 1, :] = bias[:, line * width : (line + 1) * width]
    small[lines : lines + 1, :] = ffn_gain[...]
    small[lines + 1 : lines + 2, :] = gain_sum
    loads[2].wait()
    stores = []
    for index, out in enumerate((sent_ref, kept_ref)):
        first = pl.multiple_of((1 - bit if index == 0 else bit) * half, 128)
        value = mm(normed[:, pl.ds(first, half)], low[...], TN)
        products[index, :, : 3 * width] = value.astype(BF16)
        products[index, :, 3 * width :] = small[:, pl.ds(first, half)].T.astype(BF16)
        stores += begin([(products.at[index], out)], out_sems.at[pl.ds(index, 1)])
    loads[3].wait()
    share[...] = ((grad_hidden[...] + grad) / counts[...]).astype(BF16)
    end(stores + begin([(share, share_ref)], out_sems.at[pl.ds(2, 1)]))


def post(info, pieces, pooled, weight, normed, grad_hidden, counts, gain, bias, ffn_gain, parts):
    rows, width = pooled.shape
    part = width // parts
    half = shape((width // 2, 3 * width + 128), BF16)
    return pl.pallas_call(
        lambda *refs: post_kernel(parts, *refs),
        out_shape=[shape((rows, width), BF16), half, half],
        in_specs=[SMEM] + [HBM] * (parts + 4) + [VMEM] * 4,
        out_specs=[HBM] * 3,
        scratch_shapes=[
            pltpu.VMEM((parts, rows, 3 * part), BF16),
            pltpu.VMEM((rows, 3 * width), BF16),
            pltpu.VMEM((rows, width), BF16),
            pltpu.VMEM((2,) + half.shape, BF16),
            pltpu.VMEM((128, width), F32),
            pltpu.VMEM((rows, width), F32),
            pltpu.VMEM(weight.shape, BF16),
            pltpu.VMEM((rows, width), BF16),
            pltpu.VMEM((rows, width), F32),
            pltpu.SemaphoreType.DMA((parts,)),
            pltpu.SemaphoreType.DMA((4,)),
            pltpu.SemaphoreType.DMA((3,)),
        ],
        compiler_params=params(60),
        cost_estimate=cost(12 * rows * width * width, 8 * rows * width + 6 * width * width, 0, WEIGHT),
        name="post",
    )(info, *pieces, pooled, weight, normed, grad_hidden, counts, gain, bias, ffn_gain)


def ffn_result_kernel(bit_ref, own, other, down, up, out, whole, wide, in_sems, out_sems):
    half, width = own.shape
    units = down.shape[0]
    high = width // 2
    blocks = 2 * half // high
    bit = bit_ref[0]

    def arrival(index, source):
        place = index * high % half
        return pltpu.make_async_copy(
            source.at[pl.ds(place, high)], whole.at[index], in_sems.at[index]
        )

    for index in range(blocks):
        mine = index * high // half == bit

        @pl.when(mine)
        def from_own():
            arrival(index, own).start()

        @pl.when(jnp.logical_not(mine))
        def from_other():
            arrival(index, other).start()

    copies = []
    for index in range(blocks):
        arrival(index, own).wait()
        wide[index] = whole[index].astype(F32)
        first = index * high
        if first < units:
            target = down.at[pl.ds(first, high)]
        elif first < 2 * units:
            column = (first - units) // width * width
            target = up.at[pl.ds(first % width, high), pl.ds(column, width)]
        else:
            target = out.at[pl.ds(first - 2 * units, high)]
        copies.append(pltpu.make_async_copy(wide.at[index], target, out_sems.at[index]))
        copies[-1].start()
    end(copies)


def ffn_result(bit, own, other, units):
    half, width = own.shape
    high = width // 2
    blocks = 2 * half // high
    return pl.pallas_call(
        ffn_result_kernel,
        out_shape=[shape((units, width), F32), shape((width, units), F32), shape((width, width), F32)],
        in_specs=[SMEM, HBM, HBM],
        out_specs=[HBM] * 3,
        scratch_shapes=[
            pltpu.VMEM((blocks, high, width), BF16),
            pltpu.VMEM((blocks, high, width), F32),
            pltpu.SemaphoreType.DMA((blocks,)),
            pltpu.SemaphoreType.DMA((blocks,)),
        ],
        compiler_params=params(60),
        cost_estimate=cost(0, 12 * half * width),
        name="ffn_result",
    )(bit, own, other)


def qkv_result_kernel(count, order_ref, *refs):
    pieces, (out, bias, ffn_gain, attn_gain, whole, sems) = refs[: 2 * count], refs[2 * count :]
    size = pieces[0].shape[0]
    copies = []
    for index, piece in enumerate(pieces):
        side = order_ref[count] if index < count else 1 - order_ref[count]
        place = pl.multiple_of((side * count + order_ref[index % count]) * size, 16)
        copies.append(
            pltpu.make_async_copy(piece, whole.at[pl.ds(place, size)], sems.at[index])
        )
        copies[-1].start()
    end(copies)
    wide = out.shape[1]
    out[...] = whole[:, :wide].astype(F32)
    lines = whole[:, wide:].astype(F32).T
    count = bias.shape[0]
    for line in range(count):
        bias[line, :, :] = lines[line : line + 1, :]
    ffn_gain[...] = lines[count : count + 1, :]
    attn_gain[...] = lines[count + 1 : count + 2, :]


def qkv_result(order, pieces, lines):
    size, wide = pieces[0].shape
    count = len(pieces) // 2
    rows = 2 * count * size
    return pl.pallas_call(
        lambda *refs: qkv_result_kernel(count, *refs),
        out_shape=[
            shape((rows, wide - 128), F32),
            shape((lines, 1, rows), F32),
            shape((1, rows), F32),
            shape((1, rows), F32),
        ],
        in_specs=[SMEM] + [HBM] * (2 * count),
        out_specs=[VMEM] * 4,
        scratch_shapes=[
            pltpu.VMEM((rows, wide), BF16),
            pltpu.SemaphoreType.DMA((2 * count,)),
        ],
        compiler_params=params(60),
        cost_estimate=cost(0, 6 * rows * wide, 0, 4 * WEIGHT),
        name="qkv_result",
    )(order, *pieces)


def join_kernel(order_ref, *refs):
    pieces, out = refs[:-1], refs[-1]
    size = pieces[0].shape[0]
    for index, piece in enumerate(pieces):
        out[pl.ds(pl.multiple_of(order_ref[index] * size, size), size), :] = piece[...]


def join(pieces, order):
    size, width = pieces[0].shape
    count = len(pieces)
    if size % 16:
        whole = jnp.zeros((count * size, width), BF16)
        for index, piece in enumerate(pieces):
            whole = lax.dynamic_update_slice_in_dim(whole, piece, order[index] * size, 0)
        return whole
    return pl.pallas_call(
        join_kernel,
        out_shape=shape((count * size, width), BF16),
        in_specs=[SMEM] + [VMEM] * count,
        out_specs=VMEM,
        compiler_params=params(60),
        cost_estimate=cost(0, 4 * count * size * width),
        name="join",
    )(order, *pieces)


def pairwise(values, odd, parts):
    firsts = range(1 if odd else 0, parts - 1, 2)
    pairs = [(i, i + 1) for i in firsts] + [(i + 1, i) for i in firsts]
    return lax.ppermute(values, "seq", pairs)


def rotated(values, shift, parts):
    return lax.ppermute(values, "seq", [(i, (i + shift) % parts) for i in range(parts)])


def swap(values):
    return lax.ppermute(values, "core", [(0, 1), (1, 0)])


def turned(values, axis):
    return lax.all_to_all(values, axis, 0, 0)


def add_low(first, second):
    return (first.astype(F32) + second.astype(F32)).astype(BF16)


def total_of(values):
    return jnp.sum(values.astype(F32), axis=0).astype(BF16)


def sum_plane_out(half, chips):
    rows, width = half.shape
    return turned(half.reshape(chips, rows // chips, width), "chip")


def sum_plane_back(own, chips):
    chunks = turned(jnp.broadcast_to(own, (chips,) + own.shape), "chip")
    return chunks.reshape(chips * own.shape[0], own.shape[1])


class SeqSum:
    def __init__(self, pieces, me, parts):
        self.values, self.me, self.parts = pieces, me, parts
        self.bits = parts.bit_length() - 1
        self.ways = [(bit, 0) for bit in range(self.bits - 1)] + [(self.bits - 1, 1)]
        self.ways += [(bit, 2) for bit in reversed(range(self.bits - 1))]

    def exchange(self, values, bit):
        return lax.ppermute(values, "seq", [(i, i ^ (1 << bit)) for i in range(self.parts)])

    def start(self, way):
        bit, kind = self.ways[way]
        if kind == 0:
            half = self.values.shape[1] // 2
            mine = (self.me >> bit) & 1
            piece = lambda side: total_of(
                lax.dynamic_slice_in_dim(self.values, side * half, half, 1)
            )
            self.kept, self.sent = piece(mine), piece(1 - mine)
            return self.exchange(self.sent, bit)
        if kind == 1:
            self.kept = total_of(self.values)
        else:
            self.kept = self.values
        self.sent = self.kept
        return self.exchange(self.sent, bit)

    def finish(self, way, got):
        bit, kind = self.ways[way]
        if kind < 2:
            self.values = add_low(self.kept, got)
            if kind == 0 or way + 1 == len(self.ways):
                self.values = self.values[None] if kind == 0 else self.values
            return
        first = ((self.me >> bit) & 1) == 0
        low, high = jnp.where(first, self.kept, got), jnp.where(first, got, self.kept)
        self.values = jnp.concatenate([low, high], axis=0)


def near_pieces(own, chips):
    pairs = lambda k: [(i, i ^ k) for i in range(chips)]
    return [lax.ppermute(own, "chip", pairs(k)) if k else own for k in range(chips)]


def after(values, *earlier):
    return lax.optimization_barrier((values,) + earlier)[0]


def tie(*groups):
    return lax.optimization_barrier(groups)


def body(
    byte_input_rows,
    segment_ids,
    attn_gain,
    qkv_weight,
    out_weight,
    ffn_gain,
    up_weight,
    up_bias,
    down_weight,
    cotangent,
):
    rows_in, cot = byte_input_rows[0], cotangent[0]
    ids = segment_ids
    block, width = rows_in.shape
    parts, chips = lax.axis_size("seq"), lax.axis_size("chip")
    me, core = lax.axis_index("seq"), lax.axis_index("core")
    own_rows = SEG_DEV
    length = own_rows * parts
    heads = HEADS // parts
    reach = reach_of(parts, own_rows, block)
    place = jnp.stack([me, core]).astype(jnp.int32)
    base = ((me - reach) * own_rows).astype(jnp.int32)[None]
    side = (1 - 2 * (me & 1)).astype(jnp.int32)[None]
    firsts = ids

    def both_ways(carried):
        return [pairwise(carried[0], False, parts), pairwise(carried[1], True, parts)]

    def to_owners(windows, hold=lambda carried: carried):
        carried = [windows[2 * reach], windows[0]]
        for away in range(reach - 1, -1, -1):
            carried = both_ways(carried)
            if away:
                carried = [
                    add_low(carried[1], windows[reach + away]),
                    add_low(carried[0], windows[reach - away]),
                ]
                carried = hold(carried)
        return [windows[reach]] + carried

    def exchange(messages):
        return [messages[0]] + [
            rotated(message, shift, parts) for shift, message in enumerate(messages) if shift
        ]

    half = 32
    lane = jnp.arange(128, dtype=jnp.int32)
    frequency = jnp.exp((lane % half).astype(F32) * (-math.log(10000.0) / half))
    angles = jnp.arange(length, dtype=jnp.int32).astype(F32)[:, None] * frequency[None, :]
    cosine = jnp.cos(angles)
    sine = jnp.sin(angles) * jnp.where(lane % 64 < half, -1.0, 1.0)
    own_cosine = lax.dynamic_slice_in_dim(cosine, me * own_rows, own_rows, 0)
    own_sine = lax.dynamic_slice_in_dim(sine, me * own_rows, own_rows, 0)

    windows = pool(base, side, firsts, ids, rows_in, own_rows, 2 * reach + 1)
    cot_windows = pool(base, side, firsts, ids, after(cot, windows), own_rows, 2 * reach + 1)

    def behind_first(carried):
        nonlocal cot_windows
        carried, cot_windows = tie(carried, cot_windows)
        return carried

    sums_in = to_owners(windows, behind_first)
    ids_late = after(ids, windows)
    ids_all = turned(jnp.broadcast_to(ids_late, (parts,) + ids.shape), "seq")
    positions = me * own_rows + jnp.arange(own_rows, dtype=jnp.int32)
    same = ids_all.reshape(1, -1) == positions[:, None]
    counts = jnp.sum(same.astype(F32), axis=1, keepdims=True)
    ids_column = ids.reshape(block, 1)

    gain_row = attn_gain[None, :]
    pooled, normed_attn, *qkv_out = pre(
        place, *sums_in, counts, gain_row, qkv_weight, own_cosine, own_sine, parts
    )
    qkv_in = exchange(qkv_out)
    cots_in = to_owners(cot_windows, lambda carried: after(carried, qkv_in))
    *attended_out, qkv, out_t, inverse, probs = attend(place, qkv_in, parts, heads)
    attended_in = exchange(attended_out)
    (
        pooled_out,
        grad_hidden,
        grad_bias,
        grad_ffn_gain,
        sent,
        kept,
        *grads_out,
    ) = ffn(
        place,
        attended_in,
        pooled,
        out_weight,
        ffn_gain[None, :],
        up_weight,
        up_bias[None, :],
        down_weight,
        cots_in,
        parts,
    )
    bit = core.astype(jnp.int32)[None]

    grads_in = exchange(grads_out)
    half = add_low(kept, swap(sent))
    grads_in = after(grads_in, half)
    pieces = sum_plane_out(half, chips)
    pooled_hop = both_ways(after([pooled_out, pooled_out], grads_in))
    pooled_in = [pooled_out] + pooled_hop
    low_out = attend_back(
        place, grads_in, qkv, out_t, inverse, probs, cosine, sine, parts, heads
    )
    low_out, pooled_hop = tie(low_out, pooled_hop)
    low_in = exchange(low_out)
    low_in, pieces = tie(low_in, pieces)
    ffn_sum = SeqSum(pieces, me, parts)
    ways = len(ffn_sum.ways)
    got = ffn_sum.start(0)
    low_in = after(low_in, ffn_sum.sent)
    share, qkv_sent, qkv_kept = post(
        place,
        low_in,
        pooled,
        qkv_weight,
        normed_attn,
        grad_hidden,
        counts,
        gain_row,
        grad_bias,
        grad_ffn_gain,
        parts,
    )

    share_hop = both_ways([share, share])
    share_in = [share] + share_hop
    ffn_sum.finish(0, after(got, qkv_sent))
    pieces = sum_plane_out(add_low(qkv_kept, swap(qkv_sent)), chips)
    qkv_sum = SeqSum(pieces, me, parts)
    if ways > 1:
        ffn_sum.finish(1, after(ffn_sum.start(1), pieces))
    pooled_hop = after(pooled_hop, share)
    for unused in range(1, reach):
        pooled_hop = both_ways(pooled_hop[::-1])
        pooled_in += pooled_hop
    for way in range(ways):
        qkv_sum.finish(way, qkv_sum.start(way))
        if way == 0:
            qkv_sum.values, share_hop, pooled_in = tie(qkv_sum.values, share_hop, pooled_in)
        if way + 2 < ways:
            ffn_sum.finish(way + 2, after(ffn_sum.start(way + 2), qkv_sum.values))
    ffn_own = sum_plane_back(ffn_sum.values, chips)
    share_hop = after(share_hop, qkv_sum.values)
    for unused in range(1, reach):
        share_hop = both_ways(share_hop[::-1])
        share_in += share_hop
    near = near_pieces(qkv_sum.values, chips)
    grad_input = select(base, side, firsts, ids_column, cot, share_in)
    layer_out = select(base, side, firsts, ids_column, rows_in, pooled_in)
    near = after(near, grad_input, layer_out)
    near_order = jnp.stack([lax.axis_index("chip") ^ k for k in range(chips)] + [core])
    units = up_weight.shape[1]
    ffn_own = after(ffn_own, near)
    grad_down, grad_up, grad_out = ffn_result(bit, ffn_own, swap(ffn_own), units)
    grad_qkv, grad_bias, grad_ffn_gain, grad_attn_gain = qkv_result(
        near_order.astype(jnp.int32), near + [swap(p) for p in near], units // width
    )
    return (
        layer_out[None],
        grad_input[None],
        grad_attn_gain[0],
        grad_qkv,
        grad_out,
        grad_ffn_gain[0],
        grad_up,
        grad_bias.reshape(units),
        grad_down,
    )


def solution(mesh):
    dp, seq = mesh.shape["dp"], mesh.shape["seq"]
    inner = jax.sharding.Mesh(mesh.devices.reshape(dp // 2, 2, seq), ("chip", "core", "seq"))
    rows, ids = P(("chip", "core"), "seq", None), P(("chip", "core"), "seq")
    placed = (rows, ids, P(), P(), P(), P(), P(), P(), P(), rows)
    return jax.shard_map(
        body,
        mesh=inner,
        in_specs=placed,
        out_specs=(rows, rows, P(), P(), P(), P(), P(), P(), P()),
        check_vma=False,
    )
```

```python
import math

import jax
import jax.numpy as jnp
import numpy as np
from jax import lax
from jax.experimental import pallas as pl
from jax.experimental.pallas import tpu as pltpu
from jax.sharding import PartitionSpec as P

HEADS = 8
SEG_DEV = 448
TILE = 256
BAND = TILE + 16
WEIGHT = 20
NEG = -1e30
NN = (((1,), (0,)), ((), ()))
NT = (((1,), (1,)), ((), ()))
TN = (((0,), (0,)), ((), ()))
F32 = jnp.float32
BF16 = jnp.bfloat16

SMEM = pl.BlockSpec(memory_space=pltpu.SMEM)
VMEM = pl.BlockSpec(memory_space=pltpu.VMEM)
HBM = pl.BlockSpec(memory_space=pltpu.HBM)


def mm(left, right, dims=NN):
    return lax.dot_general(left, right, dims, preferred_element_type=F32)


def shape(dims, kind):
    return jax.ShapeDtypeStruct(dims, kind)


def cost(flops, moved, exps=0, weight=1):
    return pl.CostEstimate(
        flops=int(weight * flops), bytes_accessed=int(weight * moved), transcendentals=int(weight * exps)
    )


def params(mebibytes):
    return pltpu.CompilerParams(vmem_limit_bytes=int(mebibytes * 1024 * 1024))


def begin(moves, sems):
    copies = [pltpu.make_async_copy(*move, sems.at[index]) for index, move in enumerate(moves)]
    for copy in copies:
        copy.start()
    return copies


def end(copies):
    for copy in copies:
        copy.wait()


def reach_of(parts, rows, block):
    total = rows * parts
    reach = 0
    for d in range(parts):
        low = max(0, total - (parts - d) * block)
        high = min(total, (d + 1) * block) - 1
        reach = max(reach, d - low // rows, high // rows - d)
    return reach


def band_start(first_ref, base_ref, tile):
    return pl.multiple_of((first_ref[0, tile * TILE] - base_ref[0]) // 16 * 16, 16)


def pool_kernel(base_ref, side_ref, first_ref, ids_ref, rows_ref, *refs):
    outs, total = refs[:-1], refs[-1]
    size = outs[0].shape[0]
    total[...] = jnp.zeros_like(total)
    place = lax.broadcasted_iota(jnp.int32, (BAND, TILE), 0)
    for tile in range(rows_ref.shape[0] // TILE):
        span = slice(tile * TILE, (tile + 1) * TILE)
        start = band_start(first_ref, base_ref, tile)
        local = ids_ref[:, span] - (base_ref[0] + start)
        hot = jnp.where(place == local, 1.0, 0.0).astype(BF16)
        total[pl.ds(start, BAND), :] += mm(hot, rows_ref[span, :])
    reach = len(outs) // 2
    for index, out in enumerate(outs):
        place = pl.multiple_of((reach + (index - reach) * side_ref[0]) * size, 16)
        out[...] = total[pl.ds(place, size), :].astype(BF16)


def pool(base, side, firsts, ids, rows, own_rows, count):
    block, width = rows.shape
    return pl.pallas_call(
        pool_kernel,
        out_shape=[shape((own_rows, width), BF16)] * count,
        in_specs=[SMEM, SMEM, SMEM, VMEM, VMEM],
        out_specs=[VMEM] * count,
        scratch_shapes=[pltpu.VMEM((count * own_rows + BAND, width), F32)],
        compiler_params=params(60),
        cost_estimate=cost(2 * BAND * block * width, 2 * block * width + 2 * count * own_rows * width),
        name="pool",
    )(base, side, firsts, ids, rows)


def select_kernel(base_ref, side_ref, first_ref, ids_ref, rows_ref, *refs):
    pieces, (out, table, sems) = refs[:-3], refs[-3:]
    size = pieces[0].shape[0]
    reach = len(pieces) // 2
    copies = []
    for index, piece in enumerate(pieces):
        away = (index + 1) // 2 * (1 if index % 2 else -1)
        place = pl.multiple_of((reach + away * side_ref[0]) * size, 16)
        copies.append(
            pltpu.make_async_copy(piece, table.at[pl.ds(place, size)], sems.at[index])
        )
    for copy in copies:
        copy.start()
    table[len(pieces) * size :, :] = jnp.zeros((BAND, table.shape[1]), BF16)
    for copy in copies:
        copy.wait()
    place = lax.broadcasted_iota(jnp.int32, (TILE, BAND), 1)
    for tile in range(rows_ref.shape[0] // TILE):
        span = slice(tile * TILE, (tile + 1) * TILE)
        start = band_start(first_ref, base_ref, tile)
        local = ids_ref[span, :] - (base_ref[0] + start)
        hot = jnp.where(place == local, 1.0, 0.0).astype(BF16)
        chosen = mm(hot, table[pl.ds(start, BAND), :])
        out[span, :] = (rows_ref[span, :].astype(F32) + chosen).astype(BF16)


def select(base, side, firsts, ids_column, rows, pieces, weight=1):
    block, width = rows.shape
    total = sum(piece.shape[0] for piece in pieces)
    return pl.pallas_call(
        select_kernel,
        out_shape=shape((block, width), BF16),
        in_specs=[SMEM, SMEM, SMEM, VMEM, VMEM] + [HBM] * len(pieces),
        out_specs=VMEM,
        scratch_shapes=[
            pltpu.VMEM((total + BAND, width), BF16),
            pltpu.SemaphoreType.DMA((len(pieces),)),
        ],
        compiler_params=params(60),
        cost_estimate=cost(
            2 * BAND * block * width, 4 * block * width + 2 * total * width, 0, weight
        ),
        name="select",
    )(base, side, firsts, ids_column, rows, *pieces)


def norm_parts(values):
    center = jnp.mean(values, axis=-1, keepdims=True)
    centered = values - center
    variance = jnp.mean(centered * centered, axis=-1, keepdims=True)
    scale = lax.rsqrt(variance + 1e-05)
    return centered * scale, scale


def norm_back(grad, xhat, scale, gain):
    e = grad * gain
    mean_e = jnp.mean(e, axis=-1, keepdims=True)
    mean_ex = jnp.mean(e * xhat, axis=-1, keepdims=True)
    return scale * (e - mean_e - xhat * mean_ex), jnp.sum(grad * xhat, axis=0, keepdims=True)


def partner(values):
    lanes = values.shape[1]
    lane = lax.broadcasted_iota(jnp.int32, values.shape, 1)
    return jnp.where(
        lax.rem(lane, 64) < 32, pltpu.roll(values, lanes - 32, 1), pltpu.roll(values, 32, 1)
    )


def dest(me, shift, parts):
    return lax.rem(me + shift, parts)


def source(me, shift, parts):
    return lax.rem(me + parts - shift, parts)


def pre_kernel(parts, info_ref, own, left, right, weight_ref, *refs):
    counts, gain, cosine, sine, pooled_ref, normed_ref = refs[:6]
    outs, refs = refs[6 : 6 + parts], refs[6 + parts :]
    sums, weight, pooled, normed, send, in_sems, out_sems = refs
    me = info_ref[0]
    loads = begin(
        [(own, sums.at[0]), (left, sums.at[1]), (right, sums.at[2]), (weight_ref, weight)], in_sems
    )
    end(loads[:3])
    total = sums[0].astype(F32) + sums[1].astype(F32) + sums[2].astype(F32)
    pooled[...] = total / counts[...]
    xhat, unused = norm_parts(pooled[...])
    normed[...] = (xhat * gain[...]).astype(BF16)
    stores = begin([(pooled, pooled_ref), (normed, normed_ref)], out_sems)
    loads[3].wait()
    width = pooled.shape[1]
    part = width // parts
    step = 256
    for kind in range(3):
        for first in range(0, width, step):
            column = kind * width + first
            wide = mm(normed[...], weight[:, column : column + step])
            for inner in range(0, step, 128):
                block = wide[:, inner : inner + 128]
                if kind < 2:
                    block = block * cosine[...] + partner(block) * sine[...]
                if kind == 0:
                    block = block * (1.0 / math.sqrt(width // HEADS))
                block = block.astype(BF16)
                for small in range(0, 128, min(part, 128)):
                    place = first + inner + small
                    offset = kind * part + place % part
                    send[place // part, :, offset : offset + min(part, 128)] = block[
                        :, small : small + min(part, 128)
                    ]
    end(stores)
    end(begin([(send.at[dest(me, k, parts)], out) for k, out in enumerate(outs)], out_sems))


def copy_in(pieces, place, sems, me, parts):
    copies = []
    for shift, piece in enumerate(pieces):
        copies.append(
            pltpu.make_async_copy(piece, place(source(me, shift, parts)), sems.at[shift])
        )
    for copy in copies:
        copy.start()
    return copies


def row_place(ref, rows):
    return lambda index: ref.at[pl.ds(pl.multiple_of(index * rows, 16), rows)]


def head_mask(tile, head, heads):
    if heads == 1:
        return tile
    lane = lax.broadcasted_iota(jnp.int32, tile.shape, 1)
    return jnp.where(lane // 64 == head, tile.astype(F32), 0.0).astype(BF16)


def attend_kernel(parts, heads, info_ref, *refs):
    pieces, refs = refs[:parts], refs[parts:]
    outs, refs = refs[:parts], refs[parts:]
    qkv_ref, out_ref, inverse_ref, prob_ref = refs[:4]
    qkv, out_t, v_t, scores, probs, attended, in_sems, prob_sems, out_sems = refs[4:]
    me = info_ref[0]
    rows, part = outs[0].shape
    tiles = qkv.shape[0] // TILE
    for copy in copy_in(pieces, row_place(qkv, rows), in_sems, me, parts):
        copy.wait()
    stores = begin([(qkv, qkv_ref)], out_sems)
    v_t[...] = qkv[:, 2 * part :].astype(F32).T.astype(BF16)
    key_index = lax.broadcasted_iota(jnp.int32, (TILE, TILE), 0)
    query_index = lax.broadcasted_iota(jnp.int32, (TILE, TILE), 1)
    started = []
    for head in range(heads):
        for tile in range(tiles):
            step = head * tiles + tile
            slot = step % 2
            columns = slice(tile * TILE, (tile + 1) * TILE)
            limit = (tile + 1) * TILE
            query = head_mask(qkv[columns, :part], head, heads)
            top = jnp.full((8, TILE), NEG, F32)
            for chunk in range(tile + 1):
                span = slice(chunk * TILE, (chunk + 1) * TILE)
                score = mm(qkv[span, part : 2 * part], query, NT)
                if chunk == tile:
                    score = jnp.where(key_index <= query_index, score, NEG)
                scores[slot, span, :] = score
                top = jnp.maximum(top, jnp.max(score.reshape(TILE // 8, 8, TILE), axis=0))
            top = jnp.max(top, axis=0, keepdims=True)
            if step >= 2:
                started[step - 2].wait()
            total = jnp.zeros((8, TILE), F32)
            for chunk in range(tile + 1):
                span = slice(chunk * TILE, (chunk + 1) * TILE)
                grown = jnp.exp(scores[slot, span, :] - top)
                probs[slot, span, :] = grown.astype(BF16)
                total = total + jnp.sum(grown.reshape(TILE // 8, 8, TILE), axis=0)
            inverse = 1.0 / jnp.sum(total, axis=0, keepdims=True)
            inverse_ref[head : head + 1, columns] = inverse
            copy = pltpu.make_async_copy(
                probs.at[slot, pl.ds(0, limit)],
                prob_ref.at[head, tile, pl.ds(0, limit)],
                prob_sems.at[slot],
            )
            copy.start()
            started.append(copy)
            height = slice(head * 64, (head + 1) * 64)
            out_t[height, columns] = mm(v_t[height, :limit], probs[slot, :limit, :]) * inverse
    copy = pltpu.make_async_copy(out_t, out_ref, out_sems.at[1])
    copy.start()
    attended[...] = out_t[...].T.astype(BF16)
    part_of = row_place(attended, rows)
    end(begin([(part_of(dest(me, k, parts)), out) for k, out in enumerate(outs)], in_sems))
    end(started[-2:] + stores + [copy])


def attend(info, pieces, parts, heads):
    rows, triple = pieces[0].shape
    part = triple // 3
    length = rows * parts
    tiles = length // TILE
    return pl.pallas_call(
        lambda *refs: attend_kernel(parts, heads, *refs),
        out_shape=[shape((rows, part), BF16) for unused in range(parts)]
        + [
            shape((length, triple), BF16),
            shape((part, length), F32),
            shape((8, length), F32),
            shape((heads, tiles, length, TILE), BF16),
        ],
        in_specs=[SMEM] + [HBM] * parts,
        out_specs=[HBM] * (parts + 2) + [VMEM, HBM],
        scratch_shapes=[
            pltpu.VMEM((length, triple), BF16),
            pltpu.VMEM((part, length), F32),
            pltpu.VMEM((part, length), BF16),
            pltpu.VMEM((2, length, TILE), F32),
            pltpu.VMEM((2, length, TILE), BF16),
            pltpu.VMEM((length, part), BF16),
            pltpu.SemaphoreType.DMA((parts,)),
            pltpu.SemaphoreType.DMA((2,)),
            pltpu.SemaphoreType.DMA((2,)),
        ],
        compiler_params=params(60),
        cost_estimate=cost(
            heads * length * length * 256,
            heads * length * length,
            heads * length * length // 2,
            WEIGHT,
        ),
        name="attend",
    )(info, *pieces)


def attend_back_kernel(parts, heads, info_ref, *refs):
    pieces, refs = refs[:parts], refs[parts:]
    inverse, prob_ref = refs[:2]
    sources, refs = refs[2:6], refs[6:]
    outs, refs = refs[:parts], refs[parts:]
    grads, k_t, delta, probs, dq_t, dk, dv, low = refs[:8]
    qkv, out_t, cosine, sine, in_sems, prob_sems, load_sems = refs[8:]
    me = info_ref[0]
    rows = pieces[0].shape[0]
    length, part = dk.shape
    tiles = length // TILE
    steps = [(head, tile) for head in range(heads) for tile in range(tiles)]

    def fetch(index):
        head, tile = steps[index]
        limit = (tile + 1) * TILE
        return pltpu.make_async_copy(
            prob_ref.at[head, tile, pl.ds(0, limit)],
            probs.at[index % 3, pl.ds(0, limit)],
            prob_sems.at[index % 3],
        )

    loads = begin(list(zip(sources, (qkv, out_t, cosine, sine))), load_sems)
    arrivals = copy_in(pieces, row_place(grads, rows), in_sems, me, parts)
    fetch(0).start()
    fetch(1).start()
    loads[0].wait()
    k_t[...] = qkv[:, part : 2 * part].astype(F32).T.astype(BF16)
    dk[...] = jnp.zeros_like(dk)
    dv[...] = jnp.zeros_like(dv)
    for copy in arrivals:
        copy.wait()
    turned_grads = grads[...].astype(F32).T
    turned_grads = jnp.concatenate(
        [turned_grads[h * 64 : (h + 1) * 64, :] * inverse[h : h + 1, :] for h in range(heads)]
    )
    grads[...] = turned_grads.T.astype(BF16)
    loads[1].wait()
    product = turned_grads * out_t[...]
    for head in range(heads):
        delta[head : head + 1, :] = jnp.sum(
            product[head * 64 : (head + 1) * 64, :], axis=0, keepdims=True
        )
    for index, (head, tile) in enumerate(steps):
        slot = index % 3
        if index + 2 < len(steps):
            fetch(index + 2).start()
        fetch(index).wait()
        columns = slice(tile * TILE, (tile + 1) * TILE)
        limit = (tile + 1) * TILE
        height = slice(head * 64, (head + 1) * 64)
        query = head_mask(qkv[columns, :part], head, heads)
        grad = head_mask(grads[columns, :], head, heads)
        shift = delta[head : head + 1, columns]
        prob = probs[slot, :limit, :]
        grad_prob = mm(qkv[:limit, 2 * part :], grad, NT)
        grad_score = (prob.astype(F32) * (grad_prob - shift)).astype(BF16)
        dv[:limit, :] += mm(prob, grad)
        dk[:limit, :] += mm(grad_score, query)
        dq = mm(k_t[height, :limit], grad_score)
        dq_t[height, columns] = dq
    end(loads[2:])
    head_scale = 1.0 / math.sqrt(64)
    turned = dq_t[...].T * head_scale
    for kind, values in enumerate((turned, dk[...], dv[...])):
        if kind < 2:
            values = values * cosine[:, :part] - partner(values) * sine[:, :part]
        low[:, kind * part : (kind + 1) * part] = values.astype(BF16)
    part_of = row_place(low, rows)
    end(begin([(part_of(dest(me, k, parts)), out) for k, out in enumerate(outs)], in_sems))


def attend_back(info, pieces, qkv, out_t, inverse, probs, cosine, sine, parts, heads):
    rows, part = pieces[0].shape
    length = rows * parts
    return pl.pallas_call(
        lambda *refs: attend_back_kernel(parts, heads, *refs),
        out_shape=[shape((rows, 3 * part), BF16) for unused in range(parts)],
        in_specs=[SMEM] + [HBM] * parts + [VMEM] + [HBM] * 5,
        out_specs=[HBM] * parts,
        scratch_shapes=[
            pltpu.VMEM((length, part), BF16),
            pltpu.VMEM((part, length), BF16),
            pltpu.VMEM((8, length), F32),
            pltpu.VMEM((3, length, TILE), BF16),
            pltpu.VMEM((part, length), F32),
            pltpu.VMEM((length, part), F32),
            pltpu.VMEM((length, part), F32),
            pltpu.VMEM((length, 3 * part), BF16),
            pltpu.VMEM(qkv.shape, BF16),
            pltpu.VMEM(out_t.shape, F32),
            pltpu.VMEM(cosine.shape, F32),
            pltpu.VMEM(sine.shape, F32),
            pltpu.SemaphoreType.DMA((parts,)),
            pltpu.SemaphoreType.DMA((3,)),
            pltpu.SemaphoreType.DMA((4,)),
        ],
        compiler_params=params(60),
        cost_estimate=cost(heads * length * length * 512, heads * length * length, 0, WEIGHT),
        name="attend_back",
    )(info, *pieces, inverse, probs, qkv, out_t, cosine, sine)


def pre(info, own, left, right, counts, gain, weight, cosine, sine, parts):
    rows, width = own.shape
    part = width // parts
    return pl.pallas_call(
        lambda *refs: pre_kernel(parts, *refs),
        out_shape=[shape((rows, width), F32), shape((rows, width), BF16)]
        + [shape((rows, 3 * part), BF16) for unused in range(parts)],
        in_specs=[SMEM] + [HBM] * 4 + [VMEM] * 4,
        out_specs=[HBM] * (2 + parts),
        scratch_shapes=[
            pltpu.VMEM((3, rows, width), BF16),
            pltpu.VMEM(weight.shape, BF16),
            pltpu.VMEM((rows, width), F32),
            pltpu.VMEM((rows, width), BF16),
            pltpu.VMEM((parts, rows, 3 * part), BF16),
            pltpu.SemaphoreType.DMA((4,)),
            pltpu.SemaphoreType.DMA((max(2, parts),)),
        ],
        compiler_params=params(60),
        cost_estimate=cost(6 * rows * width * width, 8 * rows * width + 6 * width * width),
        name="pre",
    )(info, own, left, right, weight, counts, gain, cosine, sine)


def ffn_kernel(parts, info_ref, *refs):
    pieces, refs = refs[:parts], refs[parts:]
    pooled_ref, out_ref, gain, up, bias, down, *cots = refs[:9]
    refs = refs[9:]
    result_ref, grad_hidden_ref, bias_grad, gain_grad, sent, kept = refs[:6]
    outs, refs = refs[6 : 6 + parts], refs[6 + parts :]
    attended_ref, normed_ref, ffn_ref, hidden_ref, forward, arrived, back, send = refs[:8]
    products, windows, pooled, out_weight, sems, product_sems, load_sems = refs[8:]
    me, bit = info_ref[0], info_ref[1]
    step = pl.program_id(0)
    steps = pl.num_programs(0)
    rows, width = pooled_ref.shape
    part = width // parts
    high = width // 2
    halves = sent.shape[0] // high

    def product_copy(index, target):
        place = pl.multiple_of(lax.rem(index, halves) * high, high)
        return pltpu.make_async_copy(
            products.at[index], target.at[pl.ds(place, high)], product_sems.at[index]
        )

    def give(index, value):
        products[index] = value.astype(BF16)

        @pl.when(index // halves == bit)
        def to_kept():
            product_copy(index, kept).start()

        @pl.when(index // halves != bit)
        def to_sent():
            product_copy(index, sent).start()

    @pl.when(step == 0)
    def first():
        copies = copy_in(pieces, lambda index: arrived.at[index], sems, me, parts)
        moves = [(out_ref, out_weight), (pooled_ref, pooled)]
        loads = begin(moves + [(cot, windows.at[k]) for k, cot in enumerate(cots)], load_sems)
        back[...] = jnp.zeros_like(back)
        end(copies + loads[:1])
        for index in range(parts):
            attended_ref[:, index * part : (index + 1) * part] = arrived[index]
        branch_in = mm(attended_ref[...], out_weight[...])
        end(loads[1:])
        ffn_ref[...] = sum(windows[k].astype(F32) for k in range(3)).astype(BF16)
        hidden = pooled[...] + branch_in
        hidden_ref[...] = hidden
        forward[...] = hidden
        xhat, unused = norm_parts(hidden)
        normed_ref[...] = (xhat * gain[...]).astype(BF16)

    gate_in = mm(normed_ref[...], up[...]) + bias[...]
    grad_active = mm(ffn_ref[...], down[...], NT)
    bell = 0.5 * (1.0 + lax.erf(gate_in * (1.0 / math.sqrt(2.0))))
    active = (gate_in * bell).astype(BF16)
    forward[...] += mm(active, down[...])
    slope = bell + gate_in * jnp.exp(-0.5 * gate_in * gate_in) * (1.0 / math.sqrt(2.0 * math.pi))
    grad_gate = (grad_active * slope).astype(BF16)
    bias_grad[...] = jnp.sum(grad_gate.astype(F32), axis=0, keepdims=True)
    back[...] += mm(grad_gate, up[...], NT)
    for half in range(2):
        side = slice(half * high, (half + 1) * high)
        give(2 * step + half, mm(active[:, side], ffn_ref[...], TN))
        give(2 * (steps + step) + half, mm(normed_ref[:, side], grad_gate, TN))

    @pl.when(step == pl.num_programs(0) - 1)
    def last():
        result_ref[...] = forward[...].astype(BF16)
        xhat, scale = norm_parts(hidden_ref[...])
        grad, gain_sum = norm_back(back[...], xhat, scale, gain[...])
        gain_grad[...] = gain_sum
        grad_hidden = ffn_ref[...].astype(F32) + grad
        grad_hidden_ref[...] = grad_hidden
        branch = grad_hidden.astype(BF16)
        for half in range(2):
            side = slice(half * high, (half + 1) * high)
            give(4 * steps + half, mm(attended_ref[:, side], branch, TN))
        attended_grad = mm(branch, out_weight[...], NT).astype(BF16)
        for index in range(parts):
            send[index] = attended_grad[:, index * part : (index + 1) * part]
        moves = [(send.at[dest(me, k, parts)], out) for k, out in enumerate(outs)]
        copies = begin(moves, sems)
        for index in range(2 * halves):
            product_copy(index, kept).wait()
        end(copies)


def ffn(info, pieces, pooled, out_weight, gain, up, bias, down, cots, parts):
    rows, width = pooled.shape
    units = up.shape[1]
    part = width // parts
    chunk = 512
    whole = lambda *dims: pl.BlockSpec(dims, lambda step: (0,) * len(dims))
    line = pl.BlockSpec((1, chunk), lambda step: (0, step))
    square = whole(rows, width)
    return pl.pallas_call(
        lambda *refs: ffn_kernel(parts, *refs),
        grid=(units // chunk,),
        out_shape=[
            shape((rows, width), BF16),
            shape((rows, width), F32),
            shape((1, units), F32),
            shape((1, width), F32),
            shape((units + width // 2, width), BF16),
            shape((units + width // 2, width), BF16),
        ]
        + [shape((rows, part), BF16) for unused in range(parts)],
        in_specs=[SMEM]
        + [HBM] * parts
        + [
            HBM,
            HBM,
            whole(1, width),
            pl.BlockSpec((width, chunk), lambda step: (0, step)),
            line,
            pl.BlockSpec((chunk, width), lambda step: (step, 0)),
            HBM,
            HBM,
            HBM,
        ],
        out_specs=[square, square, line, whole(1, width), HBM, HBM] + [HBM] * parts,
        scratch_shapes=[
            pltpu.VMEM((rows, width), BF16),
            pltpu.VMEM((rows, width), BF16),
            pltpu.VMEM((rows, width), BF16),
            pltpu.VMEM((rows, width), F32),
            pltpu.VMEM((rows, width), F32),
            pltpu.VMEM((parts, rows, part), BF16),
            pltpu.VMEM((rows, width), F32),
            pltpu.VMEM((parts, rows, part), BF16),
            pltpu.VMEM((4 * units // width + 2, width // 2, width), BF16),
            pltpu.VMEM((3, rows, width), BF16),
            pltpu.VMEM((rows, width), F32),
            pltpu.VMEM((width, width), BF16),
            pltpu.SemaphoreType.DMA((parts,)),
            pltpu.SemaphoreType.DMA((4 * units // width + 2,)),
            pltpu.SemaphoreType.DMA((5,)),
        ],
        compiler_params=params(60),
        cost_estimate=cost(
            12 * rows * width * units + 4 * rows * width * width, 12 * width * units, 2 * rows * units, WEIGHT
        ),
        name="ffn",
    )(info, *pieces, pooled, out_weight, gain, up, bias, down, *cots)


def post_kernel(parts, info_ref, *refs):
    pieces, refs = refs[:parts], refs[parts:]
    sources, (counts, gain, bias, ffn_gain) = refs[:4], refs[4:8]
    share_ref, sent_ref, kept_ref, arrived, low, share, products, small = refs[8:16]
    pooled, weight, normed, grad_hidden, sems, load_sems, out_sems = refs[16:]
    me, bit = info_ref[0], info_ref[1]
    rows, width = pooled.shape
    part = width // parts
    half = width // 2
    copies = copy_in(pieces, lambda index: arrived.at[index], sems, me, parts)
    loads = begin(list(zip(sources, (pooled, weight, normed, grad_hidden))), load_sems)
    loads[0].wait()
    xhat, scale = norm_parts(pooled[...])
    end(copies)
    for index in range(parts):
        for kind in range(3):
            place = kind * width + index * part
            low[:, place : place + part] = arrived[index, :, kind * part : (kind + 1) * part]
    loads[1].wait()
    grad, gain_sum = norm_back(mm(low[...], weight[...], NT), xhat, scale, gain[...])
    small[...] = jnp.zeros_like(small)
    lines = bias.shape[1] // width
    for line in range(lines):
        small[line : line + 1, :] = bias[:, line * width : (line + 1) * width]
    small[lines : lines + 1, :] = ffn_gain[...]
    small[lines + 1 : lines + 2, :] = gain_sum
    loads[2].wait()
    stores = []
    for index, out in enumerate((sent_ref, kept_ref)):
        first = pl.multiple_of((1 - bit if index == 0 else bit) * half, 128)
        value = mm(normed[:, pl.ds(first, half)], low[...], TN)
        products[index, :, : 3 * width] = value.astype(BF16)
        products[index, :, 3 * width :] = small[:, pl.ds(first, half)].T.astype(BF16)
        stores += begin([(products.at[index], out)], out_sems.at[pl.ds(index, 1)])
    loads[3].wait()
    share[...] = ((grad_hidden[...] + grad) / counts[...]).astype(BF16)
    end(stores + begin([(share, share_ref)], out_sems.at[pl.ds(2, 1)]))


def post(info, pieces, pooled, weight, normed, grad_hidden, counts, gain, bias, ffn_gain, parts):
    rows, width = pooled.shape
    part = width // parts
    half = shape((width // 2, 3 * width + 128), BF16)
    return pl.pallas_call(
        lambda *refs: post_kernel(parts, *refs),
        out_shape=[shape((rows, width), BF16), half, half],
        in_specs=[SMEM] + [HBM] * (parts + 4) + [VMEM] * 4,
        out_specs=[HBM] * 3,
        scratch_shapes=[
            pltpu.VMEM((parts, rows, 3 * part), BF16),
            pltpu.VMEM((rows, 3 * width), BF16),
            pltpu.VMEM((rows, width), BF16),
            pltpu.VMEM((2,) + half.shape, BF16),
            pltpu.VMEM((128, width), F32),
            pltpu.VMEM((rows, width), F32),
            pltpu.VMEM(weight.shape, BF16),
            pltpu.VMEM((rows, width), BF16),
            pltpu.VMEM((rows, width), F32),
            pltpu.SemaphoreType.DMA((parts,)),
            pltpu.SemaphoreType.DMA((4,)),
            pltpu.SemaphoreType.DMA((3,)),
        ],
        compiler_params=params(60),
        cost_estimate=cost(12 * rows * width * width, 8 * rows * width + 6 * width * width, 0, WEIGHT),
        name="post",
    )(info, *pieces, pooled, weight, normed, grad_hidden, counts, gain, bias, ffn_gain)


def ffn_result_kernel(bit_ref, own, other, down, up, out, whole, wide, in_sems, out_sems):
    half, width = own.shape
    units = down.shape[0]
    high = width // 2
    blocks = 2 * half // high
    bit = bit_ref[0]

    def arrival(index, source):
        place = index * high % half
        return pltpu.make_async_copy(
            source.at[pl.ds(place, high)], whole.at[index], in_sems.at[index]
        )

    for index in range(blocks):
        mine = index * high // half == bit

        @pl.when(mine)
        def from_own():
            arrival(index, own).start()

        @pl.when(jnp.logical_not(mine))
        def from_other():
            arrival(index, other).start()

    copies = []
    for index in range(blocks):
        arrival(index, own).wait()
        wide[index] = whole[index].astype(F32)
        first = index * high
        if first < units:
            target = down.at[pl.ds(first, high)]
        elif first < 2 * units:
            column = (first - units) // width * width
            target = up.at[pl.ds(first % width, high), pl.ds(column, width)]
        else:
            target = out.at[pl.ds(first - 2 * units, high)]
        copies.append(pltpu.make_async_copy(wide.at[index], target, out_sems.at[index]))
        copies[-1].start()
    end(copies)


def ffn_result(bit, own, other, units):
    half, width = own.shape
    high = width // 2
    blocks = 2 * half // high
    return pl.pallas_call(
        ffn_result_kernel,
        out_shape=[shape((units, width), F32), shape((width, units), F32), shape((width, width), F32)],
        in_specs=[SMEM, HBM, HBM],
        out_specs=[HBM] * 3,
        scratch_shapes=[
            pltpu.VMEM((blocks, high, width), BF16),
            pltpu.VMEM((blocks, high, width), F32),
            pltpu.SemaphoreType.DMA((blocks,)),
            pltpu.SemaphoreType.DMA((blocks,)),
        ],
        compiler_params=params(60),
        cost_estimate=cost(0, 12 * half * width),
        name="ffn_result",
    )(bit, own, other)


def qkv_result_kernel(count, order_ref, *refs):
    pieces, (out, bias, ffn_gain, attn_gain, whole, sems) = refs[: 2 * count], refs[2 * count :]
    size = pieces[0].shape[0]
    copies = []
    for index, piece in enumerate(pieces):
        side = order_ref[count] if index < count else 1 - order_ref[count]
        place = pl.multiple_of((side * count + order_ref[index % count]) * size, 16)
        copies.append(
            pltpu.make_async_copy(piece, whole.at[pl.ds(place, size)], sems.at[index])
        )
        copies[-1].start()
    end(copies)
    wide = out.shape[1]
    out[...] = whole[:, :wide].astype(F32)
    lines = whole[:, wide:].astype(F32).T
    count = bias.shape[0]
    for line in range(count):
        bias[line, :, :] = lines[line : line + 1, :]
    ffn_gain[...] = lines[count : count + 1, :]
    attn_gain[...] = lines[count + 1 : count + 2, :]


def qkv_result(order, pieces, lines):
    size, wide = pieces[0].shape
    count = len(pieces) // 2
    rows = 2 * count * size
    return pl.pallas_call(
        lambda *refs: qkv_result_kernel(count, *refs),
        out_shape=[
            shape((rows, wide - 128), F32),
            shape((lines, 1, rows), F32),
            shape((1, rows), F32),
            shape((1, rows), F32),
        ],
        in_specs=[SMEM] + [HBM] * (2 * count),
        out_specs=[VMEM] * 4,
        scratch_shapes=[
            pltpu.VMEM((rows, wide), BF16),
            pltpu.SemaphoreType.DMA((2 * count,)),
        ],
        compiler_params=params(60),
        cost_estimate=cost(0, 6 * rows * wide, 0, 4 * WEIGHT),
        name="qkv_result",
    )(order, *pieces)


def join_kernel(order_ref, *refs):
    pieces, out = refs[:-1], refs[-1]
    size = pieces[0].shape[0]
    for index, piece in enumerate(pieces):
        out[pl.ds(pl.multiple_of(order_ref[index] * size, size), size), :] = piece[...]


def join(pieces, order):
    size, width = pieces[0].shape
    count = len(pieces)
    if size % 16:
        whole = jnp.zeros((count * size, width), BF16)
        for index, piece in enumerate(pieces):
            whole = lax.dynamic_update_slice_in_dim(whole, piece, order[index] * size, 0)
        return whole
    return pl.pallas_call(
        join_kernel,
        out_shape=shape((count * size, width), BF16),
        in_specs=[SMEM] + [VMEM] * count,
        out_specs=VMEM,
        compiler_params=params(60),
        cost_estimate=cost(0, 4 * count * size * width),
        name="join",
    )(order, *pieces)


def pairwise(values, odd, parts):
    firsts = range(1 if odd else 0, parts - 1, 2)
    pairs = [(i, i + 1) for i in firsts] + [(i + 1, i) for i in firsts]
    return lax.ppermute(values, "seq", pairs)


def rotated(values, shift, parts):
    return lax.ppermute(values, "seq", [(i, (i + shift) % parts) for i in range(parts)])


def swap(values):
    return lax.ppermute(values, "core", [(0, 1), (1, 0)])


def turned(values, axis):
    return lax.all_to_all(values, axis, 0, 0)


def add_low(first, second):
    return (first.astype(F32) + second.astype(F32)).astype(BF16)


def total_of(values):
    return jnp.sum(values.astype(F32), axis=0).astype(BF16)


def sum_plane_out(half, chips):
    rows, width = half.shape
    return turned(half.reshape(chips, rows // chips, width), "chip")


def sum_plane_back(own, chips):
    chunks = turned(jnp.broadcast_to(own, (chips,) + own.shape), "chip")
    return chunks.reshape(chips * own.shape[0], own.shape[1])


class SeqSum:
    def __init__(self, pieces, me, parts):
        self.values, self.me, self.parts = pieces, me, parts
        self.bits = parts.bit_length() - 1
        self.ways = [(bit, 0) for bit in range(self.bits - 1)] + [(self.bits - 1, 1)]
        self.ways += [(bit, 2) for bit in reversed(range(self.bits - 1))]

    def exchange(self, values, bit):
        return lax.ppermute(values, "seq", [(i, i ^ (1 << bit)) for i in range(self.parts)])

    def start(self, way):
        bit, kind = self.ways[way]
        if kind == 0:
            half = self.values.shape[1] // 2
            mine = (self.me >> bit) & 1
            piece = lambda side: total_of(
                lax.dynamic_slice_in_dim(self.values, side * half, half, 1)
            )
            self.kept, self.sent = piece(mine), piece(1 - mine)
            return self.exchange(self.sent, bit)
        if kind == 1:
            self.kept = total_of(self.values)
        else:
            self.kept = self.values
        self.sent = self.kept
        return self.exchange(self.sent, bit)

    def finish(self, way, got):
        bit, kind = self.ways[way]
        if kind < 2:
            self.values = add_low(self.kept, got)
            if kind == 0 or way + 1 == len(self.ways):
                self.values = self.values[None] if kind == 0 else self.values
            return
        first = ((self.me >> bit) & 1) == 0
        low, high = jnp.where(first, self.kept, got), jnp.where(first, got, self.kept)
        self.values = jnp.concatenate([low, high], axis=0)


def near_pieces(own, chips):
    pairs = lambda k: [(i, i ^ k) for i in range(chips)]
    return [lax.ppermute(own, "chip", pairs(k)) if k else own for k in range(chips)]


def after(values, *earlier):
    return lax.optimization_barrier((values,) + earlier)[0]


def tie(*groups):
    return lax.optimization_barrier(groups)


def body(
    byte_input_rows,
    segment_ids,
    attn_gain,
    qkv_weight,
    out_weight,
    ffn_gain,
    up_weight,
    up_bias,
    down_weight,
    cotangent,
):
    rows_in, cot = byte_input_rows[0], cotangent[0]
    ids = segment_ids
    block, width = rows_in.shape
    parts, chips = lax.axis_size("seq"), lax.axis_size("chip")
    me, core = lax.axis_index("seq"), lax.axis_index("core")
    own_rows = SEG_DEV
    length = own_rows * parts
    heads = HEADS // parts
    reach = reach_of(parts, own_rows, block)
    place = jnp.stack([me, core]).astype(jnp.int32)
    base = ((me - reach) * own_rows).astype(jnp.int32)[None]
    side = (1 - 2 * (me & 1)).astype(jnp.int32)[None]
    firsts = ids

    def both_ways(carried):
        return [pairwise(carried[0], False, parts), pairwise(carried[1], True, parts)]

    def to_owners(windows, hold=lambda carried: carried):
        carried = [windows[2 * reach], windows[0]]
        for away in range(reach - 1, -1, -1):
            carried = both_ways(carried)
            if away:
                carried = [
                    add_low(carried[1], windows[reach + away]),
                    add_low(carried[0], windows[reach - away]),
                ]
                carried = hold(carried)
        return [windows[reach]] + carried

    def exchange(messages):
        return [messages[0]] + [
            rotated(message, shift, parts) for shift, message in enumerate(messages) if shift
        ]

    half = 32
    lane = jnp.arange(128, dtype=jnp.int32)
    frequency = jnp.exp((lane % half).astype(F32) * (-math.log(10000.0) / half))
    angles = jnp.arange(length, dtype=jnp.int32).astype(F32)[:, None] * frequency[None, :]
    cosine = jnp.cos(angles)
    sine = jnp.sin(angles) * jnp.where(lane % 64 < half, -1.0, 1.0)
    own_cosine = lax.dynamic_slice_in_dim(cosine, me * own_rows, own_rows, 0)
    own_sine = lax.dynamic_slice_in_dim(sine, me * own_rows, own_rows, 0)

    windows = pool(base, side, firsts, ids, rows_in, own_rows, 2 * reach + 1)
    cot_windows = pool(base, side, firsts, ids, after(cot, windows), own_rows, 2 * reach + 1)

    def behind_first(carried):
        nonlocal cot_windows
        carried, cot_windows = tie(carried, cot_windows)
        return carried

    sums_in = to_owners(windows, behind_first)
    ids_late = after(ids, windows)
    ids_all = turned(jnp.broadcast_to(ids_late, (parts,) + ids.shape), "seq")
    positions = me * own_rows + jnp.arange(own_rows, dtype=jnp.int32)
    same = ids_all.reshape(1, -1) == positions[:, None]
    counts = jnp.sum(same.astype(F32), axis=1, keepdims=True)
    ids_column = ids.reshape(block, 1)

    gain_row = attn_gain[None, :]
    pooled, normed_attn, *qkv_out = pre(
        place, *sums_in, counts, gain_row, qkv_weight, own_cosine, own_sine, parts
    )
    qkv_in = exchange(qkv_out)
    cots_in = to_owners(cot_windows, lambda carried: after(carried, qkv_in[1]))
    *attended_out, qkv, out_t, inverse, probs = attend(place, qkv_in, parts, heads)
    attended_in = exchange(attended_out)
    (
        pooled_out,
        grad_hidden,
        grad_bias,
        grad_ffn_gain,
        sent,
        kept,
        *grads_out,
    ) = ffn(
        place,
        attended_in,
        pooled,
        out_weight,
        ffn_gain[None, :],
        up_weight,
        up_bias[None, :],
        down_weight,
        cots_in,
        parts,
    )
    bit = core.astype(jnp.int32)[None]

    grads_in = exchange(grads_out)
    half = add_low(kept, swap(sent))
    grads_in = after(grads_in, half)
    pieces = sum_plane_out(half, chips)
    pooled_hop = both_ways(after([pooled_out, pooled_out], grads_in))
    pooled_in = [pooled_out] + pooled_hop
    low_out = attend_back(
        place, grads_in, qkv, out_t, inverse, probs, cosine, sine, parts, heads
    )
    low_out, pooled_hop = tie(low_out, pooled_hop)
    low_in = exchange(low_out)
    low_in, pieces = tie(low_in, pieces)
    ffn_sum = SeqSum(pieces, me, parts)
    ways = len(ffn_sum.ways)
    got = ffn_sum.start(0)
    low_in = after(low_in, ffn_sum.sent)
    share, qkv_sent, qkv_kept = post(
        place,
        low_in,
        pooled,
        qkv_weight,
        normed_attn,
        grad_hidden,
        counts,
        gain_row,
        grad_bias,
        grad_ffn_gain,
        parts,
    )

    share_hop = both_ways([share, share])
    share_in = [share] + share_hop
    ffn_sum.finish(0, after(got, qkv_sent))
    pieces = sum_plane_out(add_low(qkv_kept, swap(qkv_sent)), chips)
    qkv_sum = SeqSum(pieces, me, parts)
    if ways > 1:
        ffn_sum.finish(1, after(ffn_sum.start(1), pieces))
    pooled_hop = after(pooled_hop, share)
    for unused in range(1, reach):
        pooled_hop = both_ways(pooled_hop[::-1])
        pooled_in += pooled_hop
    for way in range(ways):
        qkv_sum.finish(way, qkv_sum.start(way))
        if way == 0:
            qkv_sum.values, share_hop, pooled_in = tie(qkv_sum.values, share_hop, pooled_in)
        if way + 2 < ways:
            ffn_sum.finish(way + 2, after(ffn_sum.start(way + 2), qkv_sum.values))
    ffn_own = sum_plane_back(ffn_sum.values, chips)
    share_hop = after(share_hop, qkv_sum.values)
    for unused in range(1, reach):
        share_hop = both_ways(share_hop[::-1])
        share_in += share_hop
    near = near_pieces(qkv_sum.values, chips)
    grad_input = select(base, side, firsts, ids_column, cot, share_in)
    layer_out = select(base, side, firsts, ids_column, rows_in, pooled_in)
    near = after(near, grad_input, layer_out)
    near_order = jnp.stack([lax.axis_index("chip") ^ k for k in range(chips)] + [core])
    units = up_weight.shape[1]
    ffn_own = after(ffn_own, near)
    grad_down, grad_up, grad_out = ffn_result(bit, ffn_own, swap(ffn_own), units)
    grad_qkv, grad_bias, grad_ffn_gain, grad_attn_gain = qkv_result(
        near_order.astype(jnp.int32), near + [swap(p) for p in near], units // width
    )
    return (
        layer_out[None],
        grad_input[None],
        grad_attn_gain[0],
        grad_qkv,
        grad_out,
        grad_ffn_gain[0],
        grad_up,
        grad_bias.reshape(units),
        grad_down,
    )


def solution(mesh):
    dp, seq = mesh.shape["dp"], mesh.shape["seq"]
    inner = jax.sharding.Mesh(mesh.devices.reshape(dp // 2, 2, seq), ("chip", "core", "seq"))
    rows, ids = P(("chip", "core"), "seq", None), P(("chip", "core"), "seq")
    placed = (rows, ids, P(), P(), P(), P(), P(), P(), P(), rows)
    return jax.shard_map(
        body,
        mesh=inner,
        in_specs=placed,
        out_specs=(rows, rows, P(), P(), P(), P(), P(), P(), P()),
        check_vma=False,
    )
```

```python
import math

import jax
import jax.numpy as jnp
import numpy as np
from jax import lax
from jax.experimental import pallas as pl
from jax.experimental.pallas import tpu as pltpu
from jax.sharding import PartitionSpec as P

HEADS = 8
SEG_DEV = 448
TILE = 256
BAND = TILE + 16
WEIGHT = 20
NEG = -1e30
NN = (((1,), (0,)), ((), ()))
NT = (((1,), (1,)), ((), ()))
TN = (((0,), (0,)), ((), ()))
F32 = jnp.float32
BF16 = jnp.bfloat16

SMEM = pl.BlockSpec(memory_space=pltpu.SMEM)
VMEM = pl.BlockSpec(memory_space=pltpu.VMEM)
HBM = pl.BlockSpec(memory_space=pltpu.HBM)


def mm(left, right, dims=NN):
    return lax.dot_general(left, right, dims, preferred_element_type=F32)


def shape(dims, kind):
    return jax.ShapeDtypeStruct(dims, kind)


def cost(flops, moved, exps=0, weight=1):
    return pl.CostEstimate(
        flops=int(weight * flops), bytes_accessed=int(weight * moved), transcendentals=int(weight * exps)
    )


def params(mebibytes):
    return pltpu.CompilerParams(vmem_limit_bytes=int(mebibytes * 1024 * 1024))


def begin(moves, sems):
    copies = [pltpu.make_async_copy(*move, sems.at[index]) for index, move in enumerate(moves)]
    for copy in copies:
        copy.start()
    return copies


def end(copies):
    for copy in copies:
        copy.wait()


def reach_of(parts, rows, block):
    total = rows * parts
    reach = 0
    for d in range(parts):
        low = max(0, total - (parts - d) * block)
        high = min(total, (d + 1) * block) - 1
        reach = max(reach, d - low // rows, high // rows - d)
    return reach


def band_start(first_ref, base_ref, tile):
    return pl.multiple_of((first_ref[0, tile * TILE] - base_ref[0]) // 16 * 16, 16)


def pool_kernel(base_ref, side_ref, first_ref, ids_ref, rows_ref, *refs):
    outs, total = refs[:-1], refs[-1]
    size = outs[0].shape[0]
    total[...] = jnp.zeros_like(total)
    place = lax.broadcasted_iota(jnp.int32, (BAND, TILE), 0)
    for tile in range(rows_ref.shape[0] // TILE):
        span = slice(tile * TILE, (tile + 1) * TILE)
        start = band_start(first_ref, base_ref, tile)
        local = ids_ref[:, span] - (base_ref[0] + start)
        hot = jnp.where(place == local, 1.0, 0.0).astype(BF16)
        total[pl.ds(start, BAND), :] += mm(hot, rows_ref[span, :])
    reach = len(outs) // 2
    for index, out in enumerate(outs):
        place = pl.multiple_of((reach + (index - reach) * side_ref[0]) * size, 16)
        out[...] = total[pl.ds(place, size), :].astype(BF16)


def pool(base, side, firsts, ids, rows, own_rows, count):
    block, width = rows.shape
    return pl.pallas_call(
        pool_kernel,
        out_shape=[shape((own_rows, width), BF16)] * count,
        in_specs=[SMEM, SMEM, SMEM, VMEM, VMEM],
        out_specs=[VMEM] * count,
        scratch_shapes=[pltpu.VMEM((count * own_rows + BAND, width), F32)],
        compiler_params=params(60),
        cost_estimate=cost(2 * BAND * block * width, 2 * block * width + 2 * count * own_rows * width),
        name="pool",
    )(base, side, firsts, ids, rows)


def select_kernel(base_ref, side_ref, first_ref, ids_ref, rows_ref, *refs):
    pieces, (out, table, sems) = refs[:-3], refs[-3:]
    size = pieces[0].shape[0]
    reach = len(pieces) // 2
    copies = []
    for index, piece in enumerate(pieces):
        away = (index + 1) // 2 * (1 if index % 2 else -1)
        place = pl.multiple_of((reach + away * side_ref[0]) * size, 16)
        copies.append(
            pltpu.make_async_copy(piece, table.at[pl.ds(place, size)], sems.at[index])
        )
    for copy in copies:
        copy.start()
    table[len(pieces) * size :, :] = jnp.zeros((BAND, table.shape[1]), BF16)
    for copy in copies:
        copy.wait()
    place = lax.broadcasted_iota(jnp.int32, (TILE, BAND), 1)
    for tile in range(rows_ref.shape[0] // TILE):
        span = slice(tile * TILE, (tile + 1) * TILE)
        start = band_start(first_ref, base_ref, tile)
        local = ids_ref[span, :] - (base_ref[0] + start)
        hot = jnp.where(place == local, 1.0, 0.0).astype(BF16)
        chosen = mm(hot, table[pl.ds(start, BAND), :])
        out[span, :] = (rows_ref[span, :].astype(F32) + chosen).astype(BF16)


def select(base, side, firsts, ids_column, rows, pieces, weight=1):
    block, width = rows.shape
    total = sum(piece.shape[0] for piece in pieces)
    return pl.pallas_call(
        select_kernel,
        out_shape=shape((block, width), BF16),
        in_specs=[SMEM, SMEM, SMEM, VMEM, VMEM] + [HBM] * len(pieces),
        out_specs=VMEM,
        scratch_shapes=[
            pltpu.VMEM((total + BAND, width), BF16),
            pltpu.SemaphoreType.DMA((len(pieces),)),
        ],
        compiler_params=params(60),
        cost_estimate=cost(
            2 * BAND * block * width, 4 * block * width + 2 * total * width, 0, weight
        ),
        name="select",
    )(base, side, firsts, ids_column, rows, *pieces)


def norm_parts(values):
    center = jnp.mean(values, axis=-1, keepdims=True)
    centered = values - center
    variance = jnp.mean(centered * centered, axis=-1, keepdims=True)
    scale = lax.rsqrt(variance + 1e-05)
    return centered * scale, scale


def norm_back(grad, xhat, scale, gain):
    e = grad * gain
    mean_e = jnp.mean(e, axis=-1, keepdims=True)
    mean_ex = jnp.mean(e * xhat, axis=-1, keepdims=True)
    return scale * (e - mean_e - xhat * mean_ex), jnp.sum(grad * xhat, axis=0, keepdims=True)


def partner(values):
    lanes = values.shape[1]
    lane = lax.broadcasted_iota(jnp.int32, values.shape, 1)
    return jnp.where(
        lax.rem(lane, 64) < 32, pltpu.roll(values, lanes - 32, 1), pltpu.roll(values, 32, 1)
    )


def dest(me, shift, parts):
    return lax.rem(me + shift, parts)


def source(me, shift, parts):
    return lax.rem(me + parts - shift, parts)


def pre_kernel(parts, info_ref, own, left, right, weight_ref, *refs):
    counts, gain, cosine, sine, pooled_ref, normed_ref = refs[:6]
    outs, refs = refs[6 : 6 + parts], refs[6 + parts :]
    sums, weight, pooled, normed, send, in_sems, out_sems = refs
    me = info_ref[0]
    loads = begin(
        [(own, sums.at[0]), (left, sums.at[1]), (right, sums.at[2]), (weight_ref, weight)], in_sems
    )
    end(loads[:3])
    total = sums[0].astype(F32) + sums[1].astype(F32) + sums[2].astype(F32)
    pooled[...] = total / counts[...]
    xhat, unused = norm_parts(pooled[...])
    normed[...] = (xhat * gain[...]).astype(BF16)
    stores = begin([(pooled, pooled_ref), (normed, normed_ref)], out_sems)
    loads[3].wait()
    width = pooled.shape[1]
    part = width // parts
    step = 256
    for kind in range(3):
        for first in range(0, width, step):
            column = kind * width + first
            wide = mm(normed[...], weight[:, column : column + step])
            for inner in range(0, step, 128):
                block = wide[:, inner : inner + 128]
                if kind < 2:
                    block = block * cosine[...] + partner(block) * sine[...]
                if kind == 0:
                    block = block * (1.0 / math.sqrt(width // HEADS))
                block = block.astype(BF16)
                for small in range(0, 128, min(part, 128)):
                    place = first + inner + small
                    offset = kind * part + place % part
                    send[place // part, :, offset : offset + min(part, 128)] = block[
                        :, small : small + min(part, 128)
                    ]
    end(stores)
    end(begin([(send.at[dest(me, k, parts)], out) for k, out in enumerate(outs)], out_sems))


def copy_in(pieces, place, sems, me, parts):
    copies = []
    for shift, piece in enumerate(pieces):
        copies.append(
            pltpu.make_async_copy(piece, place(source(me, shift, parts)), sems.at[shift])
        )
    for copy in copies:
        copy.start()
    return copies


def row_place(ref, rows):
    return lambda index: ref.at[pl.ds(pl.multiple_of(index * rows, 16), rows)]


def head_mask(tile, head, heads):
    if heads == 1:
        return tile
    lane = lax.broadcasted_iota(jnp.int32, tile.shape, 1)
    return jnp.where(lane // 64 == head, tile.astype(F32), 0.0).astype(BF16)


def attend_kernel(parts, heads, info_ref, *refs):
    pieces, refs = refs[:parts], refs[parts:]
    outs, refs = refs[:parts], refs[parts:]
    qkv_ref, out_ref, inverse_ref, prob_ref = refs[:4]
    qkv, out_t, v_t, scores, probs, attended, in_sems, prob_sems, out_sems = refs[4:]
    me = info_ref[0]
    rows, part = outs[0].shape
    tiles = qkv.shape[0] // TILE
    for copy in copy_in(pieces, row_place(qkv, rows), in_sems, me, parts):
        copy.wait()
    stores = begin([(qkv, qkv_ref)], out_sems)
    v_t[...] = qkv[:, 2 * part :].astype(F32).T.astype(BF16)
    key_index = lax.broadcasted_iota(jnp.int32, (TILE, TILE), 0)
    query_index = lax.broadcasted_iota(jnp.int32, (TILE, TILE), 1)
    started = []
    for head in range(heads):
        for tile in range(tiles):
            step = head * tiles + tile
            slot = step % 2
            columns = slice(tile * TILE, (tile + 1) * TILE)
            limit = (tile + 1) * TILE
            query = head_mask(qkv[columns, :part], head, heads)
            top = jnp.full((8, TILE), NEG, F32)
            for chunk in range(tile + 1):
                span = slice(chunk * TILE, (chunk + 1) * TILE)
                score = mm(qkv[span, part : 2 * part], query, NT)
                if chunk == tile:
                    score = jnp.where(key_index <= query_index, score, NEG)
                scores[slot, span, :] = score
                top = jnp.maximum(top, jnp.max(score.reshape(TILE // 8, 8, TILE), axis=0))
            top = jnp.max(top, axis=0, keepdims=True)
            if step >= 2:
                started[step - 2].wait()
            total = jnp.zeros((8, TILE), F32)
            for chunk in range(tile + 1):
                span = slice(chunk * TILE, (chunk + 1) * TILE)
                grown = jnp.exp(scores[slot, span, :] - top)
                probs[slot, span, :] = grown.astype(BF16)
                total = total + jnp.sum(grown.reshape(TILE // 8, 8, TILE), axis=0)
            inverse = 1.0 / jnp.sum(total, axis=0, keepdims=True)
            inverse_ref[head : head + 1, columns] = inverse
            copy = pltpu.make_async_copy(
                probs.at[slot, pl.ds(0, limit)],
                prob_ref.at[head, tile, pl.ds(0, limit)],
                prob_sems.at[slot],
            )
            copy.start()
            started.append(copy)
            height = slice(head * 64, (head + 1) * 64)
            out_t[height, columns] = mm(v_t[height, :limit], probs[slot, :limit, :]) * inverse
    copy = pltpu.make_async_copy(out_t, out_ref, out_sems.at[1])
    copy.start()
    attended[...] = out_t[...].T.astype(BF16)
    part_of = row_place(attended, rows)
    end(begin([(part_of(dest(me, k, parts)), out) for k, out in enumerate(outs)], in_sems))
    end(started[-2:] + stores + [copy])


def attend(info, pieces, parts, heads):
    rows, triple = pieces[0].shape
    part = triple // 3
    length = rows * parts
    tiles = length // TILE
    return pl.pallas_call(
        lambda *refs: attend_kernel(parts, heads, *refs),
        out_shape=[shape((rows, part), BF16) for unused in range(parts)]
        + [
            shape((length, triple), BF16),
            shape((part, length), F32),
            shape((8, length), F32),
            shape((heads, tiles, length, TILE), BF16),
        ],
        in_specs=[SMEM] + [HBM] * parts,
        out_specs=[HBM] * (parts + 2) + [VMEM, HBM],
        scratch_shapes=[
            pltpu.VMEM((length, triple), BF16),
            pltpu.VMEM((part, length), F32),
            pltpu.VMEM((part, length), BF16),
            pltpu.VMEM((2, length, TILE), F32),
            pltpu.VMEM((2, length, TILE), BF16),
            pltpu.VMEM((length, part), BF16),
            pltpu.SemaphoreType.DMA((parts,)),
            pltpu.SemaphoreType.DMA((2,)),
            pltpu.SemaphoreType.DMA((2,)),
        ],
        compiler_params=params(60),
        cost_estimate=cost(
            heads * length * length * 256,
            heads * length * length,
            heads * length * length // 2,
            WEIGHT,
        ),
        name="attend",
    )(info, *pieces)


def attend_back_kernel(parts, heads, info_ref, *refs):
    pieces, refs = refs[:parts], refs[parts:]
    inverse, prob_ref = refs[:2]
    sources, refs = refs[2:6], refs[6:]
    outs, refs = refs[:parts], refs[parts:]
    grads, k_t, delta, probs, dq_t, dk, dv, low = refs[:8]
    qkv, out_t, cosine, sine, in_sems, prob_sems, load_sems = refs[8:]
    me = info_ref[0]
    rows = pieces[0].shape[0]
    length, part = dk.shape
    tiles = length // TILE
    steps = [(head, tile) for head in range(heads) for tile in range(tiles)]

    def fetch(index):
        head, tile = steps[index]
        limit = (tile + 1) * TILE
        return pltpu.make_async_copy(
            prob_ref.at[head, tile, pl.ds(0, limit)],
            probs.at[index % 3, pl.ds(0, limit)],
            prob_sems.at[index % 3],
        )

    loads = begin(list(zip(sources, (qkv, out_t, cosine, sine))), load_sems)
    arrivals = copy_in(pieces, row_place(grads, rows), in_sems, me, parts)
    fetch(0).start()
    fetch(1).start()
    loads[0].wait()
    k_t[...] = qkv[:, part : 2 * part].astype(F32).T.astype(BF16)
    dk[...] = jnp.zeros_like(dk)
    dv[...] = jnp.zeros_like(dv)
    for copy in arrivals:
        copy.wait()
    turned_grads = grads[...].astype(F32).T
    turned_grads = jnp.concatenate(
        [turned_grads[h * 64 : (h + 1) * 64, :] * inverse[h : h + 1, :] for h in range(heads)]
    )
    grads[...] = turned_grads.T.astype(BF16)
    loads[1].wait()
    product = turned_grads * out_t[...]
    for head in range(heads):
        delta[head : head + 1, :] = jnp.sum(
            product[head * 64 : (head + 1) * 64, :], axis=0, keepdims=True
        )
    for index, (head, tile) in enumerate(steps):
        slot = index % 3
        if index + 2 < len(steps):
            fetch(index + 2).start()
        fetch(index).wait()
        columns = slice(tile * TILE, (tile + 1) * TILE)
        limit = (tile + 1) * TILE
        height = slice(head * 64, (head + 1) * 64)
        query = head_mask(qkv[columns, :part], head, heads)
        grad = head_mask(grads[columns, :], head, heads)
        shift = delta[head : head + 1, columns]
        prob = probs[slot, :limit, :]
        grad_prob = mm(qkv[:limit, 2 * part :], grad, NT)
        grad_score = (prob.astype(F32) * (grad_prob - shift)).astype(BF16)
        dv[:limit, :] += mm(prob, grad)
        dk[:limit, :] += mm(grad_score, query)
        dq = mm(k_t[height, :limit], grad_score)
        dq_t[height, columns] = dq
    end(loads[2:])
    head_scale = 1.0 / math.sqrt(64)
    turned = dq_t[...].T * head_scale
    for kind, values in enumerate((turned, dk[...], dv[...])):
        if kind < 2:
            values = values * cosine[:, :part] - partner(values) * sine[:, :part]
        low[:, kind * part : (kind + 1) * part] = values.astype(BF16)
    part_of = row_place(low, rows)
    end(begin([(part_of(dest(me, k, parts)), out) for k, out in enumerate(outs)], in_sems))


def attend_back(info, pieces, qkv, out_t, inverse, probs, cosine, sine, parts, heads):
    rows, part = pieces[0].shape
    length = rows * parts
    return pl.pallas_call(
        lambda *refs: attend_back_kernel(parts, heads, *refs),
        out_shape=[shape((rows, 3 * part), BF16) for unused in range(parts)],
        in_specs=[SMEM] + [HBM] * parts + [VMEM] + [HBM] * 5,
        out_specs=[HBM] * parts,
        scratch_shapes=[
            pltpu.VMEM((length, part), BF16),
            pltpu.VMEM((part, length), BF16),
            pltpu.VMEM((8, length), F32),
            pltpu.VMEM((3, length, TILE), BF16),
            pltpu.VMEM((part, length), F32),
            pltpu.VMEM((length, part), F32),
            pltpu.VMEM((length, part), F32),
            pltpu.VMEM((length, 3 * part), BF16),
            pltpu.VMEM(qkv.shape, BF16),
            pltpu.VMEM(out_t.shape, F32),
            pltpu.VMEM(cosine.shape, F32),
            pltpu.VMEM(sine.shape, F32),
            pltpu.SemaphoreType.DMA((parts,)),
            pltpu.SemaphoreType.DMA((3,)),
            pltpu.SemaphoreType.DMA((4,)),
        ],
        compiler_params=params(60),
        cost_estimate=cost(heads * length * length * 512, heads * length * length, 0, WEIGHT),
        name="attend_back",
    )(info, *pieces, inverse, probs, qkv, out_t, cosine, sine)


def pre(info, own, left, right, counts, gain, weight, cosine, sine, parts):
    rows, width = own.shape
    part = width // parts
    return pl.pallas_call(
        lambda *refs: pre_kernel(parts, *refs),
        out_shape=[shape((rows, width), F32), shape((rows, width), BF16)]
        + [shape((rows, 3 * part), BF16) for unused in range(parts)],
        in_specs=[SMEM] + [HBM] * 4 + [VMEM] * 4,
        out_specs=[HBM] * (2 + parts),
        scratch_shapes=[
            pltpu.VMEM((3, rows, width), BF16),
            pltpu.VMEM(weight.shape, BF16),
            pltpu.VMEM((rows, width), F32),
            pltpu.VMEM((rows, width), BF16),
            pltpu.VMEM((parts, rows, 3 * part), BF16),
            pltpu.SemaphoreType.DMA((4,)),
            pltpu.SemaphoreType.DMA((max(2, parts),)),
        ],
        compiler_params=params(60),
        cost_estimate=cost(6 * rows * width * width, 8 * rows * width + 6 * width * width),
        name="pre",
    )(info, own, left, right, weight, counts, gain, cosine, sine)


def ffn_kernel(parts, info_ref, *refs):
    pieces, refs = refs[:parts], refs[parts:]
    pooled_ref, out_ref, gain, up, bias, down, *cots = refs[:9]
    refs = refs[9:]
    result_ref, grad_hidden_ref, bias_grad, gain_grad, sent, kept = refs[:6]
    outs, refs = refs[6 : 6 + parts], refs[6 + parts :]
    attended_ref, normed_ref, ffn_ref, hidden_ref, forward, arrived, back, send = refs[:8]
    products, windows, pooled, out_weight, sems, product_sems, load_sems = refs[8:]
    me, bit = info_ref[0], info_ref[1]
    step = pl.program_id(0)
    steps = pl.num_programs(0)
    rows, width = pooled_ref.shape
    part = width // parts
    high = width // 2
    halves = sent.shape[0] // high

    def product_copy(index, target):
        place = pl.multiple_of(lax.rem(index, halves) * high, high)
        return pltpu.make_async_copy(
            products.at[index], target.at[pl.ds(place, high)], product_sems.at[index]
        )

    def give(index, value):
        products[index] = value.astype(BF16)

        @pl.when(index // halves == bit)
        def to_kept():
            product_copy(index, kept).start()

        @pl.when(index // halves != bit)
        def to_sent():
            product_copy(index, sent).start()

    @pl.when(step == 0)
    def first():
        copies = copy_in(pieces, lambda index: arrived.at[index], sems, me, parts)
        moves = [(out_ref, out_weight), (pooled_ref, pooled)]
        loads = begin(moves + [(cot, windows.at[k]) for k, cot in enumerate(cots)], load_sems)
        back[...] = jnp.zeros_like(back)
        end(copies + loads[:1])
        for index in range(parts):
            attended_ref[:, index * part : (index + 1) * part] = arrived[index]
        branch_in = mm(attended_ref[...], out_weight[...])
        end(loads[1:])
        ffn_ref[...] = sum(windows[k].astype(F32) for k in range(3)).astype(BF16)
        hidden = pooled[...] + branch_in
        hidden_ref[...] = hidden
        forward[...] = hidden
        xhat, unused = norm_parts(hidden)
        normed_ref[...] = (xhat * gain[...]).astype(BF16)

    gate_in = mm(normed_ref[...], up[...]) + bias[...]
    grad_active = mm(ffn_ref[...], down[...], NT)
    bell = 0.5 * (1.0 + lax.erf(gate_in * (1.0 / math.sqrt(2.0))))
    active = (gate_in * bell).astype(BF16)
    forward[...] += mm(active, down[...])
    slope = bell + gate_in * jnp.exp(-0.5 * gate_in * gate_in) * (1.0 / math.sqrt(2.0 * math.pi))
    grad_gate = (grad_active * slope).astype(BF16)
    bias_grad[...] = jnp.sum(grad_gate.astype(F32), axis=0, keepdims=True)
    back[...] += mm(grad_gate, up[...], NT)
    for half in range(2):
        side = slice(half * high, (half + 1) * high)
        give(2 * step + half, mm(active[:, side], ffn_ref[...], TN))
        give(2 * (steps + step) + half, mm(normed_ref[:, side], grad_gate, TN))

    @pl.when(step == pl.num_programs(0) - 1)
    def last():
        result_ref[...] = forward[...].astype(BF16)
        xhat, scale = norm_parts(hidden_ref[...])
        grad, gain_sum = norm_back(back[...], xhat, scale, gain[...])
        gain_grad[...] = gain_sum
        grad_hidden = ffn_ref[...].astype(F32) + grad
        grad_hidden_ref[...] = grad_hidden
        branch = grad_hidden.astype(BF16)
        for half in range(2):
            side = slice(half * high, (half + 1) * high)
            give(4 * steps + half, mm(attended_ref[:, side], branch, TN))
        attended_grad = mm(branch, out_weight[...], NT).astype(BF16)
        for index in range(parts):
            send[index] = attended_grad[:, index * part : (index + 1) * part]
        moves = [(send.at[dest(me, k, parts)], out) for k, out in enumerate(outs)]
        copies = begin(moves, sems)
        for index in range(2 * halves):
            product_copy(index, kept).wait()
        end(copies)


def ffn(info, pieces, pooled, out_weight, gain, up, bias, down, cots, parts):
    rows, width = pooled.shape
    units = up.shape[1]
    part = width // parts
    chunk = 512
    whole = lambda *dims: pl.BlockSpec(dims, lambda step: (0,) * len(dims))
    line = pl.BlockSpec((1, chunk), lambda step: (0, step))
    square = whole(rows, width)
    return pl.pallas_call(
        lambda *refs: ffn_kernel(parts, *refs),
        grid=(units // chunk,),
        out_shape=[
            shape((rows, width), BF16),
            shape((rows, width), F32),
            shape((1, units), F32),
            shape((1, width), F32),
            shape((units + width // 2, width), BF16),
            shape((units + width // 2, width), BF16),
        ]
        + [shape((rows, part), BF16) for unused in range(parts)],
        in_specs=[SMEM]
        + [HBM] * parts
        + [
            HBM,
            HBM,
            whole(1, width),
            pl.BlockSpec((width, chunk), lambda step: (0, step)),
            line,
            pl.BlockSpec((chunk, width), lambda step: (step, 0)),
            HBM,
            HBM,
            HBM,
        ],
        out_specs=[square, square, line, whole(1, width), HBM, HBM] + [HBM] * parts,
        scratch_shapes=[
            pltpu.VMEM((rows, width), BF16),
            pltpu.VMEM((rows, width), BF16),
            pltpu.VMEM((rows, width), BF16),
            pltpu.VMEM((rows, width), F32),
            pltpu.VMEM((rows, width), F32),
            pltpu.VMEM((parts, rows, part), BF16),
            pltpu.VMEM((rows, width), F32),
            pltpu.VMEM((parts, rows, part), BF16),
            pltpu.VMEM((4 * units // width + 2, width // 2, width), BF16),
            pltpu.VMEM((3, rows, width), BF16),
            pltpu.VMEM((rows, width), F32),
            pltpu.VMEM((width, width), BF16),
            pltpu.SemaphoreType.DMA((parts,)),
            pltpu.SemaphoreType.DMA((4 * units // width + 2,)),
            pltpu.SemaphoreType.DMA((5,)),
        ],
        compiler_params=params(60),
        cost_estimate=cost(
            12 * rows * width * units + 4 * rows * width * width, 12 * width * units, 2 * rows * units, WEIGHT
        ),
        name="ffn",
    )(info, *pieces, pooled, out_weight, gain, up, bias, down, *cots)


def post_kernel(parts, info_ref, *refs):
    pieces, refs = refs[:parts], refs[parts:]
    sources, (counts, gain, bias, ffn_gain) = refs[:4], refs[4:8]
    share_ref, sent_ref, kept_ref, arrived, low, share, products, small = refs[8:16]
    pooled, weight, normed, grad_hidden, sems, load_sems, out_sems = refs[16:]
    me, bit = info_ref[0], info_ref[1]
    rows, width = pooled.shape
    part = width // parts
    half = width // 2
    copies = copy_in(pieces, lambda index: arrived.at[index], sems, me, parts)
    loads = begin(list(zip(sources, (pooled, weight, normed, grad_hidden))), load_sems)
    loads[0].wait()
    xhat, scale = norm_parts(pooled[...])
    end(copies)
    for index in range(parts):
        for kind in range(3):
            place = kind * width + index * part
            low[:, place : place + part] = arrived[index, :, kind * part : (kind + 1) * part]
    loads[1].wait()
    grad, gain_sum = norm_back(mm(low[...], weight[...], NT), xhat, scale, gain[...])
    small[...] = jnp.zeros_like(small)
    lines = bias.shape[1] // width
    for line in range(lines):
        small[line : line + 1, :] = bias[:, line * width : (line + 1) * width]
    small[lines : lines + 1, :] = ffn_gain[...]
    small[lines + 1 : lines + 2, :] = gain_sum
    loads[2].wait()
    stores = []
    for index, out in enumerate((sent_ref, kept_ref)):
        first = pl.multiple_of((1 - bit if index == 0 else bit) * half, 128)
        value = mm(normed[:, pl.ds(first, half)], low[...], TN)
        products[index, :, : 3 * width] = value.astype(BF16)
        products[index, :, 3 * width :] = small[:, pl.ds(first, half)].T.astype(BF16)
        stores += begin([(products.at[index], out)], out_sems.at[pl.ds(index, 1)])
    loads[3].wait()
    share[...] = ((grad_hidden[...] + grad) / counts[...]).astype(BF16)
    end(stores + begin([(share, share_ref)], out_sems.at[pl.ds(2, 1)]))


def post(info, pieces, pooled, weight, normed, grad_hidden, counts, gain, bias, ffn_gain, parts):
    rows, width = pooled.shape
    part = width // parts
    half = shape((width // 2, 3 * width + 128), BF16)
    return pl.pallas_call(
        lambda *refs: post_kernel(parts, *refs),
        out_shape=[shape((rows, width), BF16), half, half],
        in_specs=[SMEM] + [HBM] * (parts + 4) + [VMEM] * 4,
        out_specs=[HBM] * 3,
        scratch_shapes=[
            pltpu.VMEM((parts, rows, 3 * part), BF16),
            pltpu.VMEM((rows, 3 * width), BF16),
            pltpu.VMEM((rows, width), BF16),
            pltpu.VMEM((2,) + half.shape, BF16),
            pltpu.VMEM((128, width), F32),
            pltpu.VMEM((rows, width), F32),
            pltpu.VMEM(weight.shape, BF16),
            pltpu.VMEM((rows, width), BF16),
            pltpu.VMEM((rows, width), F32),
            pltpu.SemaphoreType.DMA((parts,)),
            pltpu.SemaphoreType.DMA((4,)),
            pltpu.SemaphoreType.DMA((3,)),
        ],
        compiler_params=params(60),
        cost_estimate=cost(12 * rows * width * width, 8 * rows * width + 6 * width * width, 0, WEIGHT),
        name="post",
    )(info, *pieces, pooled, weight, normed, grad_hidden, counts, gain, bias, ffn_gain)


def ffn_result_kernel(bit_ref, own, other, down, up, out, whole, wide, in_sems, out_sems):
    half, width = own.shape
    units = down.shape[0]
    high = width // 2
    blocks = 2 * half // high
    bit = bit_ref[0]

    def arrival(index, source):
        place = index * high % half
        return pltpu.make_async_copy(
            source.at[pl.ds(place, high)], whole.at[index], in_sems.at[index]
        )

    for index in range(blocks):
        mine = index * high // half == bit

        @pl.when(mine)
        def from_own():
            arrival(index, own).start()

        @pl.when(jnp.logical_not(mine))
        def from_other():
            arrival(index, other).start()

    copies = []
    for index in range(blocks):
        arrival(index, own).wait()
        wide[index] = whole[index].astype(F32)
        first = index * high
        if first < units:
            target = down.at[pl.ds(first, high)]
        elif first < 2 * units:
            column = (first - units) // width * width
            target = up.at[pl.ds(first % width, high), pl.ds(column, width)]
        else:
            target = out.at[pl.ds(first - 2 * units, high)]
        copies.append(pltpu.make_async_copy(wide.at[index], target, out_sems.at[index]))
        copies[-1].start()
    end(copies)


def ffn_result(bit, own, other, units):
    half, width = own.shape
    high = width // 2
    blocks = 2 * half // high
    return pl.pallas_call(
        ffn_result_kernel,
        out_shape=[shape((units, width), F32), shape((width, units), F32), shape((width, width), F32)],
        in_specs=[SMEM, HBM, HBM],
        out_specs=[HBM] * 3,
        scratch_shapes=[
            pltpu.VMEM((blocks, high, width), BF16),
            pltpu.VMEM((blocks, high, width), F32),
            pltpu.SemaphoreType.DMA((blocks,)),
            pltpu.SemaphoreType.DMA((blocks,)),
        ],
        compiler_params=params(60),
        cost_estimate=cost(0, 12 * half * width),
        name="ffn_result",
    )(bit, own, other)


def qkv_result_kernel(count, order_ref, *refs):
    pieces, (out, bias, ffn_gain, attn_gain, whole, sems) = refs[: 2 * count], refs[2 * count :]
    size = pieces[0].shape[0]
    copies = []
    for index, piece in enumerate(pieces):
        side = order_ref[count] if index < count else 1 - order_ref[count]
        place = pl.multiple_of((side * count + order_ref[index % count]) * size, 16)
        copies.append(
            pltpu.make_async_copy(piece, whole.at[pl.ds(place, size)], sems.at[index])
        )
        copies[-1].start()
    end(copies)
    wide = out.shape[1]
    out[...] = whole[:, :wide].astype(F32)
    lines = whole[:, wide:].astype(F32).T
    count = bias.shape[0]
    for line in range(count):
        bias[line, :, :] = lines[line : line + 1, :]
    ffn_gain[...] = lines[count : count + 1, :]
    attn_gain[...] = lines[count + 1 : count + 2, :]


def qkv_result(order, pieces, lines):
    size, wide = pieces[0].shape
    count = len(pieces) // 2
    rows = 2 * count * size
    return pl.pallas_call(
        lambda *refs: qkv_result_kernel(count, *refs),
        out_shape=[
            shape((rows, wide - 128), F32),
            shape((lines, 1, rows), F32),
            shape((1, rows), F32),
            shape((1, rows), F32),
        ],
        in_specs=[SMEM] + [HBM] * (2 * count),
        out_specs=[VMEM] * 4,
        scratch_shapes=[
            pltpu.VMEM((rows, wide), BF16),
            pltpu.SemaphoreType.DMA((2 * count,)),
        ],
        compiler_params=params(60),
        cost_estimate=cost(0, 6 * rows * wide, 0, 4 * WEIGHT),
        name="qkv_result",
    )(order, *pieces)


def join_kernel(order_ref, *refs):
    pieces, out = refs[:-1], refs[-1]
    size = pieces[0].shape[0]
    for index, piece in enumerate(pieces):
        out[pl.ds(pl.multiple_of(order_ref[index] * size, size), size), :] = piece[...]


def join(pieces, order):
    size, width = pieces[0].shape
    count = len(pieces)
    if size % 16:
        whole = jnp.zeros((count * size, width), BF16)
        for index, piece in enumerate(pieces):
            whole = lax.dynamic_update_slice_in_dim(whole, piece, order[index] * size, 0)
        return whole
    return pl.pallas_call(
        join_kernel,
        out_shape=shape((count * size, width), BF16),
        in_specs=[SMEM] + [VMEM] * count,
        out_specs=VMEM,
        compiler_params=params(60),
        cost_estimate=cost(0, 4 * count * size * width),
        name="join",
    )(order, *pieces)


def pairwise(values, odd, parts):
    firsts = range(1 if odd else 0, parts - 1, 2)
    pairs = [(i, i + 1) for i in firsts] + [(i + 1, i) for i in firsts]
    return lax.ppermute(values, "seq", pairs)


def rotated(values, shift, parts):
    return lax.ppermute(values, "seq", [(i, (i + shift) % parts) for i in range(parts)])


def swap(values):
    return lax.ppermute(values, "core", [(0, 1), (1, 0)])


def turned(values, axis):
    return lax.all_to_all(values, axis, 0, 0)


def add_low(first, second):
    return (first.astype(F32) + second.astype(F32)).astype(BF16)


def total_of(values):
    return jnp.sum(values.astype(F32), axis=0).astype(BF16)


def sum_plane_out(half, chips):
    rows, width = half.shape
    return turned(half.reshape(chips, rows // chips, width), "chip")


def sum_plane_back(own, chips):
    chunks = turned(jnp.broadcast_to(own, (chips,) + own.shape), "chip")
    return chunks.reshape(chips * own.shape[0], own.shape[1])


class SeqSum:
    def __init__(self, pieces, me, parts):
        self.values, self.me, self.parts = pieces, me, parts
        self.bits = parts.bit_length() - 1
        self.ways = [(bit, 0) for bit in range(self.bits - 1)] + [(self.bits - 1, 1)]
        self.ways += [(bit, 2) for bit in reversed(range(self.bits - 1))]

    def exchange(self, values, bit):
        return lax.ppermute(values, "seq", [(i, i ^ (1 << bit)) for i in range(self.parts)])

    def start(self, way):
        bit, kind = self.ways[way]
        if kind == 0:
            half = self.values.shape[1] // 2
            mine = (self.me >> bit) & 1
            piece = lambda side: total_of(
                lax.dynamic_slice_in_dim(self.values, side * half, half, 1)
            )
            self.kept, self.sent = piece(mine), piece(1 - mine)
            return self.exchange(self.sent, bit)
        if kind == 1:
            self.kept = total_of(self.values)
        else:
            self.kept = self.values
        self.sent = self.kept
        return self.exchange(self.sent, bit)

    def finish(self, way, got):
        bit, kind = self.ways[way]
        if kind < 2:
            self.values = add_low(self.kept, got)
            if kind == 0 or way + 1 == len(self.ways):
                self.values = self.values[None] if kind == 0 else self.values
            return
        first = ((self.me >> bit) & 1) == 0
        low, high = jnp.where(first, self.kept, got), jnp.where(first, got, self.kept)
        self.values = jnp.concatenate([low, high], axis=0)


def near_pieces(own, chips):
    pairs = lambda k: [(i, i ^ k) for i in range(chips)]
    return [lax.ppermute(own, "chip", pairs(k)) if k else own for k in range(chips)]


def after(values, *earlier):
    return lax.optimization_barrier((values,) + earlier)[0]


def tie(*groups):
    return lax.optimization_barrier(groups)


def body(
    byte_input_rows,
    segment_ids,
    attn_gain,
    qkv_weight,
    out_weight,
    ffn_gain,
    up_weight,
    up_bias,
    down_weight,
    cotangent,
):
    rows_in, cot = byte_input_rows[0], cotangent[0]
    ids = segment_ids
    block, width = rows_in.shape
    parts, chips = lax.axis_size("seq"), lax.axis_size("chip")
    me, core = lax.axis_index("seq"), lax.axis_index("core")
    own_rows = SEG_DEV
    length = own_rows * parts
    heads = HEADS // parts
    reach = reach_of(parts, own_rows, block)
    place = jnp.stack([me, core]).astype(jnp.int32)
    base = ((me - reach) * own_rows).astype(jnp.int32)[None]
    side = (1 - 2 * (me & 1)).astype(jnp.int32)[None]
    firsts = ids

    def both_ways(carried):
        return [pairwise(carried[0], False, parts), pairwise(carried[1], True, parts)]

    def to_owners(windows, hold=lambda carried: carried):
        carried = [windows[2 * reach], windows[0]]
        for away in range(reach - 1, -1, -1):
            carried = both_ways(carried)
            if away:
                carried = [
                    add_low(carried[1], windows[reach + away]),
                    add_low(carried[0], windows[reach - away]),
                ]
                carried = hold(carried)
        return [windows[reach]] + carried

    def exchange(messages):
        return [messages[0]] + [
            rotated(message, shift, parts) for shift, message in enumerate(messages) if shift
        ]

    half = 32
    lane = jnp.arange(128, dtype=jnp.int32)
    frequency = jnp.exp((lane % half).astype(F32) * (-math.log(10000.0) / half))
    angles = jnp.arange(length, dtype=jnp.int32).astype(F32)[:, None] * frequency[None, :]
    cosine = jnp.cos(angles)
    sine = jnp.sin(angles) * jnp.where(lane % 64 < half, -1.0, 1.0)
    own_cosine = lax.dynamic_slice_in_dim(cosine, me * own_rows, own_rows, 0)
    own_sine = lax.dynamic_slice_in_dim(sine, me * own_rows, own_rows, 0)

    windows = pool(base, side, firsts, ids, rows_in, own_rows, 2 * reach + 1)
    cot_windows = pool(base, side, firsts, ids, after(cot, windows), own_rows, 2 * reach + 1)

    def behind_first(carried):
        nonlocal cot_windows
        carried, cot_windows = tie(carried, cot_windows)
        return carried

    sums_in = to_owners(windows, behind_first)
    ids_late = after(ids, windows)
    ids_all = turned(jnp.broadcast_to(ids_late, (parts,) + ids.shape), "seq")
    positions = me * own_rows + jnp.arange(own_rows, dtype=jnp.int32)
    same = ids_all.reshape(1, -1) == positions[:, None]
    counts = jnp.sum(same.astype(F32), axis=1, keepdims=True)
    ids_column = ids.reshape(block, 1)

    gain_row = attn_gain[None, :]
    pooled, normed_attn, *qkv_out = pre(
        place, *sums_in, counts, gain_row, qkv_weight, own_cosine, own_sine, parts
    )
    qkv_in = exchange(qkv_out)
    cots_in = to_owners(cot_windows, lambda carried: after(carried, qkv_in[1]))
    *attended_out, qkv, out_t, inverse, probs = attend(place, qkv_in, parts, heads)
    attended_in = exchange(attended_out)
    (
        pooled_out,
        grad_hidden,
        grad_bias,
        grad_ffn_gain,
        sent,
        kept,
        *grads_out,
    ) = ffn(
        place,
        attended_in,
        pooled,
        out_weight,
        ffn_gain[None, :],
        up_weight,
        up_bias[None, :],
        down_weight,
        cots_in,
        parts,
    )
    bit = core.astype(jnp.int32)[None]

    grads_in = exchange(grads_out)
    half = add_low(kept, swap(sent))
    grads_in = after(grads_in, half)
    pieces = sum_plane_out(half, chips)
    pooled_hop = both_ways(after([pooled_out, pooled_out], grads_in))
    pooled_in = [pooled_out] + pooled_hop
    low_out = attend_back(
        place, grads_in, qkv, out_t, inverse, probs, cosine, sine, parts, heads
    )
    low_out, pooled_hop = tie(low_out, pooled_hop)
    low_in = exchange(low_out)
    low_in, pieces = tie(low_in, pieces)
    ffn_sum = SeqSum(pieces, me, parts)
    ways = len(ffn_sum.ways)
    got = ffn_sum.start(0)
    low_in = after(low_in, ffn_sum.sent)
    share, qkv_sent, qkv_kept = post(
        place,
        low_in,
        pooled,
        qkv_weight,
        normed_attn,
        grad_hidden,
        counts,
        gain_row,
        grad_bias,
        grad_ffn_gain,
        parts,
    )

    share_hop = both_ways([share, share])
    share_in = [share] + share_hop
    ffn_sum.finish(0, after(got, qkv_sent))
    pieces = sum_plane_out(add_low(qkv_kept, swap(qkv_sent)), chips)
    qkv_sum = SeqSum(pieces, me, parts)
    if ways > 1:
        ffn_sum.finish(1, after(ffn_sum.start(1), pieces))
    pooled_hop = after(pooled_hop, low_in)
    for unused in range(1, reach):
        pooled_hop = both_ways(pooled_hop[::-1])
        pooled_in += pooled_hop
    for way in range(ways):
        qkv_sum.finish(way, qkv_sum.start(way))
        if way == 0:
            qkv_sum.values, share_hop, pooled_in = tie(qkv_sum.values, share_hop, pooled_in)
        if way + 2 < ways:
            ffn_sum.finish(way + 2, after(ffn_sum.start(way + 2), qkv_sum.values))
    ffn_own = sum_plane_back(ffn_sum.values, chips)
    share_hop = after(share_hop, ffn_sum.values)
    for unused in range(1, reach):
        share_hop = both_ways(share_hop[::-1])
        share_in += share_hop
    near = near_pieces(qkv_sum.values, chips)
    grad_input = select(base, side, firsts, ids_column, cot, share_in)
    layer_out = select(base, side, firsts, ids_column, rows_in, pooled_in)
    near = after(near, grad_input, layer_out)
    near_order = jnp.stack([lax.axis_index("chip") ^ k for k in range(chips)] + [core])
    units = up_weight.shape[1]
    ffn_own = after(ffn_own, near)
    grad_down, grad_up, grad_out = ffn_result(bit, ffn_own, swap(ffn_own), units)
    grad_qkv, grad_bias, grad_ffn_gain, grad_attn_gain = qkv_result(
        near_order.astype(jnp.int32), near + [swap(p) for p in near], units // width
    )
    return (
        layer_out[None],
        grad_input[None],
        grad_attn_gain[0],
        grad_qkv,
        grad_out,
        grad_ffn_gain[0],
        grad_up,
        grad_bias.reshape(units),
        grad_down,
    )


def solution(mesh):
    dp, seq = mesh.shape["dp"], mesh.shape["seq"]
    inner = jax.sharding.Mesh(mesh.devices.reshape(dp // 2, 2, seq), ("chip", "core", "seq"))
    rows, ids = P(("chip", "core"), "seq", None), P(("chip", "core"), "seq")
    placed = (rows, ids, P(), P(), P(), P(), P(), P(), P(), rows)
    return jax.shard_map(
        body,
        mesh=inner,
        in_specs=placed,
        out_specs=(rows, rows, P(), P(), P(), P(), P(), P(), P()),
        check_vma=False,
    )
```
